32 devices in a mesh: groups: 2 (over y), seq: 16 (over z, x, core).
Axes of the slice: x: 2, y: 2, z: 4, core: 2. Of those that a mesh axis runs over, the one named last changes fastest.
Arguments:
- acts: bfloat16 [2, 8192, 8192], P(None, ('groups', 'seq')), parts along dimension 1, may hold values from -6 to 6
- cots: bfloat16 [2, 8192, 1024], P(None, ('groups', 'seq')), parts along dimension 1, may hold values from -0.29882812 to 0.29882812
- proj_in: bfloat16 [8192, 128], P('seq'), may hold values from -0.0625 to 0.0625
- proj_out: bfloat16 [1024, 128], replicated, may hold values from -0.1875 to 0.1875
- lengths: int32 [2, 32], P('groups'), parts along dimension 0, may hold values from 1 to 1024, 4096 in all within a row
- slots: int32 [64], P('groups'), parts along dimension 0, may hold values from 0 to 31, as said below
- pairs: int32 [3, 2], replicated, may hold values from 0 to 1
Outputs:
- logged: bfloat16 [64, 8192], P(('groups', 'seq')), parts along dimension 0
- covariance: float32 [6, 4096, 4096], P('groups', 'seq'), parts along dimension 0
The draws below stay inside these ranges and needn't reach their ends.
There are 2 independent parts, one for each index of `groups`. The reference program is written for one: setup_inputs(seed, part) draws one part's arguments, and reference() takes and returns one part's arrays. A program takes and returns all parts, laid end to end along the dimension named above; an argument that names none is the same for every part. Nothing has to cross between parts.
Inputs may be any that keep to these rules, and one draw needn't show every extreme that they name: The slots are distinct, so no owner logs more than 2 sequences; in every draw some owner logs exactly 2.
All inputs are finite; a program needn't handle non-finite values.
Results may differ from the reference program's by a relative error of at most 0.0075.
Values may be sent and summed in bfloat16 or wider, within the bound.
No kernel may reach another device: no remote copies, remote signals or barrier semaphores. Data moves between devices by JAX's collectives and lax.ppermute only.
A program may use at most 128 MiB of HBM per device.

```python
import math
import jax
import jax.numpy as jnp
import numpy as np
from jax import lax

D = 8192
DKV = 1024
K = 64
LAYERS = 2
NPAIR = 3
SLOTS = 32
CAP = 2
TOKENS = 4096
ROW_LEN = 4096
ROWS = 1
SEQS = 32
MOST = 1024
OWN_SLOTS = 32


def draw_slots(key, part):
    key = jax.random.fold_in(key, 11)
    key_owner, key_rest, key_order = jax.random.split(key, 3)
    owners = jax.random.permutation(key_owner, OWN_SLOTS // CAP).astype(jnp.int32)
    ordered = (owners[:, None] * CAP + jnp.arange(CAP, dtype=jnp.int32)[None, :]).reshape(-1)
    remaining = ordered[CAP:][jax.random.permutation(key_rest, OWN_SLOTS - CAP)]
    chosen = jnp.concatenate([ordered[:CAP], remaining[:SEQS - CAP]])
    return chosen[jax.random.permutation(key_order, SEQS)].astype(jnp.int32)


def with_ends(array, key, low, high):
    longest = array.shape.index(max(array.shape))
    spots = []
    for shift in (0, 1):
        where = [jax.random.randint(jax.random.fold_in(key, axis), (), 0, length) for axis, length in enumerate(array.shape)]
        where[longest] = (where[longest] + shift) % array.shape[longest]
        spots.append(tuple(where))
    return array.at[spots[0]].set(low).at[spots[1]].set(high)


def block_levels(rng, extent, cuts, low, high):
    gain, own = 1.0, jax.random.fold_in(rng, 6)
    for dim, parts in cuts:
        draws = jnp.exp(jax.random.uniform(jax.random.fold_in(own, dim), (parts,), jnp.float32, low / len(cuts), high / len(cuts)))
        gain = gain * jnp.repeat(draws, extent[dim] // parts).reshape([-1 if axis == dim else 1 for axis in range(len(extent))])
    return gain


def profile(count, total, most, skew):
    loads = [(1 << 20) // math.isqrt(rank ** skew) + 1 for rank in range(2, count + 1)]
    spare, holding = total - most - (count - 1), [1] * (count - 1)
    while spare > 0:
        movable = [i for i in range(count - 1) if holding[i] < most]
        whole, left = sum([loads[i] for i in movable]), spare
        for i in movable:
            extra = min(most - holding[i], max(1, left * loads[i] // whole), spare)
            holding[i] = holding[i] + extra
            spare = spare - extra
    return np.array([most] + holding)


def ragged(key, amount, total, bound, lean):
    if amount == 2:
        one = jax.random.randint(key, (), max(1, total - bound), min(bound, total - 1) + 1)
        return jnp.stack([one, total - one])
    sizes = jnp.asarray(profile(amount, total, bound, lean), jnp.int32)
    couples = (amount - 1) // 2
    donor, sink = sizes[1:1 + 2 * couples:2], sizes[2:2 + 2 * couples:2]
    room = jnp.minimum(donor - 1, bound - sink)
    moved = jax.random.randint(jax.random.fold_in(key, 1), (couples,), 0, 1 << 20) % (room + 1)
    sizes = sizes.at[1:1 + 2 * couples:2].set(donor - moved).at[2:2 + 2 * couples:2].set(sink + moved)
    return sizes[jax.random.permutation(jax.random.fold_in(key, 2), amount)]


def noise(rng, shape, deviation, bound, pieces=(), held_as=jnp.bfloat16):
    result = deviation * jax.random.normal(rng, shape, jnp.float32)
    if pieces:
        result = result * block_levels(rng, shape, pieces, -0.22, 0.18)
    return jnp.clip(result, -bound, bound).astype(held_as)


def setup_inputs(seed: int = 0, part: int = 0) -> dict:
    key_list = jax.random.split(jax.random.key(seed), 8)
    part_keys = jax.random.split(jax.random.fold_in(key_list[7], part), 8)
    acts = noise(part_keys[0], (LAYERS, TOKENS, D), 1.0, 6.0, ((1, 16),))
    cots = noise(part_keys[1], (LAYERS, TOKENS, DKV), 0.05, 0.29882812, ((1, 16),))
    proj_in = noise(key_list[2], (D, LAYERS * K), D ** -0.5, 0.0625, ((0, 16),))
    proj_out = noise(key_list[3], (DKV, LAYERS * K), DKV ** -0.5, 0.1875)
    lengths = jax.vmap(lambda own: ragged(own, SLOTS, ROW_LEN, MOST, 2))(jax.random.split(part_keys[4], ROWS)).reshape((ROWS, SLOTS)).astype(jnp.int32)
    slots = draw_slots(jax.random.fold_in(jax.random.fold_in(key_list[7], part), 71), part)
    pairs = with_ends(jax.random.randint(key_list[6], (NPAIR, 2), 0, LAYERS), jax.random.fold_in(key_list[6], 1), 0, LAYERS - 1).astype(jnp.int32)
    return {"acts": acts, "cots": cots, "proj_in": proj_in, "proj_out": proj_out, "lengths": lengths, "slots": slots, "pairs": pairs}


def row_terms(row_acts, row_pg, row_lengths):
    ends = jnp.cumsum(row_lengths)
    starts = ends - row_lengths
    position = jnp.arange(ROW_LEN, dtype=jnp.int32)
    inside = (position[:, None] >= starts[None, :]) & (position[:, None] < ends[None, :])
    member = inside.astype(jnp.bfloat16)
    totals = []
    for layer in range(LAYERS):
        weighted = (member[:, :, None] * row_pg[layer][:, None, :]).reshape(ROW_LEN, SLOTS * K)
        block = jnp.dot(weighted.T, row_acts[layer], preferred_element_type=jnp.float32)
        totals.append(block.reshape(SLOTS, K * K))
    return jnp.stack(totals, axis=1)


def reference(acts, cots, proj_in, proj_out, lengths, slots, pairs):
    px_list = []
    pg_list = []
    for layer in range(LAYERS):
        px_list.append(jnp.dot(acts[layer], proj_in[:, layer * K:(layer + 1) * K], preferred_element_type=jnp.float32).astype(jnp.bfloat16))
        pg_list.append(jnp.dot(cots[layer], proj_out[:, layer * K:(layer + 1) * K], preferred_element_type=jnp.float32).astype(jnp.bfloat16))
    px_all = jnp.stack(px_list).reshape(LAYERS, ROWS, ROW_LEN, K).transpose(1, 0, 2, 3)
    pg_all = jnp.stack(pg_list).reshape(LAYERS, ROWS, ROW_LEN, K).transpose(1, 0, 2, 3)
    grads = lax.map(lambda items: row_terms(items[0], items[1], items[2]), (px_all, pg_all, lengths))
    grads = grads.reshape(SEQS, LAYERS, K * K)
    grads_half = grads.astype(jnp.bfloat16)
    flat_half = grads_half.reshape(SEQS, LAYERS * K * K)
    logged = jnp.zeros((OWN_SLOTS, LAYERS * K * K), jnp.bfloat16).at[slots].set(flat_half)
    tiles = []
    for index in range(NPAIR):
        left = grads_half[:, pairs[index, 0], :]
        right = grads_half[:, pairs[index, 1], :]
        product = jnp.dot(left.T, right, preferred_element_type=jnp.float32)
        tiles.append(product / jnp.float32(SEQS))
    covariance = jnp.stack(tiles)
    return logged, covariance
```

```python
import functools

import jax
import jax.numpy as jnp
from jax import lax
from jax.experimental import pallas as pl
from jax.experimental.pallas import tpu as pltpu
from jax.sharding import PartitionSpec as P

CAP = 2
MIB = 1 << 20


def digits_of(devices):
    if devices % 16 == 0 and devices >= 64:
        return ((8, devices // 8), (2, 4), (1, 2))
    if devices % 4 == 0 and devices > 4:
        return ((4, devices // 4), (2, 2), (1, 2))
    return ((1, devices),)


def shifted(index, digits, shift):
    out = index
    for (stride, size), step in zip(digits, shift):
        digit = (index // stride) % size
        out = out + ((digit + step) % size - digit) * stride
    return out


def send(value, devices, digits, shift):
    perm = [(i, shifted(i, digits, shift)) for i in range(devices)]
    return lax.ppermute(value, "seq", perm)


def gather(block, devices, digits):
    held = {(0,) * len(digits): block}
    for level, (_, size) in enumerate(digits):
        new = dict(held)
        for step in range(1, size):
            move = tuple(step if i == level else 0 for i in range(len(digits)))
            for key, value in held.items():
                new[tuple(a + b for a, b in zip(key, move))] = send(value, devices, digits, move)
        held = new
    return held


def back(me, digits, shift):
    out = me
    for (stride, size), step in zip(digits, shift):
        digit = (me // stride) % size
        out = out + ((digit + (size - step)) % size - digit) * stride
    return out


def grads_kernel(digits, shifts, per_part, rows_all, *refs):
    count = len(shifts)
    blocks = refs[:count]
    acts, cots, proj_out, lengths = refs[count:count + 4]
    outs = refs[count + 4:count + 4 + per_part]
    weights, held, sems = refs[count + 4 + per_part:]
    layers, rows, width = held.shape
    wide = proj_out.shape[1]
    width_k = wide // layers
    square = width_k * width_k
    lanes = square // per_part
    pieces = sems.shape[0]
    step = width // pieces
    me = lax.axis_index("seq")

    def copy(i):
        at = pl.ds(i * step, step)
        return pltpu.make_async_copy(acts.at[:, :, at], held.at[:, :, at], sems.at[i])

    for i in range(pieces):
        copy(i).start()
    tall = blocks[0].shape[0]
    for shift, block in zip(shifts, blocks):
        owner = back(me, digits, shift)
        weights[pl.ds(pl.multiple_of(owner * tall, tall), tall), :] = block[...]
    lane = lax.broadcasted_iota(jnp.int32, (rows, wide), 1)
    pg = [
        jnp.dot(cots[l], proj_out[...], preferred_element_type=jnp.float32).astype(jnp.bfloat16)
        for l in range(layers)
    ]
    total = [jnp.zeros((rows, wide), jnp.float32) for _ in range(layers)]
    for i in range(pieces):
        copy(i).wait()
        at = pl.ds(i * step, step)
        for l in range(layers):
            total[l] = total[l] + jnp.dot(held[l, :, at], weights[at, :], preferred_element_type=jnp.float32)
    repeat = lanes // width_k
    px = []
    for l in range(layers):
        own = total[l][:, l * width_k:(l + 1) * width_k].astype(jnp.bfloat16)
        px.append(jnp.concatenate([own] * repeat, axis=1))
    row = me // per_part
    first = (me % per_part) * rows
    sizes = lengths[pl.ds(row, 1), :]
    per_row = sizes.shape[1]
    upto = lax.broadcasted_iota(jnp.int32, (per_row, per_row), 1)
    which = lax.broadcasted_iota(jnp.int32, (per_row, per_row), 0)
    sizes = jnp.broadcast_to(sizes, (per_row, per_row))
    ends = jnp.sum(jnp.where(upto <= which, sizes, 0), axis=1, keepdims=True)
    starts = jnp.sum(jnp.where(upto < which, sizes, 0), axis=1, keepdims=True)
    position = first + lax.broadcasted_iota(jnp.int32, (per_row, rows), 1)
    member = ((position >= starts) & (position < ends)).astype(jnp.float32).astype(jnp.bfloat16)
    source = lax.broadcasted_iota(jnp.int32, (wide, lanes), 0)
    target = lax.broadcasted_iota(jnp.int32, (wide, lanes), 1) // width_k
    for k in range(per_part):
        part = (me + k) % per_part
        for l in range(layers):
            spread = (source == target + (l * width_k + part * repeat)).astype(jnp.float32).astype(jnp.bfloat16)
            left = jnp.dot(pg[l], spread, preferred_element_type=jnp.float32).astype(jnp.bfloat16)
            value = jnp.dot(member, left * px[l], preferred_element_type=jnp.float32)
            outs[k][:, l * lanes:(l + 1) * lanes] = value.astype(jnp.bfloat16)


def covariance_kernel(digits, shifts, per_part, band, *refs):
    count = len(shifts)
    blocks = refs[:count]
    slots, pairs = refs[count:count + 2]
    logged, out = refs[count + 2:count + 4]
    right = refs[count + 4]
    seqs, full = right.shape
    square = out.shape[2] * pl.num_programs(1)
    layers = full // square
    lanes = square // per_part
    per_row = blocks[0].shape[0]
    cols = out.shape[2]
    me = lax.axis_index("seq")

    @pl.when((pl.program_id(0) == 0) & (pl.program_id(1) == 0))
    def _():
        for shift, block in zip(shifts, blocks):
            owner = back(me, digits, shift)
            row = pl.ds(pl.multiple_of((owner // per_part) * per_row, per_row), per_row)
            for l in range(layers):
                at = pl.multiple_of(l * square + (owner % per_part) * lanes, lanes)
                right[row, pl.ds(at, lanes)] = block[:, l * lanes:(l + 1) * lanes]
        own = me * CAP + lax.broadcasted_iota(jnp.int32, (CAP, seqs), 0)
        picker = (jnp.broadcast_to(slots[...], (CAP, seqs)) == own).astype(jnp.float32).astype(jnp.bfloat16)
        logged[...] = jnp.dot(picker, right[...], preferred_element_type=jnp.float32).astype(jnp.bfloat16)

    pair = pl.program_id(0)
    if band % 128 == 0:
        at = pl.multiple_of(pairs[pair, 0] * square + me * band, band)
        left = right[:, pl.ds(at, band)]
    else:
        offset = me * band
        at = pl.multiple_of(pairs[pair, 0] * square + (offset // 128) * 128, 128)
        source = lax.broadcasted_iota(jnp.int32, (128, band), 0)
        target = lax.broadcasted_iota(jnp.int32, (128, band), 1)
        pick = (source == target + offset % 128).astype(jnp.float32).astype(jnp.bfloat16)
        left = jnp.dot(right[:, pl.ds(at, 128)], pick, preferred_element_type=jnp.float32).astype(jnp.bfloat16)
    at = pl.multiple_of(pairs[pair, 1] * square + pl.program_id(1) * cols, cols)
    product = lax.dot_general(
        left, right[:, pl.ds(at, cols)], (((0,), (0,)), ((), ())), preferred_element_type=jnp.float32
    )
    out[0] = product / jnp.float32(seqs)


def shards(acts, cots, proj_in, proj_out, lengths, slots, pairs):
    layers, rows, width = acts.shape
    wide = proj_out.shape[1]
    square = (wide // layers) ** 2
    devices = lax.axis_size("seq")
    rows_all, per_row = lengths.shape
    seqs = slots.shape[0]
    npair = pairs.shape[0]
    per_part = devices // rows_all
    lanes = square // per_part
    band = square // devices
    digits = digits_of(devices)
    vmem = pl.BlockSpec(memory_space=pltpu.VMEM)
    smem = pl.BlockSpec(memory_space=pltpu.SMEM)

    held = gather(proj_in, devices, digits)
    shifts = tuple(held)
    pieces = 16
    parts = pl.pallas_call(
        functools.partial(grads_kernel, digits, shifts, per_part, rows_all),
        out_shape=[jax.ShapeDtypeStruct((per_row, layers * lanes), jnp.bfloat16)] * per_part,
        in_specs=[vmem] * len(shifts) + [pl.BlockSpec(memory_space=pl.ANY), vmem, vmem, vmem],
        out_specs=[vmem] * per_part,
        scratch_shapes=[
            pltpu.VMEM((width, wide), jnp.bfloat16),
            pltpu.VMEM((layers, rows, width), jnp.bfloat16),
            pltpu.SemaphoreType.DMA((pieces,)),
        ],
        compiler_params=pltpu.CompilerParams(vmem_limit_bytes=40 * MIB),
        name="grads",
    )(*held.values(), acts, cots, proj_out, lengths)

    total = parts[0].astype(jnp.float32)
    for k in range(1, per_part):
        perm = [(i, i - i % per_part + (i + k) % per_part) for i in range(devices)]
        total = total + lax.ppermute(parts[k], "seq", perm).astype(jnp.float32)
    summed = gather(total.astype(jnp.bfloat16), devices, digits)
    shifts = tuple(summed)
    cols = 1024
    return pl.pallas_call(
        functools.partial(covariance_kernel, digits, shifts, per_part, band),
        grid=(npair, square // cols),
        out_shape=[
            jax.ShapeDtypeStruct((CAP, layers * square), jnp.bfloat16),
            jax.ShapeDtypeStruct((npair, band, square), jnp.float32),
        ],
        in_specs=[vmem] * len(shifts) + [vmem, smem],
        out_specs=[
            pl.BlockSpec((CAP, layers * square), lambda p, q: (0, 0)),
            pl.BlockSpec((1, band, cols), lambda p, q: (p, 0, q)),
        ],
        scratch_shapes=[pltpu.VMEM((seqs, layers * square), jnp.bfloat16)],
        compiler_params=pltpu.CompilerParams(vmem_limit_bytes=40 * MIB),
        name="covariance",
    )(*summed.values(), slots.reshape(1, seqs), pairs)


def solution(mesh):
    in_specs = (
        P(None, ("groups", "seq"), None),
        P(None, ("groups", "seq"), None),
        P("seq", None),
        P(),
        P("groups", None),
        P("groups"),
        P(),
    )
    out_specs = (P(("groups", "seq"), None), P("groups", "seq", None))
    return jax.shard_map(shards, mesh=mesh, in_specs=in_specs, out_specs=out_specs, check_vma=False)
```

```python
import functools

import jax
import jax.numpy as jnp
from jax import lax
from jax.experimental import pallas as pl
from jax.experimental.pallas import tpu as pltpu
from jax.sharding import PartitionSpec as P

CAP = 2
MIB = 1 << 20
VMEM = pl.BlockSpec(memory_space=pltpu.VMEM)
SMEM = pl.BlockSpec(memory_space=pltpu.SMEM)
ANY = pl.BlockSpec(memory_space=pl.ANY)


def levels(devices):
    cores = 2 if devices % 2 == 0 else 1
    wide = 4 if devices >= 64 and devices % 8 == 0 else 2 if devices % 4 == 0 else 1
    return devices // (cores * wide), wide, cores


def owners(me, devices, shift):
    deep, wide, cores = levels(devices)
    x = ((me // cores) % wide + wide - shift[0]) % wide
    core = (me % cores + cores - shift[1]) % cores
    return [z * (wide * cores) + x * cores + core for z in range(deep)]


def pg_kernel(cots, proj_out, out):
    layers = cots.shape[0]
    width_k = proj_out.shape[1] // layers
    for l in range(layers):
        pg = jnp.dot(cots[l], proj_out[...], preferred_element_type=jnp.float32)
        pg = pg.astype(jnp.bfloat16).astype(jnp.float32)
        out[l * width_k:(l + 1) * width_k, :] = pg.T[l * width_k:(l + 1) * width_k, :]


def accumulate(acts, block, held, sems, devices, shift, start):
    layers, rows, _ = acts.shape
    me = lax.axis_index("seq")
    own = owners(me, devices, shift)
    tall = block.shape[0] // len(own)
    copies = []
    for i, owner in enumerate(own):
        at = pl.ds(pl.multiple_of(owner * tall, tall), tall)
        copies.append(pltpu.make_async_copy(acts.at[:, :, at], held.at[i], sems.at[i]))
        copies[-1].start()
    total = list(start)
    for i, copy in enumerate(copies):
        copy.wait()
        part = block[i * tall:(i + 1) * tall, :]
        for l in range(layers):
            total[l] = total[l] + jnp.dot(held[i, l], part, preferred_element_type=jnp.float32)
    return total


def first_kernel(devices, shift, acts, block, out, held, sems):
    zero = jnp.zeros(out.shape[1:], jnp.float32)
    total = accumulate(acts, block, held, sems, devices, shift, [zero] * out.shape[0])
    for l, value in enumerate(total):
        out[l] = value


def next_kernel(devices, shift, acts, block, before, out, held, sems):
    total = accumulate(acts, block, held, sems, devices, shift, [before[l] for l in range(out.shape[0])])
    for l, value in enumerate(total):
        out[l] = value


def whole_kernel(devices, shifts, acts, *refs):
    count = len(shifts)
    blocks, (out, weights) = refs[:count], refs[count:]
    me = lax.axis_index("seq")
    for shift, block in zip(shifts, blocks):
        own = owners(me, devices, shift)
        tall = block.shape[0] // len(own)
        for i, owner in enumerate(own):
            weights[pl.ds(pl.multiple_of(owner * tall, tall), tall), :] = block[i * tall:(i + 1) * tall, :]
    for l in range(out.shape[0]):
        out[l] = jnp.dot(acts[l], weights[...], preferred_element_type=jnp.float32)


def grads_kernel(per_part, projected, pg_t, lengths, out):
    layers, rows, wide = projected.shape
    width_k = wide // layers
    lanes = width_k * width_k // per_part
    repeat = lanes // width_k
    me = lax.axis_index("seq")
    sizes = lengths[pl.ds(me // per_part, 1), :]
    per_row = sizes.shape[1]
    upto = lax.broadcasted_iota(jnp.int32, (per_row, per_row), 1)
    which = lax.broadcasted_iota(jnp.int32, (per_row, per_row), 0)
    sizes = jnp.broadcast_to(sizes, (per_row, per_row))
    ends = jnp.sum(jnp.where(upto <= which, sizes, 0), axis=1, keepdims=True)
    starts = jnp.sum(jnp.where(upto < which, sizes, 0), axis=1, keepdims=True)
    position = (me % per_part) * rows + lax.broadcasted_iota(jnp.int32, (per_row, rows), 1)
    member = ((position >= starts) & (position < ends)).astype(jnp.float32)
    low = lax.broadcasted_iota(jnp.int32, (per_row, 2 * width_k), 1) < width_k
    for l in range(layers):
        own = projected[l][:, l * width_k:(l + 1) * width_k].astype(jnp.bfloat16)
        px = jnp.concatenate([own, own], axis=1)
        for part in range(per_part):
            first = l * width_k + part * repeat
            terms = [(member * pg_t[first + i:first + i + 1, :]).astype(jnp.bfloat16) for i in range(repeat)]
            sums = jnp.dot(jnp.concatenate(terms, axis=0), px, preferred_element_type=jnp.float32)
            for i in range(0, repeat, 2):
                even = sums[i * per_row:(i + 1) * per_row]
                odd = sums[(i + 1) * per_row:(i + 2) * per_row]
                at = l * lanes + i * width_k
                out[part * per_row:(part + 1) * per_row, at:at + 2 * width_k] = jnp.where(low, even, odd).astype(jnp.bfloat16)


def total_kernel(parts, terms, out):
    tall = terms.shape[0] // parts
    total = terms[:tall].astype(jnp.float32)
    for i in range(1, parts):
        total = total + terms[i * tall:(i + 1) * tall].astype(jnp.float32)
    total = total.astype(jnp.bfloat16)
    for i in range(out.shape[0] // tall):
        out[i * tall:(i + 1) * tall] = total


def covariance_kernel(per_part, blocks, slots, pairs, logged, out, right, held, sems):
    npair, band, square = held.shape
    seqs, full = right.shape
    layers = full // square
    lanes = square // per_part
    me = lax.axis_index("seq")
    devices = square // band
    tall = blocks.shape[0] // devices
    for i in range(devices):
        row = (i // per_part) * tall
        for l in range(layers):
            at = l * square + (i % per_part) * lanes
            right[row:row + tall, at:at + lanes] = blocks[i * tall:(i + 1) * tall, l * lanes:(l + 1) * lanes]
    scale = jnp.float32(1.0 / seqs)
    cols = min(1024, square)
    chunks = square // cols
    copies = []
    for p in range(npair):
        if band % 128 == 0:
            at = pl.multiple_of(pairs[p, 0] * square + me * band, band)
            left = right[:, pl.ds(at, band)]
        else:
            offset = me * band
            at = pl.multiple_of(pairs[p, 0] * square + (offset // 128) * 128, 128)
            source = lax.broadcasted_iota(jnp.int32, (128, band), 0)
            target = lax.broadcasted_iota(jnp.int32, (128, band), 1)
            pick = (source == target + offset % 128).astype(jnp.float32).astype(jnp.bfloat16)
            left = jnp.dot(right[:, pl.ds(at, 128)], pick, preferred_element_type=jnp.float32).astype(jnp.bfloat16)
        for q in range(chunks):
            at = pl.multiple_of(pairs[p, 1] * square + q * cols, cols)
            product = lax.dot_general(
                left, right[:, pl.ds(at, cols)], (((0,), (0,)), ((), ())), preferred_element_type=jnp.float32
            )
            held[p, :, q * cols:(q + 1) * cols] = product * scale
            where = (p, slice(None), pl.ds(q * cols, cols))
            copy = pltpu.make_async_copy(held.at[where], out.at[where], sems.at[p * chunks + q])
            copy.start()
            copies.append(copy)
    own = me * CAP + lax.broadcasted_iota(jnp.int32, (CAP, seqs), 0)
    picker = (jnp.broadcast_to(slots[...], (CAP, seqs)) == own).astype(jnp.float32).astype(jnp.bfloat16)
    logged[...] = jnp.dot(picker, right[...], preferred_element_type=jnp.float32).astype(jnp.bfloat16)
    for copy in copies:
        copy.wait()


def shards(acts, cots, proj_in, proj_out, lengths, slots, pairs):
    layers, rows, width = acts.shape
    wide = proj_out.shape[1]
    width_k = wide // layers
    square = width_k * width_k
    devices = lax.axis_size("seq")
    rows_all, per_row = lengths.shape
    seqs = slots.shape[0]
    npair = pairs.shape[0]
    per_part = devices // rows_all
    lanes = square // per_part
    band = square // devices
    deep, across, cores = levels(devices)
    tall = proj_in.shape[0]
    params = pltpu.CompilerParams(vmem_limit_bytes=52 * MIB)

    pg_t = pl.pallas_call(
        pg_kernel,
        out_shape=jax.ShapeDtypeStruct((wide, rows), jnp.float32),
        in_specs=[VMEM, VMEM],
        out_specs=VMEM,
        compiler_params=params,
        cost_estimate=pl.CostEstimate(flops=8 << 27, bytes_accessed=cots.size * 2, transcendentals=0),
        name="pg",
    )(cots, proj_out)

    line = across * cores
    groups = [[z * line + i for z in range(deep)] for i in range(line)]
    column = lax.all_to_all(jnp.tile(proj_in, (deep, 1)), "seq", 0, 0, axis_index_groups=groups, tiled=True)
    blocks = {(0, 0): column}
    for step in range(1, across):
        perm = [(i, i + ((i // cores + step) % across - i // cores % across) * cores) for i in range(devices)]
        blocks[step, 0] = lax.ppermute(column, "seq", perm)
    for step in range(1, cores):
        perm = [(i, i + (i + step) % cores - i % cores) for i in range(devices)]
        for x in range(across):
            blocks[x, step] = lax.ppermute(blocks[x, 0], "seq", perm)
    partial_type = jax.ShapeDtypeStruct((layers, rows, wide), jnp.float32)
    if tall % 128 == 0:
        order = sorted(blocks, key=lambda shift: (shift[0], shift[1]))
        projected = None
        for shift in order:
            before = () if projected is None else (projected,)
            projected = pl.pallas_call(
                functools.partial(next_kernel if before else first_kernel, devices, shift),
                out_shape=partial_type,
                in_specs=[ANY] + [VMEM] * (1 + len(before)),
                out_specs=VMEM,
                scratch_shapes=[
                    pltpu.VMEM((deep, layers, rows, tall), jnp.bfloat16),
                    pltpu.SemaphoreType.DMA((deep,)),
                ],
                compiler_params=params,
                cost_estimate=pl.CostEstimate(flops=8 << 27, bytes_accessed=acts.size * 2 // len(order), transcendentals=0),
                name="px",
            )(acts, blocks[shift], *before)
    else:
        projected = pl.pallas_call(
            functools.partial(whole_kernel, devices, tuple(blocks)),
            out_shape=partial_type,
            in_specs=[VMEM] * (1 + len(blocks)),
            out_specs=VMEM,
            scratch_shapes=[pltpu.VMEM((width, wide), jnp.bfloat16)],
            compiler_params=params,
            name="px",
        )(acts, *blocks.values())

    parts = pl.pallas_call(
        functools.partial(grads_kernel, per_part),
        out_shape=jax.ShapeDtypeStruct((per_part * per_row, layers * lanes), jnp.bfloat16),
        in_specs=[VMEM] * 3,
        out_specs=VMEM,
        compiler_params=params,
        name="grads",
    )(projected, pg_t, lengths)
    rings = [[r * per_part + i for i in range(per_part)] for r in range(rows_all)]
    terms = lax.all_to_all(parts, "seq", 0, 0, axis_index_groups=rings, tiled=True)
    total = pl.pallas_call(
        functools.partial(total_kernel, per_part),
        out_shape=jax.ShapeDtypeStruct((devices * per_row, layers * lanes), jnp.bfloat16),
        in_specs=[VMEM],
        out_specs=VMEM,
        compiler_params=params,
        name="total",
    )(terms)
    summed = lax.all_to_all(total, "seq", 0, 0, tiled=True)
    return pl.pallas_call(
        functools.partial(covariance_kernel, per_part),
        out_shape=[
            jax.ShapeDtypeStruct((CAP, layers * square), jnp.bfloat16),
            jax.ShapeDtypeStruct((npair, band, square), jnp.float32),
        ],
        in_specs=[VMEM, VMEM, SMEM],
        out_specs=[VMEM, ANY],
        scratch_shapes=[
            pltpu.VMEM((seqs, layers * square), jnp.bfloat16),
            pltpu.VMEM((npair, band, square), jnp.float32),
            pltpu.SemaphoreType.DMA((npair * (square // min(1024, square)),)),
        ],
        compiler_params=params,
        name="covariance",
    )(summed, slots.reshape(1, seqs), pairs)


def solution(mesh):
    in_specs = (
        P(None, ("groups", "seq"), None),
        P(None, ("groups", "seq"), None),
        P("seq", None),
        P(),
        P("groups", None),
        P("groups"),
        P(),
    )
    out_specs = (P(("groups", "seq"), None), P("groups", "seq", None))
    return jax.shard_map(shards, mesh=mesh, in_specs=in_specs, out_specs=out_specs, check_vma=False)
```

```python
import functools

import jax
import jax.numpy as jnp
from jax import lax
from jax.experimental import pallas as pl
from jax.experimental.pallas import tpu as pltpu
from jax.sharding import PartitionSpec as P

CAP = 2
MIB = 1 << 20
VMEM = pl.BlockSpec(memory_space=pltpu.VMEM)
SMEM = pl.BlockSpec(memory_space=pltpu.SMEM)
ANY = pl.BlockSpec(memory_space=pl.ANY)


def levels(devices):
    cores = 2 if devices % 2 == 0 else 1
    wide = 4 if devices >= 64 and devices % 8 == 0 else 2 if devices % 4 == 0 else 1
    return devices // (cores * wide), wide, cores


def place(index, devices):
    _, wide, cores = levels(devices)
    return index // (wide * cores), index // cores % wide, index % cores


def owner(me, devices, shift):
    deep, wide, cores = levels(devices)
    z, x, core = place(me, devices)
    z = (z + (deep - shift[0])) % deep
    x = (x + (wide - shift[1])) % wide
    core = (core + (cores - shift[2])) % cores
    return (z * wide + x) * cores + core


def send(value, devices, shift):
    deep, wide, cores = levels(devices)
    perm = []
    for i in range(devices):
        z, x, core = place(i, devices)
        z, x, core = (z + shift[0]) % deep, (x + shift[1]) % wide, (core + shift[2]) % cores
        perm.append((i, (z * wide + x) * cores + core))
    return lax.ppermute(value, "seq", perm)


def chunks(spot, devices, square):
    deep, wide, cores = levels(devices)
    line = wide * cores
    band = square // devices
    if band % 128:
        return [(0, spot * (square // line), square // line)]
    return [(z * band, (z * line + spot) * band, band) for z in range(deep)]


def pg_kernel(cots, proj_out, out, held, weights, sems):
    layers = cots.shape[0]
    width_k = proj_out.shape[1] // layers
    copies = [pltpu.make_async_copy(proj_out, weights, sems.at[layers])]
    copies += [pltpu.make_async_copy(cots.at[l], held.at[l], sems.at[l]) for l in range(layers)]
    for copy in copies:
        copy.start()
    copies[0].wait()
    for l in range(layers):
        copies[1 + l].wait()
        pg = jnp.dot(held[l], weights[...], preferred_element_type=jnp.float32)
        out[l * width_k:(l + 1) * width_k, :] = pg.T[l * width_k:(l + 1) * width_k, :].astype(jnp.bfloat16)


def px_kernel(devices, shifts, begin, end, acts, *refs):
    count = len(shifts)
    blocks, refs = refs[:count], refs[count:]
    out, held, sems = refs[-3:]
    layers, rows, _ = acts.shape
    tall, wide = blocks[0].shape
    me = lax.axis_index("seq")
    copies = []
    for i, shift in enumerate(shifts):
        at = pl.ds(pl.multiple_of(owner(me, devices, shift) * tall, tall), tall)
        copies.append(pltpu.make_async_copy(acts.at[:, :, at], held.at[i], sems.at[i]))
        copies[-1].start()
    total = [jnp.zeros((rows, wide), jnp.float32) if begin else refs[0][l] for l in range(layers)]
    for i, copy in enumerate(copies):
        copy.wait()
        for l in range(layers):
            total[l] = total[l] + jnp.dot(held[i, l], blocks[i][...], preferred_element_type=jnp.float32)
    if end:
        pack(total, refs[-4], out)
    else:
        for l in range(layers):
            out[l] = total[l]


def pack(total, pg_t, out):
    layers = len(total)
    rows, wide = total[0].shape
    width_k = wide // layers
    for l in range(layers):
        at = slice(l * width_k, (l + 1) * width_k)
        out[:rows, at] = total[l][:, at].astype(jnp.bfloat16)
    for i in range(rows // wide):
        out[rows + i * wide:rows + (i + 1) * wide, :] = pg_t[:, i * wide:(i + 1) * wide]


def whole_kernel(devices, acts, *refs):
    blocks, (pg_t, out, weights) = refs[:-3], refs[-3:]
    deep, wide, cores = levels(devices)
    me = lax.axis_index("seq")
    tall = blocks[0].shape[0] // deep
    for i, block in enumerate(blocks):
        for z in range(deep):
            at = owner(me, devices, (0, i // cores, i % cores)) % (wide * cores) + z * wide * cores
            weights[pl.ds(pl.multiple_of(at * tall, tall), tall), :] = block[z * tall:(z + 1) * tall, :]
    pack([jnp.dot(acts[l], weights[...], preferred_element_type=jnp.float32) for l in range(acts.shape[0])], pg_t, out)


def grads_kernel(devices, per_part, layers, rows, shifts, *refs):
    count = len(shifts)
    feats, (lengths, out, spread) = refs[:count], refs[count:]
    wide = feats[0].shape[1]
    runs = rows // wide
    width_k = wide // layers
    square = width_k * width_k
    _, across, cores = levels(devices)
    me = lax.axis_index("seq")
    sizes = lengths[pl.ds(me // per_part, 1), :]
    per_row = sizes.shape[1]
    upto = lax.broadcasted_iota(jnp.int32, (per_row, per_row), 1)
    which = lax.broadcasted_iota(jnp.int32, (per_row, per_row), 0)
    sizes = jnp.broadcast_to(sizes, (per_row, per_row))
    ends = jnp.sum(jnp.where(upto <= which, sizes, 0), axis=1, keepdims=True)
    starts = jnp.sum(jnp.where(upto < which, sizes, 0), axis=1, keepdims=True)
    member = []
    for shift in shifts:
        first = (owner(me, devices, shift) % per_part) * rows
        position = first + lax.broadcasted_iota(jnp.int32, (per_row, wide), 1)
        for i in range(runs):
            now = position + i * wide
            member.append(((now >= starts) & (now < ends)).astype(jnp.float32))
    member = jnp.concatenate(member, axis=1)
    for f, feat in enumerate(feats):
        for i in range(runs):
            at = (f * runs + i) * wide
            spread[:, at:at + wide] = feat[rows + i * wide:rows + (i + 1) * wide, :].astype(jnp.float32)
    low = lax.broadcasted_iota(jnp.int32, (per_row, 2 * width_k), 1) < width_k
    lanes = square // (across * cores)
    spot = me % (across * cores)
    for l in range(layers):
        px = []
        for feat in feats:
            own = feat[:rows, l * width_k:(l + 1) * width_k]
            px.append(jnp.concatenate([own, own], axis=1))
        px = jnp.concatenate(px, axis=0)
        for here, there, size in chunks(spot, devices, square):
            terms = []
            for i in range(size // width_k):
                row = l * width_k + there // width_k + i
                terms.append((member * spread[pl.ds(row, 1), :]).astype(jnp.bfloat16))
            sums = jnp.dot(jnp.concatenate(terms, axis=0), px, preferred_element_type=jnp.float32)
            for i in range(0, size // width_k, 2):
                even = sums[i * per_row:(i + 1) * per_row]
                odd = sums[(i + 1) * per_row:(i + 2) * per_row]
                at = l * lanes + here + i * width_k
                out[:, at:at + 2 * width_k] = jnp.where(low, even, odd).astype(jnp.bfloat16)


def total_kernel(devices, per_part, *refs):
    terms, out = refs[:-1], refs[-1]
    deep, across, cores = levels(devices)
    tall = terms[0].shape[0]
    if out.shape[0] == tall:
        total = terms[0][...].astype(jnp.float32)
        for term in terms[1:]:
            total = total + term[...].astype(jnp.float32)
        out[...] = total.astype(jnp.bfloat16)
        return
    me = lax.axis_index("seq")
    owned = [owner(me, devices, (shift, 0, 0)) // per_part for shift in range(deep)]
    for row in range(out.shape[0] // tall):
        total = jnp.zeros(terms[0].shape, jnp.float32)
        for home, term in zip(owned, terms):
            total = total + jnp.where(home == row, term[...].astype(jnp.float32), 0.0)
        out[row * tall:(row + 1) * tall, :] = total.astype(jnp.bfloat16)


def covariance_kernel(devices, shifts, *refs):
    count = len(shifts)
    blocks, (slots, pairs, logged, out, right, held, sems) = refs[:count], refs[count:]
    npair, band, square = held.shape
    seqs, full = right.shape
    layers = full // square
    _, across, cores = levels(devices)
    lanes = square // (across * cores)
    me = lax.axis_index("seq")
    for shift, block in zip(shifts, blocks):
        spot = owner(me, devices, shift) % (across * cores)
        for here, there, size in chunks(spot, devices, square):
            for l in range(layers):
                at = pl.multiple_of(l * square + there, size)
                right[:, pl.ds(at, size)] = block[:, l * lanes + here:l * lanes + here + size]
    scale = jnp.float32(1.0 / seqs)
    cols = min(1024, square)
    steps = square // cols
    copies = []
    for p in range(npair):
        if band % 128 == 0:
            at = pl.multiple_of(pairs[p, 0] * square + me * band, band)
            left = right[:, pl.ds(at, band)]
        else:
            offset = me * band
            at = pl.multiple_of(pairs[p, 0] * square + (offset // 128) * 128, 128)
            source = lax.broadcasted_iota(jnp.int32, (128, band), 0)
            target = lax.broadcasted_iota(jnp.int32, (128, band), 1)
            pick = (source == target + offset % 128).astype(jnp.float32).astype(jnp.bfloat16)
            left = jnp.dot(right[:, pl.ds(at, 128)], pick, preferred_element_type=jnp.float32).astype(jnp.bfloat16)
        for q in range(steps):
            at = pl.multiple_of(pairs[p, 1] * square + q * cols, cols)
            product = lax.dot_general(
                left, right[:, pl.ds(at, cols)], (((0,), (0,)), ((), ())), preferred_element_type=jnp.float32
            )
            held[p, :, q * cols:(q + 1) * cols] = product * scale
            where = (p, slice(None), pl.ds(q * cols, cols))
            copy = pltpu.make_async_copy(held.at[where], out.at[where], sems.at[p * steps + q])
            copy.start()
            copies.append(copy)
    own = me * CAP + lax.broadcasted_iota(jnp.int32, (CAP, seqs), 0)
    picker = (jnp.broadcast_to(slots[...], (CAP, seqs)) == own).astype(jnp.float32).astype(jnp.bfloat16)
    logged[...] = jnp.dot(picker, right[...], preferred_element_type=jnp.float32).astype(jnp.bfloat16)
    for copy in copies:
        copy.wait()


def shards(acts, cots, proj_in, proj_out, lengths, slots, pairs):
    layers, rows, width = acts.shape
    wide = proj_out.shape[1]
    width_k = wide // layers
    square = width_k * width_k
    devices = lax.axis_size("seq")
    rows_all, per_row = lengths.shape
    seqs = slots.shape[0]
    npair = pairs.shape[0]
    per_part = devices // rows_all
    band = square // devices
    deep, across, cores = levels(devices)
    line = across * cores
    tall = proj_in.shape[0]
    params = pltpu.CompilerParams(vmem_limit_bytes=52 * MIB)

    pg_t = pl.pallas_call(
        pg_kernel,
        out_shape=jax.ShapeDtypeStruct((wide, rows), jnp.bfloat16),
        in_specs=[ANY, ANY],
        out_specs=VMEM,
        scratch_shapes=[
            pltpu.VMEM(cots.shape, jnp.bfloat16),
            pltpu.VMEM(proj_out.shape, jnp.bfloat16),
            pltpu.SemaphoreType.DMA((layers + 1,)),
        ],
        compiler_params=params,
        cost_estimate=pl.CostEstimate(flops=1 << 27, bytes_accessed=cots.size * 2, transcendentals=0),
        name="pg",
    )(cots, proj_out)

    feat_type = jax.ShapeDtypeStruct((2 * rows, wide), jnp.bfloat16)
    if tall % 128 == 0:
        spins = sorted(range(deep), key=lambda z: min(z, deep - z))
        column = {(z, 0, 0): send(proj_in, devices, (z, 0, 0)) if z else proj_in for z in spins}
        beside = {(k[0], x, 0): send(v, devices, (0, x, 0)) for x in range(1, across) for k, v in column.items()}
        twin = {(*k[:2], c): send(v, devices, (0, 0, c)) for c in range(1, cores) for k, v in column.items()}
        last = {(*k[:2], c): send(v, devices, (0, 0, c)) for c in range(1, cores) for k, v in beside.items()}
        stages = [stage for stage in (column, {**beside, **twin}, last) if stage]
        value = None
        for i, stage in enumerate(stages):
            begin, end = i == 0, i == len(stages) - 1
            more = (() if begin else (value,)) + ((pg_t,) if end else ())
            value = pl.pallas_call(
                functools.partial(px_kernel, devices, tuple(stage), begin, end),
                out_shape=feat_type if end else jax.ShapeDtypeStruct((layers, rows, wide), jnp.float32),
                in_specs=[ANY] + [VMEM] * (len(stage) + len(more)),
                out_specs=VMEM,
                scratch_shapes=[
                    pltpu.VMEM((len(stage), layers, rows, tall), jnp.bfloat16),
                    pltpu.SemaphoreType.DMA((len(stage),)),
                ],
                compiler_params=params,
                cost_estimate=pl.CostEstimate(
                    flops=2 * acts.size * wide * len(stage) // devices,
                    bytes_accessed=2 * acts.size * len(stage) // devices,
                    transcendentals=0,
                ),
                name="px",
            )(acts, *stage.values(), *more)
    else:
        groups = [[z * line + i for z in range(deep)] for i in range(line)]
        column = lax.all_to_all(jnp.tile(proj_in, (deep, 1)), "seq", 0, 0, axis_index_groups=groups, tiled=True)
        blocks = [column] + [send(column, devices, (0, x, 0)) for x in range(1, across)]
        blocks = [block if c == 0 else send(block, devices, (0, 0, c)) for block in blocks for c in range(cores)]
        value = pl.pallas_call(
            functools.partial(whole_kernel, devices),
            out_shape=feat_type,
            in_specs=[VMEM] * (2 + len(blocks)),
            out_specs=VMEM,
            scratch_shapes=[pltpu.VMEM((width, wide), jnp.bfloat16)],
            compiler_params=params,
            name="px",
        )(acts, *blocks, pg_t)

    def plane(block):
        held = {(0, x, 0): send(block, devices, (0, x, 0)) if x else block for x in range(across)}
        return {(*k[:2], c): send(v, devices, (0, 0, c)) if c else v for c in range(cores) for k, v in held.items()}

    feats = plane(value)
    lanes = layers * square // line
    sums = pl.pallas_call(
        functools.partial(grads_kernel, devices, per_part, layers, rows, tuple(feats)),
        out_shape=jax.ShapeDtypeStruct((per_row, lanes), jnp.bfloat16),
        in_specs=[VMEM] * (len(feats) + 1),
        out_specs=VMEM,
        scratch_shapes=[pltpu.VMEM((wide, rows * line), jnp.float32)],
        compiler_params=params,
        name="grads",
    )(*feats.values(), lengths)
    terms = [send(sums, devices, (z, 0, 0)) if z else sums for z in range(deep)]
    total = pl.pallas_call(
        functools.partial(total_kernel, devices, per_part),
        out_shape=jax.ShapeDtypeStruct((seqs, lanes), jnp.bfloat16),
        in_specs=[VMEM] * deep,
        out_specs=VMEM,
        compiler_params=params,
        name="total",
    )(*terms)
    full = plane(total)
    return pl.pallas_call(
        functools.partial(covariance_kernel, devices, tuple(full)),
        out_shape=[
            jax.ShapeDtypeStruct((CAP, layers * square), jnp.bfloat16),
            jax.ShapeDtypeStruct((npair, band, square), jnp.float32),
        ],
        in_specs=[VMEM] * (len(full) + 1) + [SMEM],
        out_specs=[VMEM, ANY],
        scratch_shapes=[
            pltpu.VMEM((seqs, layers * square), jnp.bfloat16),
            pltpu.VMEM((npair, band, square), jnp.float32),
            pltpu.SemaphoreType.DMA((npair * (square // min(1024, square)),)),
        ],
        compiler_params=params,
        name="covariance",
    )(*full.values(), slots.reshape(1, seqs), pairs)


def solution(mesh):
    in_specs = (
        P(None, ("groups", "seq"), None),
        P(None, ("groups", "seq"), None),
        P("seq", None),
        P(),
        P("groups", None),
        P("groups"),
        P(),
    )
    out_specs = (P(("groups", "seq"), None), P("groups", "seq", None))
    return jax.shard_map(shards, mesh=mesh, in_specs=in_specs, out_specs=out_specs, check_vma=False)
```

```python
import functools

import jax
import jax.numpy as jnp
from jax import lax
from jax.experimental import pallas as pl
from jax.experimental.pallas import tpu as pltpu
from jax.sharding import PartitionSpec as P

CAP = 2
MIB = 1 << 20
VMEM = pl.BlockSpec(memory_space=pltpu.VMEM)
SMEM = pl.BlockSpec(memory_space=pltpu.SMEM)
ANY = pl.BlockSpec(memory_space=pl.ANY)


def levels(devices):
    cores = 2 if devices % 2 == 0 else 1
    wide = 4 if devices >= 64 and devices % 8 == 0 else 2 if devices % 4 == 0 else 1
    return devices // (cores * wide), wide, cores


def place(index, devices):
    _, wide, cores = levels(devices)
    return index // (wide * cores), index // cores % wide, index % cores


def owner(me, devices, shift):
    deep, wide, cores = levels(devices)
    z, x, core = place(me, devices)
    z = (z + (deep - shift[0])) % deep
    x = (x + (wide - shift[1])) % wide
    core = (core + (cores - shift[2])) % cores
    return (z * wide + x) * cores + core


def send(value, devices, shift):
    deep, wide, cores = levels(devices)
    perm = []
    for i in range(devices):
        z, x, core = place(i, devices)
        z, x, core = (z + shift[0]) % deep, (x + shift[1]) % wide, (core + shift[2]) % cores
        perm.append((i, (z * wide + x) * cores + core))
    return lax.ppermute(value, "seq", perm)


def chunks(spot, devices, square):
    deep, wide, cores = levels(devices)
    line = wide * cores
    band = square // devices
    if band % 128:
        return [(0, spot * (square // line), square // line)]
    return [(z * band, (z * line + spot) * band, band) for z in range(deep)]


def load_kernel(acts, cots, proj_in, proj_out, held, own, pg_t, cots_held, weights, sems):
    layers = cots.shape[0]
    width_k = proj_out.shape[1] // layers
    pairs = [(proj_out, weights), (cots, cots_held), (proj_in, own), (acts, held)]
    copies = [pltpu.make_async_copy(a, b, sems.at[i]) for i, (a, b) in enumerate(pairs)]
    for copy in copies:
        copy.start()
    copies[0].wait()
    copies[1].wait()
    for l in range(layers):
        pg = jnp.dot(cots_held[l], weights[...], preferred_element_type=jnp.float32)
        pg_t[l * width_k:(l + 1) * width_k, :] = pg.T[l * width_k:(l + 1) * width_k, :].astype(jnp.bfloat16)
    copies[2].wait()
    copies[3].wait()


def stack_kernel(count, *refs):
    out = refs[-1]
    at = 0
    for ref in refs[:count]:
        out[at:at + ref.shape[0], :] = ref[...]
        at += ref.shape[0]


def px_kernel(devices, keys, begin, end, keep, acts, *refs):
    count = len(keys)
    arrays, refs = refs[:count], refs[count:]
    layers, rows, _ = acts.shape
    wide = arrays[0].shape[1]
    me = lax.axis_index("seq")
    if keep:
        stack_kernel(count, *arrays, refs[-1])
        refs = refs[:-1]
    total = [jnp.zeros((rows, wide), jnp.float32) if begin else refs[0][l] for l in range(layers)]
    for array, shifts in zip(arrays, keys):
        tall = array.shape[0] // len(shifts)
        for i, shift in enumerate(shifts):
            at = pl.ds(pl.multiple_of(owner(me, devices, shift) * tall, tall), tall)
            block = array[i * tall:(i + 1) * tall, :]
            for l in range(layers):
                total[l] = total[l] + jnp.dot(acts[l, :, at], block, preferred_element_type=jnp.float32)
    if end:
        pack(total, refs[-2], refs[-1])
    else:
        for l in range(layers):
            refs[-1][l] = total[l]


def pack(total, pg_t, out):
    layers = len(total)
    rows, wide = total[0].shape
    width_k = wide // layers
    for l in range(layers):
        at = slice(l * width_k, (l + 1) * width_k)
        out[:rows, at] = total[l][:, at].astype(jnp.bfloat16)
    for i in range(rows // wide):
        out[rows + i * wide:rows + (i + 1) * wide, :] = pg_t[:, i * wide:(i + 1) * wide]


def whole_kernel(devices, acts, *refs):
    blocks, (pg_t, out, weights) = refs[:-3], refs[-3:]
    deep, wide, cores = levels(devices)
    me = lax.axis_index("seq")
    tall = blocks[0].shape[0] // deep
    for i, block in enumerate(blocks):
        for z in range(deep):
            at = owner(me, devices, (0, i // cores, i % cores)) % (wide * cores) + z * wide * cores
            weights[pl.ds(pl.multiple_of(at * tall, tall), tall), :] = block[z * tall:(z + 1) * tall, :]
    pack([jnp.dot(acts[l], weights[...], preferred_element_type=jnp.float32) for l in range(acts.shape[0])], pg_t, out)


def grads_kernel(devices, per_part, layers, rows, shifts, *refs):
    count = len(shifts)
    feats, (lengths, out, spread) = refs[:count], refs[count:]
    wide = feats[0].shape[1]
    runs = rows // wide
    width_k = wide // layers
    square = width_k * width_k
    _, across, cores = levels(devices)
    me = lax.axis_index("seq")
    sizes = lengths[pl.ds(me // per_part, 1), :]
    per_row = sizes.shape[1]
    upto = lax.broadcasted_iota(jnp.int32, (per_row, per_row), 1)
    which = lax.broadcasted_iota(jnp.int32, (per_row, per_row), 0)
    sizes = jnp.broadcast_to(sizes, (per_row, per_row))
    ends = jnp.sum(jnp.where(upto <= which, sizes, 0), axis=1, keepdims=True)
    starts = jnp.sum(jnp.where(upto < which, sizes, 0), axis=1, keepdims=True)
    member = []
    for shift in shifts:
        first = (owner(me, devices, shift) % per_part) * rows
        position = first + lax.broadcasted_iota(jnp.int32, (per_row, wide), 1)
        for i in range(runs):
            now = position + i * wide
            member.append(((now >= starts) & (now < ends)).astype(jnp.float32))
    member = jnp.concatenate(member, axis=1)
    for f, feat in enumerate(feats):
        for i in range(runs):
            at = (f * runs + i) * wide
            spread[:, at:at + wide] = feat[rows + i * wide:rows + (i + 1) * wide, :].astype(jnp.float32)
    low = lax.broadcasted_iota(jnp.int32, (per_row, 2 * width_k), 1) < width_k
    lanes = square // (across * cores)
    spot = me % (across * cores)
    for l in range(layers):
        px = []
        for feat in feats:
            own = feat[:rows, l * width_k:(l + 1) * width_k]
            px.append(jnp.concatenate([own, own], axis=1))
        px = jnp.concatenate(px, axis=0)
        for here, there, size in chunks(spot, devices, square):
            terms = []
            for i in range(size // width_k):
                row = l * width_k + there // width_k + i
                terms.append((member * spread[pl.ds(row, 1), :]).astype(jnp.bfloat16))
            sums = jnp.dot(jnp.concatenate(terms, axis=0), px, preferred_element_type=jnp.float32)
            for i in range(0, size // width_k, 2):
                even = sums[i * per_row:(i + 1) * per_row]
                odd = sums[(i + 1) * per_row:(i + 2) * per_row]
                at = l * lanes + here + i * width_k
                out[:, at:at + 2 * width_k] = jnp.where(low, even, odd).astype(jnp.bfloat16)


def total_kernel(devices, per_part, *refs):
    terms, out = refs[:-1], refs[-1]
    deep, across, cores = levels(devices)
    tall = terms[0].shape[0]
    if out.shape[0] == tall:
        total = terms[0][...].astype(jnp.float32)
        for term in terms[1:]:
            total = total + term[...].astype(jnp.float32)
        out[...] = total.astype(jnp.bfloat16)
        return
    me = lax.axis_index("seq")
    owned = [owner(me, devices, (shift, 0, 0)) // per_part for shift in range(deep)]
    for row in range(out.shape[0] // tall):
        total = jnp.zeros(terms[0].shape, jnp.float32)
        for home, term in zip(owned, terms):
            total = total + jnp.where(home == row, term[...].astype(jnp.float32), 0.0)
        out[row * tall:(row + 1) * tall, :] = total.astype(jnp.bfloat16)


def covariance_kernel(devices, shifts, *refs):
    count = len(shifts)
    blocks, (slots, pairs, logged, out, right, held, sems) = refs[:count], refs[count:]
    npair, band, square = held.shape
    seqs, full = right.shape
    layers = full // square
    _, across, cores = levels(devices)
    lanes = square // (across * cores)
    me = lax.axis_index("seq")
    for shift, block in zip(shifts, blocks):
        spot = owner(me, devices, shift) % (across * cores)
        for here, there, size in chunks(spot, devices, square):
            for l in range(layers):
                at = pl.multiple_of(l * square + there, size)
                right[:, pl.ds(at, size)] = block[:, l * lanes + here:l * lanes + here + size]
    scale = jnp.float32(1.0 / seqs)
    cols = min(1024, square)
    steps = square // cols
    copies = []
    for p in range(npair):
        if band % 128 == 0:
            at = pl.multiple_of(pairs[p, 0] * square + me * band, band)
            left = right[:, pl.ds(at, band)]
        else:
            offset = me * band
            at = pl.multiple_of(pairs[p, 0] * square + (offset // 128) * 128, 128)
            source = lax.broadcasted_iota(jnp.int32, (128, band), 0)
            target = lax.broadcasted_iota(jnp.int32, (128, band), 1)
            pick = (source == target + offset % 128).astype(jnp.float32).astype(jnp.bfloat16)
            left = jnp.dot(right[:, pl.ds(at, 128)], pick, preferred_element_type=jnp.float32).astype(jnp.bfloat16)
        for q in range(steps):
            at = pl.multiple_of(pairs[p, 1] * square + q * cols, cols)
            product = lax.dot_general(
                left, right[:, pl.ds(at, cols)], (((0,), (0,)), ((), ())), preferred_element_type=jnp.float32
            )
            held[p, :, q * cols:(q + 1) * cols] = product * scale
            where = (p, slice(None), pl.ds(q * cols, cols))
            copy = pltpu.make_async_copy(held.at[where], out.at[where], sems.at[p * steps + q])
            copy.start()
            copies.append(copy)
    own = me * CAP + lax.broadcasted_iota(jnp.int32, (CAP, seqs), 0)
    picker = (jnp.broadcast_to(slots[...], (CAP, seqs)) == own).astype(jnp.float32).astype(jnp.bfloat16)
    logged[...] = jnp.dot(picker, right[...], preferred_element_type=jnp.float32).astype(jnp.bfloat16)
    for copy in copies:
        copy.wait()


def shards(acts, cots, proj_in, proj_out, lengths, slots, pairs):
    layers, rows, width = acts.shape
    wide = proj_out.shape[1]
    width_k = wide // layers
    square = width_k * width_k
    devices = lax.axis_size("seq")
    rows_all, per_row = lengths.shape
    seqs = slots.shape[0]
    npair = pairs.shape[0]
    per_part = devices // rows_all
    band = square // devices
    deep, across, cores = levels(devices)
    line = across * cores
    tall = proj_in.shape[0]
    params = pltpu.CompilerParams(vmem_limit_bytes=24 * MIB)

    light = pl.CostEstimate(flops=1, bytes_accessed=1, transcendentals=0)
    held, own, pg_t = pl.pallas_call(
        load_kernel,
        out_shape=(
            pltpu.VMEM(acts.shape, jnp.bfloat16),
            pltpu.VMEM(proj_in.shape, jnp.bfloat16),
            pltpu.VMEM((wide, rows), jnp.bfloat16),
        ),
        in_specs=[ANY] * 4,
        out_specs=(VMEM,) * 3,
        scratch_shapes=[
            pltpu.VMEM(cots.shape, jnp.bfloat16),
            pltpu.VMEM(proj_out.shape, jnp.bfloat16),
            pltpu.SemaphoreType.DMA((4,)),
        ],
        compiler_params=params,
        cost_estimate=light,
        name="load",
    )(acts, cots, proj_in, proj_out)

    def stack(arrays, after):
        return pl.pallas_call(
            functools.partial(stack_kernel, len(arrays)),
            out_shape=jax.ShapeDtypeStruct((sum(a.shape[0] for a in arrays), wide), jnp.bfloat16),
            in_specs=[VMEM] * len(arrays) + [ANY] * len(after),
            out_specs=VMEM,
            compiler_params=params,
            cost_estimate=light,
            name="stack",
        )(*arrays, *after)

    def px(entries, before=None, end=False, keep=False):
        more = (() if before is None else (before,)) + ((pg_t,) if end else ())
        arrays, keys = zip(*entries)
        count = sum(map(len, keys))
        sums = feat_type if end else jax.ShapeDtypeStruct((layers, rows, wide), jnp.float32)
        stacked = [jax.ShapeDtypeStruct((count * tall, wide), jnp.bfloat16)] if keep else []
        result = pl.pallas_call(
            functools.partial(px_kernel, devices, keys, before is None, end, keep),
            out_shape=[sums] + stacked,
            in_specs=[VMEM] * (1 + len(arrays) + len(more)),
            out_specs=[VMEM] * (1 + len(stacked)),
            compiler_params=params,
            cost_estimate=light,
            name="px",
        )(held, *arrays, *more)
        return result if keep else result[0]

    feat_type = jax.ShapeDtypeStruct((2 * rows, wide), jnp.bfloat16)
    if tall % 128 == 0 and deep > 2 and across == 2 and cores == 2:
        spins = sorted(range(1, deep), key=lambda z: min(z, deep - z))
        near, far = spins[:-1], spins[-1]
        got = [send(proj_in, devices, (z, 0, 0)) for z in near]
        side = send(proj_in, devices, (0, 1, 0))
        got_far = send(proj_in, devices, (far, 0, 0))
        got = stack(got, (pg_t, side))
        side_near = send(got, devices, (0, 1, 0))
        value, column = px([(own, [(0, 0, 0)]), (got, [(z, 0, 0) for z in near])], keep=True)
        twin = send(column, devices, (0, 0, 1))
        side_far = send(got_far, devices, (0, 1, 0))
        twin_far = send(got_far, devices, (0, 0, 1))
        side = stack([side, side_near], (value,))
        twin_side = send(side, devices, (0, 0, 1))
        first = [0, *near]
        value = px([(side, [(z, 1, 0) for z in first]), (got_far, [(far, 0, 0)])], value)
        twin_side_far = send(side_far, devices, (0, 0, 1))
        value = px(
            [(twin, [(z, 0, 1) for z in first]), (twin_far, [(far, 0, 1)]), (side_far, [(far, 1, 0)])], value
        )
        value = px([(twin_side, [(z, 1, 1) for z in first]), (twin_side_far, [(far, 1, 1)])], value, end=True)
    else:
        groups = [[z * line + i for z in range(deep)] for i in range(line)]
        column = lax.all_to_all(jnp.tile(proj_in, (deep, 1)), "seq", 0, 0, axis_index_groups=groups, tiled=True)
        blocks = [column] + [send(column, devices, (0, x, 0)) for x in range(1, across)]
        blocks = [block if c == 0 else send(block, devices, (0, 0, c)) for block in blocks for c in range(cores)]
        value = pl.pallas_call(
            functools.partial(whole_kernel, devices),
            out_shape=feat_type,
            in_specs=[VMEM] * (2 + len(blocks)),
            out_specs=VMEM,
            scratch_shapes=[pltpu.VMEM((width, wide), jnp.bfloat16)],
            compiler_params=params,
            name="px",
        )(held, *blocks, pg_t)

    def plane(block):
        held = {(0, x, 0): send(block, devices, (0, x, 0)) if x else block for x in range(across)}
        return {(*k[:2], c): send(v, devices, (0, 0, c)) if c else v for c in range(cores) for k, v in held.items()}

    feats = plane(value)
    lanes = layers * square // line
    sums = pl.pallas_call(
        functools.partial(grads_kernel, devices, per_part, layers, rows, tuple(feats)),
        out_shape=jax.ShapeDtypeStruct((per_row, lanes), jnp.bfloat16),
        in_specs=[VMEM] * (len(feats) + 1),
        out_specs=VMEM,
        scratch_shapes=[pltpu.VMEM((wide, rows * line), jnp.float32)],
        compiler_params=params,
        name="grads",
    )(*feats.values(), lengths)
    terms = [send(sums, devices, (z, 0, 0)) if z else sums for z in range(deep)]
    total = pl.pallas_call(
        functools.partial(total_kernel, devices, per_part),
        out_shape=jax.ShapeDtypeStruct((seqs, lanes), jnp.bfloat16),
        in_specs=[VMEM] * deep,
        out_specs=VMEM,
        compiler_params=params,
        name="total",
    )(*terms)
    full = plane(total)
    return pl.pallas_call(
        functools.partial(covariance_kernel, devices, tuple(full)),
        out_shape=[
            jax.ShapeDtypeStruct((CAP, layers * square), jnp.bfloat16),
            jax.ShapeDtypeStruct((npair, band, square), jnp.float32),
        ],
        in_specs=[VMEM] * (len(full) + 1) + [SMEM],
        out_specs=[VMEM, ANY],
        scratch_shapes=[
            pltpu.VMEM((seqs, layers * square), jnp.bfloat16),
            pltpu.VMEM((npair, band, square), jnp.float32),
            pltpu.SemaphoreType.DMA((npair * (square // min(1024, square)),)),
        ],
        compiler_params=params,
        name="covariance",
    )(*full.values(), slots.reshape(1, seqs), pairs)


def solution(mesh):
    in_specs = (
        P(None, ("groups", "seq"), None),
        P(None, ("groups", "seq"), None),
        P("seq", None),
        P(),
        P("groups", None),
        P("groups"),
        P(),
    )
    out_specs = (P(("groups", "seq"), None), P("groups", "seq", None))
    return jax.shard_map(shards, mesh=mesh, in_specs=in_specs, out_specs=out_specs, check_vma=False)
```

```python
import functools

import jax
import jax.numpy as jnp
from jax import lax
from jax.experimental import pallas as pl
from jax.experimental.pallas import tpu as pltpu
from jax.sharding import PartitionSpec as P

CAP = 2
MIB = 1 << 20
VMEM = pl.BlockSpec(memory_space=pltpu.VMEM)
SMEM = pl.BlockSpec(memory_space=pltpu.SMEM)
ANY = pl.BlockSpec(memory_space=pl.ANY)
HBM = pl.BlockSpec(memory_space=pltpu.HBM)


def levels(devices):
    cores = 2 if devices % 2 == 0 else 1
    wide = 4 if devices >= 64 and devices % 8 == 0 else 2 if devices % 4 == 0 else 1
    return devices // (cores * wide), wide, cores


def place(index, devices):
    _, wide, cores = levels(devices)
    return index // (wide * cores), index // cores % wide, index % cores


def owner(me, devices, shift):
    deep, wide, cores = levels(devices)
    z, x, core = place(me, devices)
    z = (z + (deep - shift[0])) % deep
    x = (x + (wide - shift[1])) % wide
    core = (core + (cores - shift[2])) % cores
    return (z * wide + x) * cores + core


def send(value, devices, shift):
    deep, wide, cores = levels(devices)
    perm = []
    for i in range(devices):
        z, x, core = place(i, devices)
        z, x, core = (z + shift[0]) % deep, (x + shift[1]) % wide, (core + shift[2]) % cores
        perm.append((i, (z * wide + x) * cores + core))
    return lax.ppermute(value, "seq", perm)


def chunks(spot, devices, square):
    deep, wide, cores = levels(devices)
    line = wide * cores
    band = square // devices
    if band % 128:
        return [(0, spot * (square // line), square // line)]
    return [(z * band, (z * line + spot) * band, band) for z in range(deep)]


def load_kernel(acts, cots, proj_in, proj_out, held, own, pg_t, cots_held, weights, sems):
    layers = cots.shape[0]
    width_k = proj_out.shape[1] // layers
    pairs = [(proj_out, weights), (cots, cots_held), (proj_in, own), (acts, held)]
    copies = [pltpu.make_async_copy(a, b, sems.at[i]) for i, (a, b) in enumerate(pairs)]
    for copy in copies:
        copy.start()
    copies[0].wait()
    copies[1].wait()
    for l in range(layers):
        pg = jnp.dot(cots_held[l], weights[...], preferred_element_type=jnp.float32)
        pg_t[l * width_k:(l + 1) * width_k, :] = pg.T[l * width_k:(l + 1) * width_k, :].astype(jnp.bfloat16)
    copies[2].wait()
    copies[3].wait()


def stack_kernel(count, *refs):
    out = refs[-1]
    at = 0
    for ref in refs[:count]:
        out[at:at + ref.shape[0], :] = ref[...]
        at += ref.shape[0]


def px_kernel(devices, keys, begin, end, keep, acts, *refs):
    count = len(keys)
    arrays, refs = refs[:count], refs[count:]
    layers, rows, _ = acts.shape
    wide = arrays[0].shape[1]
    me = lax.axis_index("seq")
    if keep:
        stack_kernel(count, *arrays, refs[-1])
        refs = refs[:-1]
    total = [jnp.zeros((rows, wide), jnp.float32) if begin else refs[0][l] for l in range(layers)]
    for array, shifts in zip(arrays, keys):
        tall = array.shape[0] // len(shifts)
        for i, shift in enumerate(shifts):
            at = pl.ds(pl.multiple_of(owner(me, devices, shift) * tall, tall), tall)
            block = array[i * tall:(i + 1) * tall, :]
            for l in range(layers):
                total[l] = total[l] + jnp.dot(acts[l, :, at], block, preferred_element_type=jnp.float32)
    if end:
        pack(total, refs[-2], refs[-1])
    else:
        for l in range(layers):
            refs[-1][l] = total[l]


def pack(total, pg_t, out):
    layers = len(total)
    rows, wide = total[0].shape
    width_k = wide // layers
    for l in range(layers):
        at = slice(l * width_k, (l + 1) * width_k)
        out[:rows, at] = total[l][:, at].astype(jnp.bfloat16)
    for i in range(rows // wide):
        out[rows + i * wide:rows + (i + 1) * wide, :] = pg_t[:, i * wide:(i + 1) * wide]


def whole_kernel(devices, acts, *refs):
    blocks, (pg_t, out, weights) = refs[:-3], refs[-3:]
    deep, wide, cores = levels(devices)
    me = lax.axis_index("seq")
    tall = blocks[0].shape[0] // deep
    for i, block in enumerate(blocks):
        for z in range(deep):
            at = owner(me, devices, (0, i // cores, i % cores)) % (wide * cores) + z * wide * cores
            weights[pl.ds(pl.multiple_of(at * tall, tall), tall), :] = block[z * tall:(z + 1) * tall, :]
    pack([jnp.dot(acts[l], weights[...], preferred_element_type=jnp.float32) for l in range(acts.shape[0])], pg_t, out)


def grads_kernel(devices, per_part, layers, rows, shifts, *refs):
    count = len(shifts)
    feats, (lengths, out, spread) = refs[:count], refs[count:]
    wide = feats[0].shape[1]
    runs = rows // wide
    width_k = wide // layers
    square = width_k * width_k
    _, across, cores = levels(devices)
    me = lax.axis_index("seq")
    sizes = lengths[pl.ds(me // per_part, 1), :]
    per_row = sizes.shape[1]
    upto = lax.broadcasted_iota(jnp.int32, (per_row, per_row), 1)
    which = lax.broadcasted_iota(jnp.int32, (per_row, per_row), 0)
    sizes = jnp.broadcast_to(sizes, (per_row, per_row))
    ends = jnp.sum(jnp.where(upto <= which, sizes, 0), axis=1, keepdims=True)
    starts = jnp.sum(jnp.where(upto < which, sizes, 0), axis=1, keepdims=True)
    member = []
    for shift in shifts:
        first = (owner(me, devices, shift) % per_part) * rows
        position = first + lax.broadcasted_iota(jnp.int32, (per_row, wide), 1)
        for i in range(runs):
            now = position + i * wide
            member.append(((now >= starts) & (now < ends)).astype(jnp.float32))
    member = jnp.concatenate(member, axis=1)
    for f, feat in enumerate(feats):
        for i in range(runs):
            at = (f * runs + i) * wide
            spread[:, at:at + wide] = feat[rows + i * wide:rows + (i + 1) * wide, :].astype(jnp.float32)
    low = lax.broadcasted_iota(jnp.int32, (per_row, 2 * width_k), 1) < width_k
    lanes = square // (across * cores)
    spot = me % (across * cores)
    for l in range(layers):
        px = []
        for feat in feats:
            own = feat[:rows, l * width_k:(l + 1) * width_k]
            px.append(jnp.concatenate([own, own], axis=1))
        px = jnp.concatenate(px, axis=0)
        for here, there, size in chunks(spot, devices, square):
            terms = []
            for i in range(size // width_k):
                row = l * width_k + there // width_k + i
                terms.append((member * spread[pl.ds(row, 1), :]).astype(jnp.bfloat16))
            sums = jnp.dot(jnp.concatenate(terms, axis=0), px, preferred_element_type=jnp.float32)
            for i in range(0, size // width_k, 2):
                even = sums[i * per_row:(i + 1) * per_row]
                odd = sums[(i + 1) * per_row:(i + 2) * per_row]
                at = l * lanes + here + i * width_k
                out[:, at:at + 2 * width_k] = jnp.where(low, even, odd).astype(jnp.bfloat16)


def total_kernel(devices, per_part, *refs):
    terms, out = refs[:-1], refs[-1]
    deep, across, cores = levels(devices)
    tall = terms[0].shape[0]
    if out.shape[0] == tall:
        total = terms[0][...].astype(jnp.float32)
        for term in terms[1:]:
            total = total + term[...].astype(jnp.float32)
        out[...] = total.astype(jnp.bfloat16)
        return
    me = lax.axis_index("seq")
    owned = [owner(me, devices, (shift, 0, 0)) // per_part for shift in range(deep)]
    for row in range(out.shape[0] // tall):
        total = jnp.zeros(terms[0].shape, jnp.float32)
        for home, term in zip(owned, terms):
            total = total + jnp.where(home == row, term[...].astype(jnp.float32), 0.0)
        out[row * tall:(row + 1) * tall, :] = total.astype(jnp.bfloat16)


def covariance_kernel(devices, shifts, *refs):
    count = len(shifts)
    blocks, (slots, pairs, logged, out, right, held, sems) = refs[:count], refs[count:]
    npair, band, square = held.shape
    seqs, full = right.shape
    layers = full // square
    _, across, cores = levels(devices)
    lanes = square // (across * cores)
    me = lax.axis_index("seq")
    for shift, block in zip(shifts, blocks):
        spot = owner(me, devices, shift) % (across * cores)
        for here, there, size in chunks(spot, devices, square):
            for l in range(layers):
                at = pl.multiple_of(l * square + there, size)
                right[:, pl.ds(at, size)] = block[:, l * lanes + here:l * lanes + here + size]
    scale = jnp.float32(1.0 / seqs)
    cols = min(1024, square)
    steps = square // cols
    copies = []
    for p in range(npair):
        if band % 128 == 0:
            at = pl.multiple_of(pairs[p, 0] * square + me * band, band)
            left = right[:, pl.ds(at, band)]
        else:
            offset = me * band
            at = pl.multiple_of(pairs[p, 0] * square + (offset // 128) * 128, 128)
            source = lax.broadcasted_iota(jnp.int32, (128, band), 0)
            target = lax.broadcasted_iota(jnp.int32, (128, band), 1)
            pick = (source == target + offset % 128).astype(jnp.float32).astype(jnp.bfloat16)
            left = jnp.dot(right[:, pl.ds(at, 128)], pick, preferred_element_type=jnp.float32).astype(jnp.bfloat16)
        for q in range(steps):
            at = pl.multiple_of(pairs[p, 1] * square + q * cols, cols)
            product = lax.dot_general(
                left, right[:, pl.ds(at, cols)], (((0,), (0,)), ((), ())), preferred_element_type=jnp.float32
            )
            held[p, :, q * cols:(q + 1) * cols] = product * scale
            where = (p, slice(None), pl.ds(q * cols, cols))
            copy = pltpu.make_async_copy(held.at[where], out.at[where], sems.at[p * steps + q])
            copy.start()
            copies.append(copy)
    own = me * CAP + lax.broadcasted_iota(jnp.int32, (CAP, seqs), 0)
    picker = (jnp.broadcast_to(slots[...], (CAP, seqs)) == own).astype(jnp.float32).astype(jnp.bfloat16)
    logged[...] = jnp.dot(picker, right[...], preferred_element_type=jnp.float32).astype(jnp.bfloat16)
    for copy in copies:
        copy.wait()


def part_kernel(devices, shifts, more, mine, *refs):
    array, refs = refs[0], refs[1:]
    if more:
        rest, slots = refs[:len(more) - 1], refs[len(more) - 1]
        refs = refs[len(more):]
    pairs, (side, out, held, sems) = refs[0], refs[-4:]
    npair, band, _ = held.shape
    seqs, full = mine.shape
    deep, across, cores = levels(devices)
    line = across * cores
    square = band * devices
    lanes = square // line
    layers = full // lanes
    me = lax.axis_index("seq")
    scale = jnp.float32(1.0 / seqs)
    copies = []
    for p in range(npair):
        at = pl.multiple_of(pairs[p, 0] * lanes + me // line * band, band)
        left = mine[:, pl.ds(at, band)]
        for i, shift in enumerate(shifts):
            spot = owner(me, devices, shift) % line
            right = array[i * seqs:(i + 1) * seqs, pl.ds(pl.multiple_of(pairs[p, 1] * lanes, lanes), lanes)]
            product = lax.dot_general(left, right, (((0,), (0,)), ((), ())), preferred_element_type=jnp.float32)
            held[p, :, i * lanes:(i + 1) * lanes] = product * scale
            for here, there, size in chunks(spot, devices, square):
                to = pl.ds(pl.multiple_of(there, size), size)
                copies.append(
                    pltpu.make_async_copy(held.at[p, :, pl.ds(i * lanes + here, size)], out.at[p, :, to], sems.at[len(copies)])
                )
                copies[-1].start()
    if not more:
        side[...] = jnp.zeros(side.shape, side.dtype)
    else:
        own = me * CAP + lax.broadcasted_iota(jnp.int32, (CAP, seqs), 0)
        picker = (jnp.broadcast_to(slots[...], (CAP, seqs)) == own).astype(jnp.float32).astype(jnp.bfloat16)
        blocks = [array[i * seqs:(i + 1) * seqs, :] for i in range(len(shifts))] + [ref[...] for ref in (mine, *rest)]
        for shift, block in zip((*shifts, *more), blocks):
            spot = owner(me, devices, shift) % line
            picked = jnp.dot(picker, block, preferred_element_type=jnp.float32).astype(jnp.bfloat16)
            for here, there, size in chunks(spot, devices, square):
                for l in range(layers):
                    to = pl.ds(pl.multiple_of(l * square + there, size), size)
                    side[:, to] = picked[:, l * lanes + here:l * lanes + here + size]
    for copy in copies:
        copy.wait()


def shards(acts, cots, proj_in, proj_out, lengths, slots, pairs):
    layers, rows, width = acts.shape
    wide = proj_out.shape[1]
    width_k = wide // layers
    square = width_k * width_k
    devices = lax.axis_size("seq")
    rows_all, per_row = lengths.shape
    seqs = slots.shape[0]
    npair = pairs.shape[0]
    per_part = devices // rows_all
    band = square // devices
    deep, across, cores = levels(devices)
    line = across * cores
    tall = proj_in.shape[0]
    params = pltpu.CompilerParams(vmem_limit_bytes=24 * MIB)

    light = pl.CostEstimate(flops=1, bytes_accessed=1, transcendentals=0)
    held, own, pg_t = pl.pallas_call(
        load_kernel,
        out_shape=(
            pltpu.VMEM(acts.shape, jnp.bfloat16),
            pltpu.VMEM(proj_in.shape, jnp.bfloat16),
            pltpu.VMEM((wide, rows), jnp.bfloat16),
        ),
        in_specs=[HBM] * 4,
        out_specs=(VMEM,) * 3,
        scratch_shapes=[
            pltpu.VMEM(cots.shape, jnp.bfloat16),
            pltpu.VMEM(proj_out.shape, jnp.bfloat16),
            pltpu.SemaphoreType.DMA((4,)),
        ],
        compiler_params=params,
        cost_estimate=light,
        name="load",
    )(*[pltpu.with_memory_space_constraint(a, pltpu.HBM) for a in (acts, cots, proj_in, proj_out)])

    def stack(arrays, after):
        return pl.pallas_call(
            functools.partial(stack_kernel, len(arrays)),
            out_shape=jax.ShapeDtypeStruct((sum(a.shape[0] for a in arrays), arrays[0].shape[1]), jnp.bfloat16),
            in_specs=[VMEM] * len(arrays) + [ANY] * len(after),
            out_specs=VMEM,
            compiler_params=params,
            cost_estimate=light,
            name="stack",
        )(*arrays, *after)

    def px(entries, before=None, end=False, keep=False):
        more = (() if before is None else (before,)) + ((pg_t,) if end else ())
        arrays, keys = zip(*entries)
        count = sum(map(len, keys))
        sums = feat_type if end else jax.ShapeDtypeStruct((layers, rows, wide), jnp.float32)
        stacked = [jax.ShapeDtypeStruct((count * tall, wide), jnp.bfloat16)] if keep else []
        result = pl.pallas_call(
            functools.partial(px_kernel, devices, keys, before is None, end, keep),
            out_shape=[sums] + stacked,
            in_specs=[VMEM] * (1 + len(arrays) + len(more)),
            out_specs=[VMEM] * (1 + len(stacked)),
            compiler_params=params,
            cost_estimate=light,
            name="px",
        )(held, *arrays, *more)
        return result if keep else result[0]

    feat_type = jax.ShapeDtypeStruct((2 * rows, wide), jnp.bfloat16)
    if tall % 128 == 0 and deep > 2 and across == 2 and cores == 2:
        spins = sorted(range(1, deep), key=lambda z: min(z, deep - z))
        near, far = spins[:-1], spins[-1]
        got = [send(proj_in, devices, (z, 0, 0)) for z in near]
        side = send(proj_in, devices, (0, 1, 0))
        got_far = send(proj_in, devices, (far, 0, 0))
        got = stack(got, (pg_t, side))
        side_near = send(got, devices, (0, 1, 0))
        side_far = send(got_far, devices, (0, 1, 0))
        value, column = px(
            [(own, [(0, 0, 0)]), (got, [(z, 0, 0) for z in near]), (got_far, [(far, 0, 0)])], keep=True
        )
        twin = send(column, devices, (0, 0, 1))
        side = stack([side, side_near, side_far], (value,))
        twin_side = send(side, devices, (0, 0, 1))
        order = [0, *near, far]
        value = px([(side, [(z, 1, 0) for z in order]), (twin, [(z, 0, 1) for z in order])], value)
        value = px([(twin_side, [(z, 1, 1) for z in order])], value, end=True)
    else:
        groups = [[z * line + i for z in range(deep)] for i in range(line)]
        column = lax.all_to_all(jnp.tile(proj_in, (deep, 1)), "seq", 0, 0, axis_index_groups=groups, tiled=True)
        blocks = [column] + [send(column, devices, (0, x, 0)) for x in range(1, across)]
        blocks = [block if c == 0 else send(block, devices, (0, 0, c)) for block in blocks for c in range(cores)]
        value = pl.pallas_call(
            functools.partial(whole_kernel, devices),
            out_shape=feat_type,
            in_specs=[VMEM] * (2 + len(blocks)),
            out_specs=VMEM,
            scratch_shapes=[pltpu.VMEM((width, wide), jnp.bfloat16)],
            compiler_params=params,
            name="px",
        )(held, *blocks, pg_t)

    def plane(block):
        held = {(0, x, 0): send(block, devices, (0, x, 0)) if x else block for x in range(across)}
        return {(*k[:2], c): send(v, devices, (0, 0, c)) if c else v for c in range(cores) for k, v in held.items()}

    feats = plane(value)
    lanes = layers * square // line
    sums = pl.pallas_call(
        functools.partial(grads_kernel, devices, per_part, layers, rows, tuple(feats)),
        out_shape=jax.ShapeDtypeStruct((per_row, lanes), jnp.bfloat16),
        in_specs=[VMEM] * (len(feats) + 1),
        out_specs=VMEM,
        scratch_shapes=[pltpu.VMEM((wide, rows * line), jnp.float32)],
        compiler_params=params,
        name="grads",
    )(*feats.values(), lengths)
    terms = [send(sums, devices, (z, 0, 0)) if z else sums for z in range(deep)]
    total = pl.pallas_call(
        functools.partial(total_kernel, devices, per_part),
        out_shape=jax.ShapeDtypeStruct((seqs, lanes), jnp.bfloat16),
        in_specs=[VMEM] * deep,
        out_specs=VMEM,
        compiler_params=params,
        name="total",
    )(*terms)
    logged_type = jax.ShapeDtypeStruct((CAP, layers * square), jnp.bfloat16)
    covariance_type = jax.ShapeDtypeStruct((npair, band, square), jnp.float32)
    if band % 128 == 0 and across == 2 and cores == 2:
        width = square // line
        shape = (npair, band, width)
        covariance = None
        side = send(total, devices, (0, 1, 0))
        for shifts in (((0, 0, 0),), ((0, 1, 0),), ((0, 0, 1), (0, 1, 1))):
            last = len(shifts) > 1
            arrays = [total, total if covariance is None else send(both, devices, (0, 0, 1)) if last else side]
            specs = [VMEM] * len(arrays)
            more = ()
            if last:
                more = ((0, 0, 0), (0, 1, 0))
                arrays += [side, slots.reshape(1, seqs)]
                specs += [VMEM, VMEM]
            arrays.append(pairs)
            specs.append(SMEM)
            alias = {}
            if covariance is not None:
                alias = {len(arrays): 1}
                arrays.append(covariance)
                specs.append(ANY)
            result = pl.pallas_call(
                functools.partial(part_kernel, devices, shifts, more),
                out_shape=[logged_type if last else jax.ShapeDtypeStruct((8, 128), jnp.float32), covariance_type],
                in_specs=specs,
                out_specs=[VMEM, ANY],
                scratch_shapes=[
                    pltpu.VMEM((npair, band, len(shifts) * width), jnp.float32),
                    pltpu.SemaphoreType.DMA((npair * len(shifts) * deep,)),
                ],
                input_output_aliases=alias,
                compiler_params=params,
                cost_estimate=pl.CostEstimate(
                    flops=2 * npair * seqs * band * width * len(shifts),
                    bytes_accessed=4 * npair * band * width * len(shifts),
                    transcendentals=0,
                ),
                name="covariance",
            )(*arrays)
            if covariance is None:
                both = stack([total, side], (result[0],))
            covariance = result[1]
        return result[0], covariance
    full = plane(total)
    return pl.pallas_call(
        functools.partial(covariance_kernel, devices, tuple(full)),
        out_shape=[logged_type, covariance_type],
        in_specs=[VMEM] * (len(full) + 1) + [SMEM],
        out_specs=[VMEM, ANY],
        scratch_shapes=[
            pltpu.VMEM((seqs, layers * square), jnp.bfloat16),
            pltpu.VMEM((npair, band, square), jnp.float32),
            pltpu.SemaphoreType.DMA((npair * (square // min(1024, square)),)),
        ],
        compiler_params=params,
        name="covariance",
    )(*full.values(), slots.reshape(1, seqs), pairs)


def solution(mesh):
    in_specs = (
        P(None, ("groups", "seq"), None),
        P(None, ("groups", "seq"), None),
        P("seq", None),
        P(),
        P("groups", None),
        P("groups"),
        P(),
    )
    out_specs = (P(("groups", "seq"), None), P("groups", "seq", None))
    return jax.shard_map(shards, mesh=mesh, in_specs=in_specs, out_specs=out_specs, check_vma=False)
```

```python
import functools

import jax
import jax.numpy as jnp
from jax import lax
from jax.experimental import pallas as pl
from jax.experimental.pallas import tpu as pltpu
from jax.sharding import PartitionSpec as P

CAP = 2
MIB = 1 << 20
VMEM = pl.BlockSpec(memory_space=pltpu.VMEM)
SMEM = pl.BlockSpec(memory_space=pltpu.SMEM)
ANY = pl.BlockSpec(memory_space=pl.ANY)
HBM = pl.BlockSpec(memory_space=pltpu.HBM)


def levels(devices):
    cores = 2 if devices % 2 == 0 else 1
    wide = 4 if devices >= 64 and devices % 8 == 0 else 2 if devices % 4 == 0 else 1
    return devices // (cores * wide), wide, cores


def place(index, devices):
    _, wide, cores = levels(devices)
    return index // (wide * cores), index // cores % wide, index % cores


def owner(me, devices, shift):
    deep, wide, cores = levels(devices)
    z, x, core = place(me, devices)
    z = (z + (deep - shift[0])) % deep
    x = (x + (wide - shift[1])) % wide
    core = (core + (cores - shift[2])) % cores
    return (z * wide + x) * cores + core


def send(value, devices, shift):
    deep, wide, cores = levels(devices)
    perm = []
    for i in range(devices):
        z, x, core = place(i, devices)
        z, x, core = (z + shift[0]) % deep, (x + shift[1]) % wide, (core + shift[2]) % cores
        perm.append((i, (z * wide + x) * cores + core))
    return lax.ppermute(value, "seq", perm)


def load_kernel(acts, cots, proj_in, proj_out, held, own, pg_t, cots_held, weights, sems):
    layers = cots.shape[0]
    width_k = proj_out.shape[1] // layers
    pairs = [(proj_out, weights), (cots, cots_held), (proj_in, own), (acts, held)]
    copies = [pltpu.make_async_copy(a, b, sems.at[i]) for i, (a, b) in enumerate(pairs)]
    for copy in copies:
        copy.start()
    copies[0].wait()
    copies[1].wait()
    for l in range(layers):
        pg = jnp.dot(cots_held[l], weights[...], preferred_element_type=jnp.float32)
        pg_t[l * width_k:(l + 1) * width_k, :] = pg.T[l * width_k:(l + 1) * width_k, :].astype(jnp.bfloat16)
    copies[2].wait()
    copies[3].wait()


def stack_kernel(count, *refs):
    out = refs[-1]
    at = 0
    for ref in refs[:count]:
        out[at:at + ref.shape[0], :] = ref[...]
        at += ref.shape[0]


def px_kernel(devices, keys, begin, end, keep, acts, *refs):
    count = len(keys)
    arrays, refs = refs[:count], refs[count:]
    layers, rows, _ = acts.shape
    wide = arrays[0].shape[1]
    me = lax.axis_index("seq")
    if keep:
        stack_kernel(count, *arrays, refs[-1])
        refs = refs[:-1]
    total = [jnp.zeros((rows, wide), jnp.float32) if begin else refs[0][l] for l in range(layers)]
    for array, shifts in zip(arrays, keys):
        tall = array.shape[0] // len(shifts)
        for i, shift in enumerate(shifts):
            at = pl.ds(pl.multiple_of(owner(me, devices, shift) * tall, tall), tall)
            block = array[i * tall:(i + 1) * tall, :]
            for l in range(layers):
                total[l] = total[l] + jnp.dot(acts[l, :, at], block, preferred_element_type=jnp.float32)
    if end:
        pack(total, refs[-2], refs[-1])
    else:
        for l in range(layers):
            refs[-1][l] = total[l]


def pack(total, pg_t, out):
    layers = len(total)
    rows, wide = total[0].shape
    width_k = wide // layers
    for l in range(layers):
        at = slice(l * width_k, (l + 1) * width_k)
        out[:rows, at] = total[l][:, at].astype(jnp.bfloat16)
    for i in range(rows // wide):
        out[rows + i * wide:rows + (i + 1) * wide, :] = pg_t[:, i * wide:(i + 1) * wide]


def whole_kernel(devices, acts, *refs):
    blocks, (pg_t, out, weights) = refs[:-3], refs[-3:]
    deep, wide, cores = levels(devices)
    me = lax.axis_index("seq")
    tall = blocks[0].shape[0] // deep
    for i, block in enumerate(blocks):
        for z in range(deep):
            at = owner(me, devices, (0, i // cores, i % cores)) % (wide * cores) + z * wide * cores
            weights[pl.ds(pl.multiple_of(at * tall, tall), tall), :] = block[z * tall:(z + 1) * tall, :]
    pack([jnp.dot(acts[l], weights[...], preferred_element_type=jnp.float32) for l in range(acts.shape[0])], pg_t, out)


def grads_kernel(devices, per_part, layers, rows, shifts, *refs):
    count = len(shifts)
    feats, lengths, outs, spread = refs[:count], refs[count], refs[count + 1:-1], refs[-1]
    wide = feats[0].shape[1]
    runs = rows // wide
    width_k = wide // layers
    square = width_k * width_k
    deep, across, cores = levels(devices)
    me = lax.axis_index("seq")
    sizes = lengths[pl.ds(me // per_part, 1), :]
    per_row = sizes.shape[1]
    upto = lax.broadcasted_iota(jnp.int32, (per_row, per_row), 1)
    which = lax.broadcasted_iota(jnp.int32, (per_row, per_row), 0)
    sizes = jnp.broadcast_to(sizes, (per_row, per_row))
    ends = jnp.sum(jnp.where(upto <= which, sizes, 0), axis=1, keepdims=True)
    starts = jnp.sum(jnp.where(upto < which, sizes, 0), axis=1, keepdims=True)
    member = []
    for shift in shifts:
        first = (owner(me, devices, shift) % per_part) * rows
        position = first + lax.broadcasted_iota(jnp.int32, (per_row, wide), 1)
        for i in range(runs):
            now = position + i * wide
            member.append(((now >= starts) & (now < ends)).astype(jnp.float32))
    member = jnp.concatenate(member, axis=1)
    for f, feat in enumerate(feats):
        for i in range(runs):
            at = (f * runs + i) * wide
            spread[:, at:at + wide] = feat[rows + i * wide:rows + (i + 1) * wide, :].astype(jnp.float32)
    low = lax.broadcasted_iota(jnp.int32, (per_row, 2 * width_k), 1) < width_k
    line = across * cores
    spot = me % line
    if len(outs) == 1:
        size = square // line
        homes = [spot]
    else:
        size = square // devices
        homes = [(me // line + k) % deep * line + spot for k in range(deep)]
    for l in range(layers):
        px = []
        for feat in feats:
            own = feat[:rows, l * width_k:(l + 1) * width_k]
            px.append(jnp.concatenate([own, own], axis=1))
        px = jnp.concatenate(px, axis=0)
        for home, out in zip(homes, outs):
            terms = []
            for i in range(size // width_k):
                row = l * width_k + home * (size // width_k) + i
                terms.append((member * spread[pl.ds(row, 1), :]).astype(jnp.bfloat16))
            sums = jnp.dot(jnp.concatenate(terms, axis=0), px, preferred_element_type=jnp.float32)
            for i in range(0, size // width_k, 2):
                even = sums[i * per_row:(i + 1) * per_row]
                odd = sums[(i + 1) * per_row:(i + 2) * per_row]
                at = l * size + i * width_k
                out[:, at:at + 2 * width_k] = jnp.where(low, even, odd).astype(jnp.bfloat16)


def total_kernel(devices, per_part, *refs):
    terms, out = refs[:-1], refs[-1]
    deep, across, cores = levels(devices)
    tall = terms[0].shape[0]
    if out.shape[0] == tall:
        total = terms[0][...].astype(jnp.float32)
        for term in terms[1:]:
            total = total + term[...].astype(jnp.float32)
        out[...] = total.astype(jnp.bfloat16)
        return
    me = lax.axis_index("seq")
    owned = [owner(me, devices, (shift, 0, 0)) // per_part for shift in range(deep)]
    for row in range(out.shape[0] // tall):
        total = jnp.zeros(terms[0].shape, jnp.float32)
        for home, term in zip(owned, terms):
            total = total + jnp.where(home == row, term[...].astype(jnp.float32), 0.0)
        out[row * tall:(row + 1) * tall, :] = total.astype(jnp.bfloat16)


def covariance_kernel(devices, shifts, *refs):
    count = len(shifts)
    blocks, (slots, pairs, logged, out, right, held, sems) = refs[:count], refs[count:]
    npair, band, square = held.shape
    seqs, full = right.shape
    layers = full // square
    _, across, cores = levels(devices)
    lanes = square // (across * cores)
    me = lax.axis_index("seq")
    for shift, block in zip(shifts, blocks):
        spot = owner(me, devices, shift) % (across * cores)
        for l in range(layers):
            at = pl.multiple_of(l * square + spot * lanes, lanes)
            right[:, pl.ds(at, lanes)] = block[:, l * lanes:(l + 1) * lanes]
    scale = jnp.float32(1.0 / seqs)
    cols = min(1024, square)
    steps = square // cols
    copies = []
    for p in range(npair):
        if band % 128 == 0:
            at = pl.multiple_of(pairs[p, 0] * square + me * band, band)
            left = right[:, pl.ds(at, band)]
        else:
            offset = me * band
            at = pl.multiple_of(pairs[p, 0] * square + (offset // 128) * 128, 128)
            source = lax.broadcasted_iota(jnp.int32, (128, band), 0)
            target = lax.broadcasted_iota(jnp.int32, (128, band), 1)
            pick = (source == target + offset % 128).astype(jnp.float32).astype(jnp.bfloat16)
            left = jnp.dot(right[:, pl.ds(at, 128)], pick, preferred_element_type=jnp.float32).astype(jnp.bfloat16)
        for q in range(steps):
            at = pl.multiple_of(pairs[p, 1] * square + q * cols, cols)
            product = lax.dot_general(
                left, right[:, pl.ds(at, cols)], (((0,), (0,)), ((), ())), preferred_element_type=jnp.float32
            )
            held[p, :, q * cols:(q + 1) * cols] = product * scale
            where = (p, slice(None), pl.ds(q * cols, cols))
            copy = pltpu.make_async_copy(held.at[where], out.at[where], sems.at[p * steps + q])
            copy.start()
            copies.append(copy)
    own = me * CAP + lax.broadcasted_iota(jnp.int32, (CAP, seqs), 0)
    picker = (jnp.broadcast_to(slots[...], (CAP, seqs)) == own).astype(jnp.float32).astype(jnp.bfloat16)
    logged[...] = jnp.dot(picker, right[...], preferred_element_type=jnp.float32).astype(jnp.bfloat16)
    for copy in copies:
        copy.wait()


def part_kernel(devices, keys, more, count, mine, *refs):
    arrays, refs = refs[:len(keys)], refs[len(keys):]
    pairs, (side, out, held, sems) = refs[count], refs[-4:]
    _, band, _ = held.shape
    npair = pairs.shape[0]
    seqs, full = mine.shape
    square = band * devices
    layers = full // band
    me = lax.axis_index("seq")
    scale = jnp.float32(1.0 / seqs)

    def pieces(shifts, array):
        return [(owner(me, devices, shift), array.at[pl.ds(i * seqs, seqs)]) for i, shift in enumerate(shifts)]

    bands = [piece for shifts, array in zip(keys, arrays) for piece in pieces(shifts, array)]
    copies = []
    for p in range(npair):
        at = pl.multiple_of(pairs[p, 0] * band, band)
        left = mine[:, pl.ds(at, band)].astype(jnp.float32).T.astype(jnp.bfloat16)
        at = pl.multiple_of(pairs[p, 1] * band, band)
        for home, piece in bands:
            i = len(copies)
            held[i] = jnp.dot(left, piece[:, pl.ds(at, band)], preferred_element_type=jnp.float32) * scale
            to = pl.ds(pl.multiple_of(home * band, band), band)
            copies.append(pltpu.make_async_copy(held.at[i], out.at[p, :, to], sems.at[i]))
            copies[-1].start()
    if not more:
        side[...] = jnp.zeros(side.shape, side.dtype)
    else:
        rest, slots = refs[0], refs[1]
        own = me * CAP + lax.broadcasted_iota(jnp.int32, (CAP, seqs), 0)
        picker = (jnp.broadcast_to(slots[...], (CAP, seqs)) == own).astype(jnp.float32).astype(jnp.bfloat16)
        bands = bands + pieces(more, rest)
        values = jnp.concatenate([piece[...] for _, piece in bands], axis=1)
        picked = jnp.dot(picker, values, preferred_element_type=jnp.float32).astype(jnp.bfloat16)
        for i, (home, _) in enumerate(bands):
            for l in range(layers):
                to = pl.ds(pl.multiple_of(l * square + home * band, band), band)
                side[:, to] = picked[:, i * full + l * band:i * full + (l + 1) * band]
    for copy in copies:
        copy.wait()


def shards(acts, cots, proj_in, proj_out, lengths, slots, pairs):
    layers, rows, width = acts.shape
    wide = proj_out.shape[1]
    width_k = wide // layers
    square = width_k * width_k
    devices = lax.axis_size("seq")
    rows_all, per_row = lengths.shape
    seqs = slots.shape[0]
    npair = pairs.shape[0]
    per_part = devices // rows_all
    band = square // devices
    deep, across, cores = levels(devices)
    line = across * cores
    tall = proj_in.shape[0]
    params = pltpu.CompilerParams(vmem_limit_bytes=24 * MIB)

    light = pl.CostEstimate(flops=1, bytes_accessed=1, transcendentals=0)
    held, own, pg_t = pl.pallas_call(
        load_kernel,
        out_shape=(
            pltpu.VMEM(acts.shape, jnp.bfloat16),
            pltpu.VMEM(proj_in.shape, jnp.bfloat16),
            pltpu.VMEM((wide, rows), jnp.bfloat16),
        ),
        in_specs=[HBM] * 4,
        out_specs=(VMEM,) * 3,
        scratch_shapes=[
            pltpu.VMEM(cots.shape, jnp.bfloat16),
            pltpu.VMEM(proj_out.shape, jnp.bfloat16),
            pltpu.SemaphoreType.DMA((4,)),
        ],
        compiler_params=params,
        cost_estimate=light,
        name="load",
    )(*[pltpu.with_memory_space_constraint(a, pltpu.HBM) for a in (acts, cots, proj_in, proj_out)])

    def stack(arrays, after):
        return pl.pallas_call(
            functools.partial(stack_kernel, len(arrays)),
            out_shape=jax.ShapeDtypeStruct((sum(a.shape[0] for a in arrays), arrays[0].shape[1]), jnp.bfloat16),
            in_specs=[VMEM] * len(arrays) + [ANY] * len(after),
            out_specs=VMEM,
            compiler_params=params,
            cost_estimate=light,
            name="stack",
        )(*arrays, *after)

    def px(entries, before=None, end=False, keep=False):
        more = (() if before is None else (before,)) + ((pg_t,) if end else ())
        arrays, keys = zip(*entries)
        count = sum(map(len, keys))
        sums = feat_type if end else jax.ShapeDtypeStruct((layers, rows, wide), jnp.float32)
        stacked = [jax.ShapeDtypeStruct((count * tall, wide), jnp.bfloat16)] if keep else []
        result = pl.pallas_call(
            functools.partial(px_kernel, devices, keys, before is None, end, keep),
            out_shape=[sums] + stacked,
            in_specs=[VMEM] * (1 + len(arrays) + len(more)),
            out_specs=[VMEM] * (1 + len(stacked)),
            compiler_params=params,
            cost_estimate=light,
            name="px",
        )(held, *arrays, *more)
        return result if keep else result[0]

    feat_type = jax.ShapeDtypeStruct((2 * rows, wide), jnp.bfloat16)
    spins = sorted(range(1, deep), key=lambda z: min(z, deep - z))
    near, far = spins[:-1], spins[-1]
    staged = tall % 128 == 0 and deep > 2 and across == 2 and cores == 2
    if staged:
        got = [send(proj_in, devices, (z, 0, 0)) for z in near]
        side = send(proj_in, devices, (0, 1, 0))
        got_far = send(proj_in, devices, (far, 0, 0))
        got = stack(got, (pg_t, side))
        side_near = send(got, devices, (0, 1, 0))
        side_far = send(got_far, devices, (0, 1, 0))
        value, column = px(
            [(own, [(0, 0, 0)]), (got, [(z, 0, 0) for z in near]), (got_far, [(far, 0, 0)])], keep=True
        )
        twin = send(column, devices, (0, 0, 1))
        side = stack([side, side_near, side_far], (value,))
        twin_side = send(side, devices, (0, 0, 1))
        order = [0, *near, far]
        value = px([(side, [(z, 1, 0) for z in order]), (twin, [(z, 0, 1) for z in order])], value)
        value = px([(twin_side, [(z, 1, 1) for z in order])], value, end=True)
    else:
        groups = [[z * line + i for z in range(deep)] for i in range(line)]
        column = lax.all_to_all(jnp.tile(proj_in, (deep, 1)), "seq", 0, 0, axis_index_groups=groups, tiled=True)
        blocks = [column] + [send(column, devices, (0, x, 0)) for x in range(1, across)]
        blocks = [block if c == 0 else send(block, devices, (0, 0, c)) for block in blocks for c in range(cores)]
        value = pl.pallas_call(
            functools.partial(whole_kernel, devices),
            out_shape=feat_type,
            in_specs=[VMEM] * (2 + len(blocks)),
            out_specs=VMEM,
            scratch_shapes=[pltpu.VMEM((width, wide), jnp.bfloat16)],
            compiler_params=params,
            name="px",
        )(held, *blocks, pg_t)

    def plane(block):
        held = {(0, x, 0): send(block, devices, (0, x, 0)) if x else block for x in range(across)}
        return {(*k[:2], c): send(v, devices, (0, 0, c)) if c else v for c in range(cores) for k, v in held.items()}

    feats = plane(value)
    split = staged and band % 128 == 0
    lanes = layers * band if split else layers * square // line
    sums = pl.pallas_call(
        functools.partial(grads_kernel, devices, per_part, layers, rows, tuple(feats)),
        out_shape=[jax.ShapeDtypeStruct((per_row, lanes), jnp.bfloat16)] * (deep if split else 1),
        in_specs=[VMEM] * (len(feats) + 1),
        out_specs=[VMEM] * (deep if split else 1),
        scratch_shapes=[pltpu.VMEM((wide, rows * line), jnp.float32)],
        compiler_params=params,
        cost_estimate=light,
        name="grads",
    )(*feats.values(), lengths)
    sums = sums if split else sums * deep
    terms = [send(sums[z], devices, (z, 0, 0)) if z else sums[z] for z in range(deep)]
    total = pl.pallas_call(
        functools.partial(total_kernel, devices, per_part),
        out_shape=jax.ShapeDtypeStruct((seqs, lanes), jnp.bfloat16),
        in_specs=[VMEM] * deep,
        out_specs=VMEM,
        compiler_params=params,
        cost_estimate=light,
        name="total",
    )(*terms)
    logged_type = jax.ShapeDtypeStruct((CAP, layers * square), jnp.bfloat16)
    covariance_type = jax.ShapeDtypeStruct((npair, band, square), jnp.float32)

    def part(entries, before=None, more=()):
        arrays, keys = zip(*entries)
        count = sum(map(len, keys)) * npair
        extra = [more[0], slots.reshape(1, seqs)] if more else []
        operands = [total, *arrays, *extra, pairs]
        specs = [VMEM] * (len(operands) - 1) + [SMEM]
        alias = {}
        if before is not None:
            alias = {len(operands): 1}
            operands.append(before)
            specs.append(ANY)
        return pl.pallas_call(
            functools.partial(part_kernel, devices, keys, more[1] if more else (), len(extra)),
            out_shape=[logged_type if more else jax.ShapeDtypeStruct((8, 128), jnp.float32), covariance_type],
            in_specs=specs,
            out_specs=[VMEM, ANY],
            scratch_shapes=[pltpu.VMEM((count, band, band), jnp.float32), pltpu.SemaphoreType.DMA((count,))],
            input_output_aliases=alias,
            compiler_params=params,
            cost_estimate=light,
            name="covariance",
        )(*operands)

    if split:
        got = [send(total, devices, (z, 0, 0)) for z in near]
        side = send(total, devices, (0, 1, 0))
        got_far = send(total, devices, (far, 0, 0))
        got = stack(got, (side,))
        side_near = send(got, devices, (0, 1, 0))
        side_far = send(got_far, devices, (0, 1, 0))
        done, covariance = part(
            [(total, [(0, 0, 0)]), (got, [(z, 0, 0) for z in near]), (got_far, [(far, 0, 0)])]
        )
        both = stack([total, got, got_far, side, side_near, side_far], (done,))
        twin = send(both, devices, (0, 0, 1))
        order = [0, *near, far]
        _, covariance = part(
            [(side, [(0, 1, 0)]), (side_near, [(z, 1, 0) for z in near]), (side_far, [(far, 1, 0)])], covariance
        )
        logged, covariance = part(
            [(twin, [(z, x, 1) for x in range(2) for z in order])],
            covariance,
            (both, [(z, x, 0) for x in range(2) for z in order]),
        )
        return logged, covariance
    full = plane(total)
    return pl.pallas_call(
        functools.partial(covariance_kernel, devices, tuple(full)),
        out_shape=[logged_type, covariance_type],
        in_specs=[VMEM] * (len(full) + 1) + [SMEM],
        out_specs=[VMEM, ANY],
        scratch_shapes=[
            pltpu.VMEM((seqs, layers * square), jnp.bfloat16),
            pltpu.VMEM((npair, band, square), jnp.float32),
            pltpu.SemaphoreType.DMA((npair * (square // min(1024, square)),)),
        ],
        compiler_params=params,
        name="covariance",
    )(*full.values(), slots.reshape(1, seqs), pairs)


def solution(mesh):
    in_specs = (
        P(None, ("groups", "seq"), None),
        P(None, ("groups", "seq"), None),
        P("seq", None),
        P(),
        P("groups", None),
        P("groups"),
        P(),
    )
    out_specs = (P(("groups", "seq"), None), P("groups", "seq", None))
    return jax.shard_map(shards, mesh=mesh, in_specs=in_specs, out_specs=out_specs, check_vma=False)
```

```python
import functools

import jax
import jax.numpy as jnp
from jax import lax
from jax.experimental import pallas as pl
from jax.experimental.pallas import tpu as pltpu
from jax.sharding import PartitionSpec as P

CAP = 2
MIB = 1 << 20
VMEM = pl.BlockSpec(memory_space=pltpu.VMEM)
SMEM = pl.BlockSpec(memory_space=pltpu.SMEM)
ANY = pl.BlockSpec(memory_space=pl.ANY)
HBM = pl.BlockSpec(memory_space=pltpu.HBM)


def levels(devices):
    cores = 2 if devices % 2 == 0 else 1
    wide = 4 if devices >= 64 and devices % 8 == 0 else 2 if devices % 4 == 0 else 1
    return devices // (cores * wide), wide, cores


def place(index, devices):
    _, wide, cores = levels(devices)
    return index // (wide * cores), index // cores % wide, index % cores


def owner(me, devices, shift):
    deep, wide, cores = levels(devices)
    z, x, core = place(me, devices)
    z = (z + (deep - shift[0])) % deep
    x = (x + (wide - shift[1])) % wide
    core = (core + (cores - shift[2])) % cores
    return (z * wide + x) * cores + core


def send(value, devices, shift):
    deep, wide, cores = levels(devices)
    perm = []
    for i in range(devices):
        z, x, core = place(i, devices)
        z, x, core = (z + shift[0]) % deep, (x + shift[1]) % wide, (core + shift[2]) % cores
        perm.append((i, (z * wide + x) * cores + core))
    return lax.ppermute(value, "seq", perm)


def chunks(spot, devices, square):
    deep, wide, cores = levels(devices)
    line = wide * cores
    band = square // devices
    if band % 128:
        return [(0, spot * (square // line), square // line)]
    return [(z * band, (z * line + spot) * band, band) for z in range(deep)]


def load_kernel(devices, staged, acts, cots, proj_in, proj_out, *refs):
    own, pg_t, cots_held, weights, sems = refs[-5:]
    layers = cots.shape[0]
    width_k = proj_out.shape[1] // layers
    pairs = [(proj_out, weights), (cots, cots_held), (proj_in, own)]
    if staged:
        tall = proj_in.shape[0]
        me = lax.axis_index("seq")
        slots = [(held, b) for held in refs[1:-5] for b in range(held.shape[0])]
        slots = [*zip(slots, staged, [1] * len(staged)), *zip([(refs[0], b) for b in range(len(staged))], staged, [0] * len(staged))]
        for (held, b), shift, core in slots:
            at = pl.ds(pl.multiple_of(owner(me, devices, (*shift[:2], core)) * tall, tall), tall)
            pairs.append((acts.at[:, :, at], held.at[b]))
    else:
        pairs.append((acts, refs[0]))
    copies = [pltpu.make_async_copy(a, b, sems.at[i]) for i, (a, b) in enumerate(pairs)]
    for copy in copies:
        copy.start()
    copies[0].wait()
    copies[1].wait()
    for l in range(layers):
        pg = jnp.dot(cots_held[l], weights[...], preferred_element_type=jnp.float32)
        pg_t[l * width_k:(l + 1) * width_k, :] = pg.T[l * width_k:(l + 1) * width_k, :].astype(jnp.bfloat16)
    for copy in copies[2:]:
        copy.wait()


def stack_kernel(count, *refs):
    out = refs[-1]
    at = 0
    for ref in refs[:count]:
        out[at:at + ref.shape[0], :] = ref[...]
        at += ref.shape[0]


def joined(total):
    width_k = total[0].shape[1] // len(total)
    return jnp.concatenate([value[:, l * width_k:(l + 1) * width_k] for l, value in enumerate(total)], axis=1)


def px_kernel(devices, first, keys, begin, cuts, held, *refs):
    count = len(keys)
    given, refs = refs[:cuts], refs[cuts:]
    arrays, out = refs[:count], refs[-1]
    _, layers, rows, _ = held.shape
    wide = out.shape[1]
    kept = [(held, first + i) for i in range(sum(map(len, keys)))]
    for half, acts in enumerate((kept, [(array, i) for array in given for i in range(array.shape[0])])):
        spots = iter(acts)
        total = [jnp.zeros((rows, wide), jnp.float32) for _ in range(layers)]
        for array, shifts in zip(arrays, keys):
            tall = array.shape[0] // len(shifts)
            for i in range(len(shifts)):
                from_, at = next(spots)
                block = array[i * tall:(i + 1) * tall, :]
                for l in range(layers):
                    total[l] = total[l] + jnp.dot(from_[at, l], block, preferred_element_type=jnp.float32)
        value = joined(total)
        where = slice(half * rows, (half + 1) * rows)
        out[where, :] = value if begin else refs[count][where, :] + value


def pack_kernel(mine, theirs, pg, px, feat):
    rows = mine.shape[0] // 2
    for half in range(2):
        here, there = slice(half * rows, (half + 1) * rows), slice((1 - half) * rows, (2 - half) * rows)
        value = (mine[here, :] + theirs[there, :]).astype(jnp.bfloat16)
        px[here, :] = value
        feat[here, :] = value
    feat[2 * rows:, :] = pg[...]


def pg_kernel(devices, layers, planes, shifts, *refs):
    count = len(refs) - 1 - len(shifts)
    pgs, outs, spread = refs[:count], refs[count:-1], refs[-1]
    wide, rows = pgs[0].shape
    _, across, cores = levels(devices)
    line = across * cores
    width_k = wide // layers
    size = width_k // (planes * line)
    for i, pg in enumerate(pgs):
        spread[:, i * rows:(i + 1) * rows] = pg[...].astype(jnp.float32)
    me = lax.axis_index("seq")
    for shift, out in zip(shifts, outs):
        spot = owner(me, devices, shift) % line
        picked = [
            spread[pl.ds(l * width_k + (z * line + spot) * size + i, 1), :]
            for l in range(layers)
            for z in range(planes)
            for i in range(size)
        ]
        picked = jnp.concatenate(picked, axis=0).astype(jnp.bfloat16)
        tall, lanes = picked.shape[0], out.shape[1]
        for i in range(picked.shape[1] // lanes):
            out[i * tall:(i + 1) * tall, :] = picked[:, i * lanes:(i + 1) * lanes]


def whole_kernel(devices, acts, *refs):
    blocks, (out, weights) = refs[:-2], refs[-2:]
    deep, wide, cores = levels(devices)
    me = lax.axis_index("seq")
    tall = blocks[0].shape[0] // deep
    for i, block in enumerate(blocks):
        for z in range(deep):
            at = owner(me, devices, (0, i // cores, i % cores)) % (wide * cores) + z * wide * cores
            weights[pl.ds(pl.multiple_of(at * tall, tall), tall), :] = block[z * tall:(z + 1) * tall, :]
    total = [jnp.dot(acts[l], weights[...], preferred_element_type=jnp.float32) for l in range(acts.shape[0])]
    out[...] = joined(total).astype(jnp.bfloat16)


def grads_kernel(devices, per_part, layers, rows, planes, shifts, packed, *refs):
    feats, (pg, lengths, out, spread) = refs[:-4], refs[-4:]
    wide = feats[0].shape[1]
    width_k = wide // layers
    _, across, cores = levels(devices)
    me = lax.axis_index("seq")
    sizes = lengths[pl.ds(me // per_part, 1), :]
    per_row = sizes.shape[1]
    upto = lax.broadcasted_iota(jnp.int32, (per_row, per_row), 1)
    which = lax.broadcasted_iota(jnp.int32, (per_row, per_row), 0)
    sizes = jnp.broadcast_to(sizes, (per_row, per_row))
    ends = jnp.sum(jnp.where(upto <= which, sizes, 0), axis=1, keepdims=True)
    starts = jnp.sum(jnp.where(upto < which, sizes, 0), axis=1, keepdims=True)
    member = []
    for shift in shifts:
        first = (owner(me, devices, shift) % per_part) * rows
        position = first + lax.broadcasted_iota(jnp.int32, (per_row, rows), 1)
        member.append(((position >= starts) & (position < ends)).astype(jnp.float32))
    member = jnp.concatenate(member, axis=1)
    tall, near = pg.shape
    spread[:, :near] = pg[...].astype(jnp.float32)
    if packed:
        far = feats[1][2 * rows:, :].astype(jnp.float32)
        for i in range(far.shape[0] // tall):
            at = near + i * wide
            spread[:, at:at + wide] = far[i * tall:(i + 1) * tall]
        px = [feats[0][...], feats[1][:2 * rows, :]]
    else:
        px = [feat[...] for feat in feats]
    px = jnp.concatenate(px, axis=0)
    low = lax.broadcasted_iota(jnp.int32, (per_row, 2 * width_k), 1) < width_k
    size = tall // layers
    for l in range(layers):
        own = px[:, l * width_k:(l + 1) * width_k]
        own = jnp.concatenate([own, own], axis=1)
        for z in range(planes):
            first = l * size + z * (size // planes)
            terms = [
                (member * spread[first + i:first + i + 1, :]).astype(jnp.bfloat16) for i in range(size // planes)
            ]
            sums = jnp.dot(jnp.concatenate(terms, axis=0), own, preferred_element_type=jnp.float32)
            for i in range(0, size // planes, 2):
                even = sums[i * per_row:(i + 1) * per_row]
                odd = sums[(i + 1) * per_row:(i + 2) * per_row]
                at = (first + i) * width_k
                out[:, at:at + 2 * width_k] = jnp.where(low, even, odd).astype(jnp.bfloat16)


def total_kernel(devices, per_part, *refs):
    terms, out = refs[:-1], refs[-1]
    deep, across, cores = levels(devices)
    tall = terms[0].shape[0]
    if out.shape[0] == tall:
        total = terms[0][...].astype(jnp.float32)
        for term in terms[1:]:
            total = total + term[...].astype(jnp.float32)
        out[...] = total.astype(jnp.bfloat16)
        return
    me = lax.axis_index("seq")
    owned = [owner(me, devices, (shift, 0, 0)) // per_part for shift in range(deep)]
    for row in range(out.shape[0] // tall):
        total = jnp.zeros(terms[0].shape, jnp.float32)
        for home, term in zip(owned, terms):
            total = total + jnp.where(home == row, term[...].astype(jnp.float32), 0.0)
        out[row * tall:(row + 1) * tall, :] = total.astype(jnp.bfloat16)


def covariance_kernel(devices, shifts, *refs):
    count = len(shifts)
    blocks, (slots, pairs, logged, out, right, held, sems) = refs[:count], refs[count:]
    npair, band, square = held.shape
    seqs, full = right.shape
    layers = full // square
    _, across, cores = levels(devices)
    lanes = square // (across * cores)
    me = lax.axis_index("seq")
    for shift, block in zip(shifts, blocks):
        spot = owner(me, devices, shift) % (across * cores)
        for here, there, size in chunks(spot, devices, square):
            for l in range(layers):
                at = pl.multiple_of(l * square + there, size)
                right[:, pl.ds(at, size)] = block[:, l * lanes + here:l * lanes + here + size]
    scale = jnp.float32(1.0 / seqs)
    cols = min(1024, square)
    steps = square // cols
    copies = []
    for p in range(npair):
        if band % 128 == 0:
            at = pl.multiple_of(pairs[p, 0] * square + me * band, band)
            left = right[:, pl.ds(at, band)]
        else:
            offset = me * band
            at = pl.multiple_of(pairs[p, 0] * square + (offset // 128) * 128, 128)
            source = lax.broadcasted_iota(jnp.int32, (128, band), 0)
            target = lax.broadcasted_iota(jnp.int32, (128, band), 1)
            pick = (source == target + offset % 128).astype(jnp.float32).astype(jnp.bfloat16)
            left = jnp.dot(right[:, pl.ds(at, 128)], pick, preferred_element_type=jnp.float32).astype(jnp.bfloat16)
        for q in range(steps):
            at = pl.multiple_of(pairs[p, 1] * square + q * cols, cols)
            product = lax.dot_general(
                left, right[:, pl.ds(at, cols)], (((0,), (0,)), ((), ())), preferred_element_type=jnp.float32
            )
            held[p, :, q * cols:(q + 1) * cols] = product * scale
            where = (p, slice(None), pl.ds(q * cols, cols))
            copy = pltpu.make_async_copy(held.at[where], out.at[where], sems.at[p * steps + q])
            copy.start()
            copies.append(copy)
    own = me * CAP + lax.broadcasted_iota(jnp.int32, (CAP, seqs), 0)
    picker = (jnp.broadcast_to(slots[...], (CAP, seqs)) == own).astype(jnp.float32).astype(jnp.bfloat16)
    logged[...] = jnp.dot(picker, right[...], preferred_element_type=jnp.float32).astype(jnp.bfloat16)
    for copy in copies:
        copy.wait()


def part_kernel(devices, shifts, more, mine, *refs):
    array, refs = refs[0], refs[1:]
    if more:
        rest, slots = refs[:len(more) - 1], refs[len(more) - 1]
        refs = refs[len(more):]
    pairs, (side, out, held, sems) = refs[0], refs[-4:]
    npair, band, _ = held.shape
    seqs, full = mine.shape
    deep, across, cores = levels(devices)
    line = across * cores
    square = band * devices
    lanes = square // line
    layers = full // lanes
    me = lax.axis_index("seq")
    scale = jnp.float32(1.0 / seqs)
    copies = []
    for p in range(npair):
        at = pl.multiple_of(pairs[p, 0] * lanes + me // line * band, band)
        left = mine[:, pl.ds(at, band)]
        for i, shift in enumerate(shifts):
            spot = owner(me, devices, shift) % line
            right = array[i * seqs:(i + 1) * seqs, pl.ds(pl.multiple_of(pairs[p, 1] * lanes, lanes), lanes)]
            product = lax.dot_general(left, right, (((0,), (0,)), ((), ())), preferred_element_type=jnp.float32)
            held[p, :, i * lanes:(i + 1) * lanes] = product * scale
            for here, there, size in chunks(spot, devices, square):
                to = pl.ds(pl.multiple_of(there, size), size)
                copies.append(
                    pltpu.make_async_copy(held.at[p, :, pl.ds(i * lanes + here, size)], out.at[p, :, to], sems.at[len(copies)])
                )
                copies[-1].start()
    if not more:
        side[...] = jnp.zeros(side.shape, side.dtype)
    else:
        own = me * CAP + lax.broadcasted_iota(jnp.int32, (CAP, seqs), 0)
        picker = (jnp.broadcast_to(slots[...], (CAP, seqs)) == own).astype(jnp.float32).astype(jnp.bfloat16)
        blocks = [array[i * seqs:(i + 1) * seqs, :] for i in range(len(shifts))] + [ref[...] for ref in (mine, *rest)]
        for shift, block in zip((*shifts, *more), blocks):
            spot = owner(me, devices, shift) % line
            picked = jnp.dot(picker, block, preferred_element_type=jnp.float32).astype(jnp.bfloat16)
            for here, there, size in chunks(spot, devices, square):
                for l in range(layers):
                    to = pl.ds(pl.multiple_of(l * square + there, size), size)
                    side[:, to] = picked[:, l * lanes + here:l * lanes + here + size]
    for copy in copies:
        copy.wait()


def shards(acts, cots, proj_in, proj_out, lengths, slots, pairs):
    layers, rows, width = acts.shape
    wide = proj_out.shape[1]
    width_k = wide // layers
    square = width_k * width_k
    devices = lax.axis_size("seq")
    rows_all, per_row = lengths.shape
    seqs = slots.shape[0]
    npair = pairs.shape[0]
    per_part = devices // rows_all
    band = square // devices
    deep, across, cores = levels(devices)
    line = across * cores
    tall = proj_in.shape[0]
    params = pltpu.CompilerParams(vmem_limit_bytes=24 * MIB)

    light = pl.CostEstimate(flops=1, bytes_accessed=1, transcendentals=0)
    spins = sorted(range(1, deep), key=lambda z: min(z, deep - z))
    staged = tall % 128 == 0 and band % 128 == 0 and deep > 2 and across == 2 and cores == 2
    order = [(z, x, 0) for x in range(across) for z in (0, *spins)] if staged else []
    cuts = 2
    kept = [pltpu.VMEM(acts.shape, jnp.bfloat16)]
    if staged:
        kept = [pltpu.VMEM((count, layers, rows, tall), jnp.bfloat16) for count in (len(order), *[len(order) // cuts] * cuts)]
    *held, own, pg_t = pl.pallas_call(
        functools.partial(load_kernel, devices, order),
        out_shape=(*kept, pltpu.VMEM(proj_in.shape, jnp.bfloat16), pltpu.VMEM((wide, rows), jnp.bfloat16)),
        in_specs=[HBM] * 4,
        out_specs=(VMEM,) * (2 + len(kept)),
        scratch_shapes=[
            pltpu.VMEM(cots.shape, jnp.bfloat16),
            pltpu.VMEM(proj_out.shape, jnp.bfloat16),
            pltpu.SemaphoreType.DMA((3 + (devices if staged else 1),)),
        ],
        compiler_params=params,
        cost_estimate=light,
        name="load",
    )(*[pltpu.with_memory_space_constraint(a, pltpu.HBM) for a in (acts, cots, proj_in, proj_out)])

    def call(kernel, name, types, arrays, after=(), scratch=()):
        return pl.pallas_call(
            kernel,
            out_shape=types,
            in_specs=[VMEM] * len(arrays) + [ANY] * len(after),
            out_specs=[VMEM] * len(types),
            scratch_shapes=list(scratch),
            compiler_params=params,
            cost_estimate=light,
            name=name,
        )(*arrays, *after)

    def plane(block):
        got = {(0, x, 0): send(block, devices, (0, x, 0)) if x else block for x in range(across)}
        return {(*k[:2], c): send(v, devices, (0, 0, c)) if c else v for c in range(cores) for k, v in got.items()}

    def stack(arrays, after):
        return pl.pallas_call(
            functools.partial(stack_kernel, len(arrays)),
            out_shape=jax.ShapeDtypeStruct((sum(a.shape[0] for a in arrays), arrays[0].shape[1]), jnp.bfloat16),
            in_specs=[VMEM] * len(arrays) + [ANY] * len(after),
            out_specs=VMEM,
            compiler_params=params,
            cost_estimate=light,
            name="stack",
        )(*arrays, *after)

    planes = deep if staged else 1
    quarter = layers * width_k // line
    if staged:
        near, far = spins[:-1], spins[-1]
        given = [send(array, devices, (0, 0, 1)) for array in held[1:]]
        got = [send(proj_in, devices, (z, 0, 0)) for z in near]
        side = send(proj_in, devices, (0, 1, 0))
        got_far = send(proj_in, devices, (far, 0, 0))
        got = stack(got, (pg_t, side))
        side_near = send(got, devices, (0, 1, 0))
        side_far = send(got_far, devices, (0, 1, 0))
        pg, pg_side = call(
            functools.partial(pg_kernel, devices, layers, planes, ((0, 0, 0), (0, 1, 0))),
            "pg",
            [
                jax.ShapeDtypeStruct((quarter, 2 * rows), jnp.bfloat16),
                jax.ShapeDtypeStruct((quarter * 2 * rows // wide, wide), jnp.bfloat16),
            ],
            [pg_t, send(pg_t, devices, (0, 0, 1))],
            scratch=[pltpu.VMEM((wide, 2 * rows), jnp.float32)],
        )
        partial_type = jax.ShapeDtypeStruct((2 * rows, wide), jnp.float32)
        value = None
        for x, arrays in enumerate(([own, got, got_far], [side, side_near, side_far])):
            keys = ([(0, x, 0)], [(z, x, 0) for z in near], [(far, x, 0)])
            value = call(
                functools.partial(px_kernel, devices, x * deep, keys, x == 0, cuts // 2),
                "px",
                [partial_type],
                [held[0], *given[x * cuts // 2:(x + 1) * cuts // 2], *arrays] + ([] if x == 0 else [value]),
                after=[pg_side] if x == 0 else (),
            )[0]
        px, feat = call(
            pack_kernel,
            "pack",
            [
                jax.ShapeDtypeStruct((2 * rows, wide), jnp.bfloat16),
                jax.ShapeDtypeStruct((2 * rows + pg_side.shape[0], wide), jnp.bfloat16),
            ],
            [value, send(value, devices, (0, 0, 1)), pg_side],
        )
        feats = [px, send(feat, devices, (0, 1, 0))]
        shifts = ((0, 0, 0), (0, 0, 1), (0, 1, 0), (0, 1, 1))
    else:
        groups = [[z * line + i for z in range(deep)] for i in range(line)]
        column = lax.all_to_all(jnp.tile(proj_in, (deep, 1)), "seq", 0, 0, axis_index_groups=groups, tiled=True)
        blocks = [column] + [send(column, devices, (0, x, 0)) for x in range(1, across)]
        blocks = [block if c == 0 else send(block, devices, (0, 0, c)) for block in blocks for c in range(cores)]
        value = pl.pallas_call(
            functools.partial(whole_kernel, devices),
            out_shape=jax.ShapeDtypeStruct((rows, wide), jnp.bfloat16),
            in_specs=[VMEM] * (1 + len(blocks)),
            out_specs=VMEM,
            scratch_shapes=[pltpu.VMEM((width, wide), jnp.bfloat16)],
            compiler_params=params,
            name="px",
        )(*held, *blocks)
        feats = plane(value)
        shifts = tuple(feats)
        feats = list(feats.values())
        pg = call(
            functools.partial(pg_kernel, devices, layers, planes, ((0, 0, 0),)),
            "pg",
            [jax.ShapeDtypeStruct((quarter, line * rows), jnp.bfloat16)],
            list(plane(pg_t).values()),
            scratch=[pltpu.VMEM((wide, line * rows), jnp.float32)],
        )[0]

    lanes = layers * square // line
    sums = call(
        functools.partial(grads_kernel, devices, per_part, layers, rows, planes, shifts, staged),
        "grads",
        [jax.ShapeDtypeStruct((per_row, lanes), jnp.bfloat16)],
        [*feats, pg, lengths],
        scratch=[pltpu.VMEM((quarter, rows * line), jnp.float32)],
    )[0]
    terms = [send(sums, devices, (z, 0, 0)) if z else sums for z in range(deep)]
    total = pl.pallas_call(
        functools.partial(total_kernel, devices, per_part),
        out_shape=jax.ShapeDtypeStruct((seqs, lanes), jnp.bfloat16),
        in_specs=[VMEM] * deep,
        out_specs=VMEM,
        compiler_params=params,
        name="total",
    )(*terms)
    logged_type = jax.ShapeDtypeStruct((CAP, layers * square), jnp.bfloat16)
    covariance_type = jax.ShapeDtypeStruct((npair, band, square), jnp.float32)
    if staged:
        width = square // line
        shape = (npair, band, width)
        covariance = None
        side = send(total, devices, (0, 1, 0))
        for shifts in (((0, 0, 0),), ((0, 1, 0),), ((0, 0, 1), (0, 1, 1))):
            last = len(shifts) > 1
            arrays = [total, total if covariance is None else send(both, devices, (0, 0, 1)) if last else side]
            specs = [VMEM] * len(arrays)
            more = ()
            if last:
                more = ((0, 0, 0), (0, 1, 0))
                arrays += [side, slots.reshape(1, seqs)]
                specs += [VMEM, VMEM]
            arrays.append(pairs)
            specs.append(SMEM)
            alias = {}
            if covariance is not None:
                alias = {len(arrays): 1}
                arrays.append(covariance)
                specs.append(ANY)
            result = pl.pallas_call(
                functools.partial(part_kernel, devices, shifts, more),
                out_shape=[logged_type if last else jax.ShapeDtypeStruct((8, 128), jnp.float32), covariance_type],
                in_specs=specs,
                out_specs=[VMEM, ANY],
                scratch_shapes=[
                    pltpu.VMEM((npair, band, len(shifts) * width), jnp.float32),
                    pltpu.SemaphoreType.DMA((npair * len(shifts) * deep,)),
                ],
                input_output_aliases=alias,
                compiler_params=params,
                cost_estimate=pl.CostEstimate(
                    flops=2 * npair * seqs * band * width * len(shifts),
                    bytes_accessed=4 * npair * band * width * len(shifts),
                    transcendentals=0,
                ),
                name="covariance",
            )(*arrays)
            if covariance is None:
                both = stack([total, side], (result[0],))
            covariance = result[1]
        return result[0], covariance
    full = plane(total)
    return pl.pallas_call(
        functools.partial(covariance_kernel, devices, tuple(full)),
        out_shape=[logged_type, covariance_type],
        in_specs=[VMEM] * (len(full) + 1) + [SMEM],
        out_specs=[VMEM, ANY],
        scratch_shapes=[
            pltpu.VMEM((seqs, layers * square), jnp.bfloat16),
            pltpu.VMEM((npair, band, square), jnp.float32),
            pltpu.SemaphoreType.DMA((npair * (square // min(1024, square)),)),
        ],
        compiler_params=params,
        name="covariance",
    )(*full.values(), slots.reshape(1, seqs), pairs)


def solution(mesh):
    in_specs = (
        P(None, ("groups", "seq"), None),
        P(None, ("groups", "seq"), None),
        P("seq", None),
        P(),
        P("groups", None),
        P("groups"),
        P(),
    )
    out_specs = (P(("groups", "seq"), None), P("groups", "seq", None))
    return jax.shard_map(shards, mesh=mesh, in_specs=in_specs, out_specs=out_specs, check_vma=False)
```

```python
import functools

import jax
import jax.numpy as jnp
from jax import lax
from jax.experimental import pallas as pl
from jax.experimental.pallas import tpu as pltpu
from jax.sharding import PartitionSpec as P

CAP = 2
MIB = 1 << 20
VMEM = pl.BlockSpec(memory_space=pltpu.VMEM)
SMEM = pl.BlockSpec(memory_space=pltpu.SMEM)
ANY = pl.BlockSpec(memory_space=pl.ANY)
HBM = pl.BlockSpec(memory_space=pltpu.HBM)


def levels(devices):
    cores = 2 if devices % 2 == 0 else 1
    wide = 4 if devices >= 64 and devices % 8 == 0 else 2 if devices % 4 == 0 else 1
    return devices // (cores * wide), wide, cores


def place(index, devices):
    _, wide, cores = levels(devices)
    return index // (wide * cores), index // cores % wide, index % cores


def owner(me, devices, shift):
    deep, wide, cores = levels(devices)
    z, x, core = place(me, devices)
    z = z ^ shift[0] if deep & (deep - 1) == 0 else (z + (deep - shift[0])) % deep
    x = (x + (wide - shift[1])) % wide
    core = (core + (cores - shift[2])) % cores
    return (z * wide + x) * cores + core


def send(value, devices, shift):
    deep, wide, cores = levels(devices)
    perm = []
    for i in range(devices):
        z, x, core = place(i, devices)
        z = z ^ shift[0] if deep & (deep - 1) == 0 else (z + shift[0]) % deep
        x, core = (x + shift[1]) % wide, (core + shift[2]) % cores
        perm.append((i, (z * wide + x) * cores + core))
    return lax.ppermute(value, "seq", perm)


def chunks(spot, devices, square):
    deep, wide, cores = levels(devices)
    line = wide * cores
    band = square // devices
    if band % 128:
        return [(0, spot * (square // line), square // line)]
    return [(z * band, (z * line + spot) * band, band) for z in range(deep)]


def load_kernel(acts, cots, proj_in, proj_out, held, own, pg_t, cots_held, weights, sems):
    layers = cots.shape[0]
    width_k = proj_out.shape[1] // layers
    pairs = [(proj_out, weights), (cots, cots_held), (proj_in, own), (acts, held)]
    copies = [pltpu.make_async_copy(a, b, sems.at[i]) for i, (a, b) in enumerate(pairs)]
    for copy in copies:
        copy.start()
    copies[0].wait()
    copies[1].wait()
    for l in range(layers):
        pg = jnp.dot(cots_held[l], weights[...], preferred_element_type=jnp.float32)
        pg_t[l * width_k:(l + 1) * width_k, :] = pg.T[l * width_k:(l + 1) * width_k, :].astype(jnp.bfloat16)
    copies[2].wait()
    copies[3].wait()


def stack_kernel(count, *refs):
    out = refs[-1]
    at = 0
    for ref in refs[:count]:
        out[at:at + ref.shape[0], :] = ref[...]
        at += ref.shape[0]


def px_kernel(devices, keys, begin, end, keep, acts, *refs):
    count = len(keys)
    arrays, refs = refs[:count], refs[count:]
    layers, rows, _ = acts.shape
    wide = arrays[0].shape[1]
    me = lax.axis_index("seq")
    if keep:
        stack_kernel(count, *arrays, refs[-1])
        refs = refs[:-1]
    total = [jnp.zeros((rows, wide), jnp.float32) if begin else refs[0][l] for l in range(layers)]
    for array, shifts in zip(arrays, keys):
        tall = array.shape[0] // len(shifts)
        for i, shift in enumerate(shifts):
            at = pl.ds(pl.multiple_of(owner(me, devices, shift) * tall, tall), tall)
            block = array[i * tall:(i + 1) * tall, :]
            for l in range(layers):
                total[l] = total[l] + jnp.dot(acts[l, :, at], block, preferred_element_type=jnp.float32)
    if end:
        pack(total, refs[-2], refs[-1])
    else:
        for l in range(layers):
            refs[-1][l] = total[l]


def pack(total, pg_t, out):
    layers = len(total)
    rows, wide = total[0].shape
    width_k = wide // layers
    for l in range(layers):
        at = slice(l * width_k, (l + 1) * width_k)
        out[:rows, at] = total[l][:, at].astype(jnp.bfloat16)
    for i in range(rows // wide):
        out[rows + i * wide:rows + (i + 1) * wide, :] = pg_t[:, i * wide:(i + 1) * wide]


def whole_kernel(devices, acts, *refs):
    blocks, (pg_t, out, weights) = refs[:-3], refs[-3:]
    deep, wide, cores = levels(devices)
    me = lax.axis_index("seq")
    tall = blocks[0].shape[0] // deep
    for i, block in enumerate(blocks):
        for z in range(deep):
            at = owner(me, devices, (0, i // cores, i % cores)) % (wide * cores) + z * wide * cores
            weights[pl.ds(pl.multiple_of(at * tall, tall), tall), :] = block[z * tall:(z + 1) * tall, :]
    pack([jnp.dot(acts[l], weights[...], preferred_element_type=jnp.float32) for l in range(acts.shape[0])], pg_t, out)


def grads_kernel(devices, per_part, layers, rows, shifts, *refs):
    count = len(shifts)
    feats, (lengths, out, spread) = refs[:count], refs[count:]
    wide = feats[0].shape[1]
    runs = rows // wide
    width_k = wide // layers
    square = width_k * width_k
    _, across, cores = levels(devices)
    me = lax.axis_index("seq")
    sizes = lengths[pl.ds(me // per_part, 1), :]
    per_row = sizes.shape[1]
    upto = lax.broadcasted_iota(jnp.int32, (per_row, per_row), 1)
    which = lax.broadcasted_iota(jnp.int32, (per_row, per_row), 0)
    sizes = jnp.broadcast_to(sizes, (per_row, per_row))
    ends = jnp.sum(jnp.where(upto <= which, sizes, 0), axis=1, keepdims=True)
    starts = jnp.sum(jnp.where(upto < which, sizes, 0), axis=1, keepdims=True)
    member = []
    for shift in shifts:
        first = (owner(me, devices, shift) % per_part) * rows
        position = first + lax.broadcasted_iota(jnp.int32, (per_row, wide), 1)
        for i in range(runs):
            now = position + i * wide
            member.append(((now >= starts) & (now < ends)).astype(jnp.float32))
    member = jnp.concatenate(member, axis=1)
    for f, feat in enumerate(feats):
        for i in range(runs):
            at = (f * runs + i) * wide
            spread[:, at:at + wide] = feat[rows + i * wide:rows + (i + 1) * wide, :].astype(jnp.float32)
    low = lax.broadcasted_iota(jnp.int32, (per_row, 2 * width_k), 1) < width_k
    lanes = square // (across * cores)
    spot = me % (across * cores)
    for l in range(layers):
        px = []
        for feat in feats:
            own = feat[:rows, l * width_k:(l + 1) * width_k]
            px.append(jnp.concatenate([own, own], axis=1))
        px = jnp.concatenate(px, axis=0)
        for here, there, size in chunks(spot, devices, square):
            terms = []
            for i in range(size // width_k):
                row = l * width_k + there // width_k + i
                terms.append((member * spread[pl.ds(row, 1), :]).astype(jnp.bfloat16))
            sums = jnp.dot(jnp.concatenate(terms, axis=0), px, preferred_element_type=jnp.float32)
            for i in range(0, size // width_k, 2):
                even = sums[i * per_row:(i + 1) * per_row]
                odd = sums[(i + 1) * per_row:(i + 2) * per_row]
                at = l * lanes + here + i * width_k
                out[:, at:at + 2 * width_k] = jnp.where(low, even, odd).astype(jnp.bfloat16)


def total_kernel(devices, per_part, *refs):
    terms, out = refs[:-1], refs[-1]
    deep, across, cores = levels(devices)
    tall = terms[0].shape[0]
    if out.shape[0] == tall:
        total = terms[0][...].astype(jnp.float32)
        for term in terms[1:]:
            total = total + term[...].astype(jnp.float32)
        out[...] = total.astype(jnp.bfloat16)
        return
    me = lax.axis_index("seq")
    owned = [owner(me, devices, (shift, 0, 0)) // per_part for shift in range(deep)]
    for row in range(out.shape[0] // tall):
        total = jnp.zeros(terms[0].shape, jnp.float32)
        for home, term in zip(owned, terms):
            total = total + jnp.where(home == row, term[...].astype(jnp.float32), 0.0)
        out[row * tall:(row + 1) * tall, :] = total.astype(jnp.bfloat16)


def covariance_kernel(devices, shifts, *refs):
    count = len(shifts)
    blocks, (slots, pairs, logged, out, right, held, sems) = refs[:count], refs[count:]
    npair, band, square = held.shape
    seqs, full = right.shape
    layers = full // square
    _, across, cores = levels(devices)
    lanes = square // (across * cores)
    me = lax.axis_index("seq")
    for shift, block in zip(shifts, blocks):
        spot = owner(me, devices, shift) % (across * cores)
        for here, there, size in chunks(spot, devices, square):
            for l in range(layers):
                at = pl.multiple_of(l * square + there, size)
                right[:, pl.ds(at, size)] = block[:, l * lanes + here:l * lanes + here + size]
    scale = jnp.float32(1.0 / seqs)
    cols = min(1024, square)
    steps = square // cols
    copies = []
    for p in range(npair):
        if band % 128 == 0:
            at = pl.multiple_of(pairs[p, 0] * square + me * band, band)
            left = right[:, pl.ds(at, band)]
        else:
            offset = me * band
            at = pl.multiple_of(pairs[p, 0] * square + (offset // 128) * 128, 128)
            source = lax.broadcasted_iota(jnp.int32, (128, band), 0)
            target = lax.broadcasted_iota(jnp.int32, (128, band), 1)
            pick = (source == target + offset % 128).astype(jnp.float32).astype(jnp.bfloat16)
            left = jnp.dot(right[:, pl.ds(at, 128)], pick, preferred_element_type=jnp.float32).astype(jnp.bfloat16)
        for q in range(steps):
            at = pl.multiple_of(pairs[p, 1] * square + q * cols, cols)
            product = lax.dot_general(
                left, right[:, pl.ds(at, cols)], (((0,), (0,)), ((), ())), preferred_element_type=jnp.float32
            )
            held[p, :, q * cols:(q + 1) * cols] = product * scale
            where = (p, slice(None), pl.ds(q * cols, cols))
            copy = pltpu.make_async_copy(held.at[where], out.at[where], sems.at[p * steps + q])
            copy.start()
            copies.append(copy)
    own = me * CAP + lax.broadcasted_iota(jnp.int32, (CAP, seqs), 0)
    picker = (jnp.broadcast_to(slots[...], (CAP, seqs)) == own).astype(jnp.float32).astype(jnp.bfloat16)
    logged[...] = jnp.dot(picker, right[...], preferred_element_type=jnp.float32).astype(jnp.bfloat16)
    for copy in copies:
        copy.wait()


def part_kernel(devices, shifts, more, mine, *refs):
    array, refs = refs[0], refs[1:]
    if more:
        rest, slots = refs[:len(more) - 1], refs[len(more) - 1]
        refs = refs[len(more):]
    pairs, (side, out, held, sems) = refs[0], refs[-4:]
    npair, band, _ = held.shape
    seqs, full = mine.shape
    deep, across, cores = levels(devices)
    line = across * cores
    square = band * devices
    lanes = square // line
    layers = full // lanes
    me = lax.axis_index("seq")
    scale = jnp.float32(1.0 / seqs)
    copies = []
    for p in range(npair):
        at = pl.multiple_of(pairs[p, 0] * lanes + me // line * band, band)
        left = mine[:, pl.ds(at, band)]
        for i, shift in enumerate(shifts):
            spot = owner(me, devices, shift) % line
            right = array[i * seqs:(i + 1) * seqs, pl.ds(pl.multiple_of(pairs[p, 1] * lanes, lanes), lanes)]
            product = lax.dot_general(left, right, (((0,), (0,)), ((), ())), preferred_element_type=jnp.float32)
            held[p, :, i * lanes:(i + 1) * lanes] = product * scale
            for here, there, size in chunks(spot, devices, square):
                to = pl.ds(pl.multiple_of(there, size), size)
                copies.append(
                    pltpu.make_async_copy(held.at[p, :, pl.ds(i * lanes + here, size)], out.at[p, :, to], sems.at[len(copies)])
                )
                copies[-1].start()
    if not more:
        side[...] = jnp.zeros(side.shape, side.dtype)
    else:
        own = me * CAP + lax.broadcasted_iota(jnp.int32, (CAP, seqs), 0)
        picker = (jnp.broadcast_to(slots[...], (CAP, seqs)) == own).astype(jnp.float32).astype(jnp.bfloat16)
        blocks = [array[i * seqs:(i + 1) * seqs, :] for i in range(len(shifts))] + [ref[...] for ref in (mine, *rest)]
        for shift, block in zip((*shifts, *more), blocks):
            spot = owner(me, devices, shift) % line
            picked = jnp.dot(picker, block, preferred_element_type=jnp.float32).astype(jnp.bfloat16)
            for here, there, size in chunks(spot, devices, square):
                for l in range(layers):
                    to = pl.ds(pl.multiple_of(l * square + there, size), size)
                    side[:, to] = picked[:, l * lanes + here:l * lanes + here + size]
    for copy in copies:
        copy.wait()


def shards(acts, cots, proj_in, proj_out, lengths, slots, pairs):
    layers, rows, width = acts.shape
    wide = proj_out.shape[1]
    width_k = wide // layers
    square = width_k * width_k
    devices = lax.axis_size("seq")
    rows_all, per_row = lengths.shape
    seqs = slots.shape[0]
    npair = pairs.shape[0]
    per_part = devices // rows_all
    band = square // devices
    deep, across, cores = levels(devices)
    line = across * cores
    tall = proj_in.shape[0]
    params = pltpu.CompilerParams(vmem_limit_bytes=24 * MIB)

    light = pl.CostEstimate(flops=1, bytes_accessed=1, transcendentals=0)
    held, own, pg_t = pl.pallas_call(
        load_kernel,
        out_shape=(
            pltpu.VMEM(acts.shape, jnp.bfloat16),
            pltpu.VMEM(proj_in.shape, jnp.bfloat16),
            pltpu.VMEM((wide, rows), jnp.bfloat16),
        ),
        in_specs=[HBM] * 4,
        out_specs=(VMEM,) * 3,
        scratch_shapes=[
            pltpu.VMEM(cots.shape, jnp.bfloat16),
            pltpu.VMEM(proj_out.shape, jnp.bfloat16),
            pltpu.SemaphoreType.DMA((4,)),
        ],
        compiler_params=params,
        cost_estimate=light,
        name="load",
    )(*[pltpu.with_memory_space_constraint(a, pltpu.HBM) for a in (acts, cots, proj_in, proj_out)])

    def stack(arrays, after):
        return pl.pallas_call(
            functools.partial(stack_kernel, len(arrays)),
            out_shape=jax.ShapeDtypeStruct((sum(a.shape[0] for a in arrays), arrays[0].shape[1]), jnp.bfloat16),
            in_specs=[VMEM] * len(arrays) + [ANY] * len(after),
            out_specs=VMEM,
            compiler_params=params,
            cost_estimate=light,
            name="stack",
        )(*arrays, *after)

    def px(entries, before=None, end=False, keep=False):
        more = (() if before is None else (before,)) + ((pg_t,) if end else ())
        arrays, keys = zip(*entries)
        count = sum(map(len, keys))
        sums = feat_type if end else jax.ShapeDtypeStruct((layers, rows, wide), jnp.float32)
        stacked = [jax.ShapeDtypeStruct((count * tall, wide), jnp.bfloat16)] if keep else []
        result = pl.pallas_call(
            functools.partial(px_kernel, devices, keys, before is None, end, keep),
            out_shape=[sums] + stacked,
            in_specs=[VMEM] * (1 + len(arrays) + len(more)),
            out_specs=[VMEM] * (1 + len(stacked)),
            compiler_params=params,
            cost_estimate=light,
            name="px",
        )(held, *arrays, *more)
        return result if keep else result[0]

    feat_type = jax.ShapeDtypeStruct((2 * rows, wide), jnp.bfloat16)
    if tall % 128 == 0 and deep > 2 and across == 2 and cores == 2:
        got = send(proj_in, devices, (1, 0, 0))
        side = send(proj_in, devices, (0, 1, 0))
        far = range(2, deep)
        got_far = [send(proj_in, devices, (z, 0, 0)) for z in far]
        got = stack([got], (side,))
        side_near = send(got, devices, (0, 1, 0))
        got_far = stack(got_far, (pg_t, side_near))
        side_far = send(got_far, devices, (0, 1, 0))
        value, column = px(
            [(own, [(0, 0, 0)]), (got, [(1, 0, 0)]), (got_far, [(z, 0, 0) for z in far])], keep=True
        )
        twin = send(column, devices, (0, 0, 1))
        side = stack([side, side_near, side_far], (value,))
        twin_side = send(side, devices, (0, 0, 1))
        order = range(deep)
        value = px([(side, [(z, 1, 0) for z in order]), (twin, [(z, 0, 1) for z in order])], value)
        value = px([(twin_side, [(z, 1, 1) for z in order])], value, end=True)
    else:
        groups = [[z * line + i for z in range(deep)] for i in range(line)]
        column = lax.all_to_all(jnp.tile(proj_in, (deep, 1)), "seq", 0, 0, axis_index_groups=groups, tiled=True)
        blocks = [column] + [send(column, devices, (0, x, 0)) for x in range(1, across)]
        blocks = [block if c == 0 else send(block, devices, (0, 0, c)) for block in blocks for c in range(cores)]
        value = pl.pallas_call(
            functools.partial(whole_kernel, devices),
            out_shape=feat_type,
            in_specs=[VMEM] * (2 + len(blocks)),
            out_specs=VMEM,
            scratch_shapes=[pltpu.VMEM((width, wide), jnp.bfloat16)],
            compiler_params=params,
            name="px",
        )(held, *blocks, pg_t)

    def plane(block):
        held = {(0, x, 0): send(block, devices, (0, x, 0)) if x else block for x in range(across)}
        return {(*k[:2], c): send(v, devices, (0, 0, c)) if c else v for c in range(cores) for k, v in held.items()}

    feats = plane(value)
    lanes = layers * square // line
    sums = pl.pallas_call(
        functools.partial(grads_kernel, devices, per_part, layers, rows, tuple(feats)),
        out_shape=jax.ShapeDtypeStruct((per_row, lanes), jnp.bfloat16),
        in_specs=[VMEM] * (len(feats) + 1),
        out_specs=VMEM,
        scratch_shapes=[pltpu.VMEM((wide, rows * line), jnp.float32)],
        compiler_params=params,
        name="grads",
    )(*feats.values(), lengths)
    terms = [send(sums, devices, (z, 0, 0)) if z else sums for z in range(deep)]
    total = pl.pallas_call(
        functools.partial(total_kernel, devices, per_part),
        out_shape=jax.ShapeDtypeStruct((seqs, lanes), jnp.bfloat16),
        in_specs=[VMEM] * deep,
        out_specs=VMEM,
        compiler_params=params,
        name="total",
    )(*terms)
    logged_type = jax.ShapeDtypeStruct((CAP, layers * square), jnp.bfloat16)
    covariance_type = jax.ShapeDtypeStruct((npair, band, square), jnp.float32)
    if band % 128 == 0 and across == 2 and cores == 2:
        width = square // line
        shape = (npair, band, width)
        covariance = None
        side = send(total, devices, (0, 1, 0))
        for shifts in (((0, 0, 0),), ((0, 1, 0),), ((0, 0, 1), (0, 1, 1))):
            last = len(shifts) > 1
            arrays = [total, total if covariance is None else send(both, devices, (0, 0, 1)) if last else side]
            specs = [VMEM] * len(arrays)
            more = ()
            if last:
                more = ((0, 0, 0), (0, 1, 0))
                arrays += [side, slots.reshape(1, seqs)]
                specs += [VMEM, VMEM]
            arrays.append(pairs)
            specs.append(SMEM)
            alias = {}
            if covariance is not None:
                alias = {len(arrays): 1}
                arrays.append(covariance)
                specs.append(ANY)
            result = pl.pallas_call(
                functools.partial(part_kernel, devices, shifts, more),
                out_shape=[logged_type if last else jax.ShapeDtypeStruct((8, 128), jnp.float32), covariance_type],
                in_specs=specs,
                out_specs=[VMEM, ANY],
                scratch_shapes=[
                    pltpu.VMEM((npair, band, len(shifts) * width), jnp.float32),
                    pltpu.SemaphoreType.DMA((npair * len(shifts) * deep,)),
                ],
                input_output_aliases=alias,
                compiler_params=params,
                cost_estimate=pl.CostEstimate(
                    flops=2 * npair * seqs * band * width * len(shifts),
                    bytes_accessed=4 * npair * band * width * len(shifts),
                    transcendentals=0,
                ),
                name="covariance",
            )(*arrays)
            if covariance is None:
                both = stack([total, side], (result[0],))
            covariance = result[1]
        return result[0], covariance
    full = plane(total)
    return pl.pallas_call(
        functools.partial(covariance_kernel, devices, tuple(full)),
        out_shape=[logged_type, covariance_type],
        in_specs=[VMEM] * (len(full) + 1) + [SMEM],
        out_specs=[VMEM, ANY],
        scratch_shapes=[
            pltpu.VMEM((seqs, layers * square), jnp.bfloat16),
            pltpu.VMEM((npair, band, square), jnp.float32),
            pltpu.SemaphoreType.DMA((npair * (square // min(1024, square)),)),
        ],
        compiler_params=params,
        name="covariance",
    )(*full.values(), slots.reshape(1, seqs), pairs)


def solution(mesh):
    in_specs = (
        P(None, ("groups", "seq"), None),
        P(None, ("groups", "seq"), None),
        P("seq", None),
        P(),
        P("groups", None),
        P("groups"),
        P(),
    )
    out_specs = (P(("groups", "seq"), None), P("groups", "seq", None))
    return jax.shard_map(shards, mesh=mesh, in_specs=in_specs, out_specs=out_specs, check_vma=False)
```

```python
import functools

import jax
import jax.numpy as jnp
from jax import lax
from jax.experimental import pallas as pl
from jax.experimental.pallas import tpu as pltpu
from jax.sharding import PartitionSpec as P

CAP = 2
MIB = 1 << 20
VMEM = pl.BlockSpec(memory_space=pltpu.VMEM)
SMEM = pl.BlockSpec(memory_space=pltpu.SMEM)
ANY = pl.BlockSpec(memory_space=pl.ANY)
HBM = pl.BlockSpec(memory_space=pltpu.HBM)


def levels(devices):
    cores = 2 if devices % 2 == 0 else 1
    wide = 4 if devices >= 64 and devices % 8 == 0 else 2 if devices % 4 == 0 else 1
    return devices // (cores * wide), wide, cores


def place(index, devices):
    _, wide, cores = levels(devices)
    return index // (wide * cores), index // cores % wide, index % cores


def owner(me, devices, shift):
    deep, wide, cores = levels(devices)
    z, x, core = place(me, devices)
    z = z ^ shift[0] if deep & (deep - 1) == 0 else (z + (deep - shift[0])) % deep
    x = (x + (wide - shift[1])) % wide
    core = (core + (cores - shift[2])) % cores
    return (z * wide + x) * cores + core


def send(value, devices, shift):
    deep, wide, cores = levels(devices)
    perm = []
    for i in range(devices):
        z, x, core = place(i, devices)
        z = z ^ shift[0] if deep & (deep - 1) == 0 else (z + shift[0]) % deep
        x, core = (x + shift[1]) % wide, (core + shift[2]) % cores
        perm.append((i, (z * wide + x) * cores + core))
    return lax.ppermute(value, "seq", perm)


def chunks(spot, devices, square):
    deep, wide, cores = levels(devices)
    line = wide * cores
    band = square // devices
    if band % 128:
        return [(0, spot * (square // line), square // line)]
    return [(z * band, (z * line + spot) * band, band) for z in range(deep)]


def load_kernel(acts, cots, proj_in, proj_out, held, own, pg_t, cots_held, weights, sems):
    layers = cots.shape[0]
    width_k = proj_out.shape[1] // layers
    pairs = [(proj_out, weights), (cots, cots_held), (proj_in, own), (acts, held)]
    copies = [pltpu.make_async_copy(a, b, sems.at[i]) for i, (a, b) in enumerate(pairs)]
    for copy in copies:
        copy.start()
    copies[0].wait()
    copies[1].wait()
    for l in range(layers):
        pg = jnp.dot(cots_held[l], weights[...], preferred_element_type=jnp.float32)
        pg_t[l * width_k:(l + 1) * width_k, :] = pg.T[l * width_k:(l + 1) * width_k, :].astype(jnp.bfloat16)
    copies[2].wait()
    copies[3].wait()


def stack_kernel(count, *refs):
    out = refs[-1]
    at = 0
    for ref in refs[:count]:
        out[at:at + ref.shape[0], :] = ref[...]
        at += ref.shape[0]


def px_kernel(devices, keys, begin, end, keep, acts, *refs):
    count = len(keys)
    arrays, refs = refs[:count], refs[count:]
    layers, rows, _ = acts.shape
    wide = arrays[0].shape[1]
    me = lax.axis_index("seq")
    if keep:
        stack_kernel(count, *arrays, refs[-1])
        refs = refs[:-1]
    total = [jnp.zeros((rows, wide), jnp.float32) if begin else refs[0][l] for l in range(layers)]
    for array, shifts in zip(arrays, keys):
        tall = array.shape[0] // len(shifts)
        for i, shift in enumerate(shifts):
            at = pl.ds(pl.multiple_of(owner(me, devices, shift) * tall, tall), tall)
            block = array[i * tall:(i + 1) * tall, :]
            for l in range(layers):
                total[l] = total[l] + jnp.dot(acts[l, :, at], block, preferred_element_type=jnp.float32)
    if end:
        pack(total, refs[-2], refs[-1])
    else:
        for l in range(layers):
            refs[-1][l] = total[l]


def pack(total, pg_t, out):
    layers = len(total)
    rows, wide = total[0].shape
    width_k = wide // layers
    for l in range(layers):
        at = slice(l * width_k, (l + 1) * width_k)
        out[:rows, at] = total[l][:, at].astype(jnp.bfloat16)
    for i in range(rows // wide):
        out[rows + i * wide:rows + (i + 1) * wide, :] = pg_t[:, i * wide:(i + 1) * wide]


def whole_kernel(devices, acts, *refs):
    blocks, (pg_t, out, weights) = refs[:-3], refs[-3:]
    deep, wide, cores = levels(devices)
    me = lax.axis_index("seq")
    tall = blocks[0].shape[0] // deep
    for i, block in enumerate(blocks):
        for z in range(deep):
            at = owner(me, devices, (0, i // cores, i % cores)) % (wide * cores) + z * wide * cores
            weights[pl.ds(pl.multiple_of(at * tall, tall), tall), :] = block[z * tall:(z + 1) * tall, :]
    pack([jnp.dot(acts[l], weights[...], preferred_element_type=jnp.float32) for l in range(acts.shape[0])], pg_t, out)


def grads_kernel(devices, per_part, layers, rows, shifts, *refs):
    count = len(shifts)
    feats, (lengths, out, spread) = refs[:count], refs[count:]
    wide = feats[0].shape[1]
    runs = rows // wide
    width_k = wide // layers
    square = width_k * width_k
    _, across, cores = levels(devices)
    me = lax.axis_index("seq")
    sizes = lengths[pl.ds(me // per_part, 1), :]
    per_row = sizes.shape[1]
    upto = lax.broadcasted_iota(jnp.int32, (per_row, per_row), 1)
    which = lax.broadcasted_iota(jnp.int32, (per_row, per_row), 0)
    sizes = jnp.broadcast_to(sizes, (per_row, per_row))
    ends = jnp.sum(jnp.where(upto <= which, sizes, 0), axis=1, keepdims=True)
    starts = jnp.sum(jnp.where(upto < which, sizes, 0), axis=1, keepdims=True)
    member = []
    for shift in shifts:
        first = (owner(me, devices, shift) % per_part) * rows
        position = first + lax.broadcasted_iota(jnp.int32, (per_row, wide), 1)
        for i in range(runs):
            now = position + i * wide
            member.append(((now >= starts) & (now < ends)).astype(jnp.float32))
    member = jnp.concatenate(member, axis=1)
    for f, feat in enumerate(feats):
        for i in range(runs):
            at = (f * runs + i) * wide
            spread[:, at:at + wide] = feat[rows + i * wide:rows + (i + 1) * wide, :].astype(jnp.float32)
    low = lax.broadcasted_iota(jnp.int32, (per_row, 2 * width_k), 1) < width_k
    lanes = square // (across * cores)
    spot = me % (across * cores)
    for l in range(layers):
        px = []
        for feat in feats:
            own = feat[:rows, l * width_k:(l + 1) * width_k]
            px.append(jnp.concatenate([own, own], axis=1))
        px = jnp.concatenate(px, axis=0)
        for here, there, size in chunks(spot, devices, square):
            terms = []
            for i in range(size // width_k):
                row = l * width_k + there // width_k + i
                terms.append((member * spread[pl.ds(row, 1), :]).astype(jnp.bfloat16))
            sums = jnp.dot(jnp.concatenate(terms, axis=0), px, preferred_element_type=jnp.float32)
            for i in range(0, size // width_k, 2):
                even = sums[i * per_row:(i + 1) * per_row]
                odd = sums[(i + 1) * per_row:(i + 2) * per_row]
                at = l * lanes + here + i * width_k
                out[:, at:at + 2 * width_k] = jnp.where(low, even, odd).astype(jnp.bfloat16)


def total_kernel(devices, per_part, *refs):
    terms, out = refs[:-1], refs[-1]
    deep, across, cores = levels(devices)
    tall = terms[0].shape[0]
    if out.shape[0] == tall:
        total = terms[0][...].astype(jnp.float32)
        for term in terms[1:]:
            total = total + term[...].astype(jnp.float32)
        out[...] = total.astype(jnp.bfloat16)
        return
    me = lax.axis_index("seq")
    owned = [owner(me, devices, (shift, 0, 0)) // per_part for shift in range(deep)]
    for row in range(out.shape[0] // tall):
        total = jnp.zeros(terms[0].shape, jnp.float32)
        for home, term in zip(owned, terms):
            total = total + jnp.where(home == row, term[...].astype(jnp.float32), 0.0)
        out[row * tall:(row + 1) * tall, :] = total.astype(jnp.bfloat16)


def covariance_kernel(devices, shifts, *refs):
    count = len(shifts)
    blocks, (slots, pairs, logged, out, right, held, sems) = refs[:count], refs[count:]
    npair, band, square = held.shape
    seqs, full = right.shape
    layers = full // square
    _, across, cores = levels(devices)
    lanes = square // (across * cores)
    me = lax.axis_index("seq")
    for shift, block in zip(shifts, blocks):
        spot = owner(me, devices, shift) % (across * cores)
        for here, there, size in chunks(spot, devices, square):
            for l in range(layers):
                at = pl.multiple_of(l * square + there, size)
                right[:, pl.ds(at, size)] = block[:, l * lanes + here:l * lanes + here + size]
    scale = jnp.float32(1.0 / seqs)
    cols = min(1024, square)
    steps = square // cols
    copies = []
    for p in range(npair):
        if band % 128 == 0:
            at = pl.multiple_of(pairs[p, 0] * square + me * band, band)
            left = right[:, pl.ds(at, band)]
        else:
            offset = me * band
            at = pl.multiple_of(pairs[p, 0] * square + (offset // 128) * 128, 128)
            source = lax.broadcasted_iota(jnp.int32, (128, band), 0)
            target = lax.broadcasted_iota(jnp.int32, (128, band), 1)
            pick = (source == target + offset % 128).astype(jnp.float32).astype(jnp.bfloat16)
            left = jnp.dot(right[:, pl.ds(at, 128)], pick, preferred_element_type=jnp.float32).astype(jnp.bfloat16)
        for q in range(steps):
            at = pl.multiple_of(pairs[p, 1] * square + q * cols, cols)
            product = lax.dot_general(
                left, right[:, pl.ds(at, cols)], (((0,), (0,)), ((), ())), preferred_element_type=jnp.float32
            )
            held[p, :, q * cols:(q + 1) * cols] = product * scale
            where = (p, slice(None), pl.ds(q * cols, cols))
            copy = pltpu.make_async_copy(held.at[where], out.at[where], sems.at[p * steps + q])
            copy.start()
            copies.append(copy)
    own = me * CAP + lax.broadcasted_iota(jnp.int32, (CAP, seqs), 0)
    picker = (jnp.broadcast_to(slots[...], (CAP, seqs)) == own).astype(jnp.float32).astype(jnp.bfloat16)
    logged[...] = jnp.dot(picker, right[...], preferred_element_type=jnp.float32).astype(jnp.bfloat16)
    for copy in copies:
        copy.wait()


def own_kernel(devices, mine, pairs, token, out, held, sems):
    npair, band, lanes = held.shape
    seqs, full = mine.shape
    _, across, cores = levels(devices)
    line = across * cores
    me = lax.axis_index("seq")
    scale = jnp.float32(1.0 / seqs)
    copies = []
    for p in range(npair):
        at = pl.multiple_of(pairs[p, 0] * lanes + me // line * band, band)
        right = mine[:, pl.ds(pl.multiple_of(pairs[p, 1] * lanes, lanes), lanes)]
        product = lax.dot_general(
            mine[:, pl.ds(at, band)], right, (((0,), (0,)), ((), ())), preferred_element_type=jnp.float32
        )
        held[p] = product * scale
        for here, there, size in chunks(me % line, devices, band * devices):
            to = pl.ds(pl.multiple_of(there, size), size)
            copies.append(pltpu.make_async_copy(held.at[p, :, pl.ds(here, size)], out.at[p, :, to], sems.at[len(copies)]))
            copies[-1].start()
    token[...] = jnp.zeros(token.shape, token.dtype)
    for copy in copies:
        copy.wait()


def rest_kernel(devices, keys, *refs):
    arrays, (slots, pairs, _, logged, out, held, right, sems) = refs[:len(keys)], refs[len(keys):]
    npair, band, lanes = held.shape
    seqs, full = right.shape
    deep, across, cores = levels(devices)
    line = across * cores
    square = band * devices
    layers = full // square
    me = lax.axis_index("seq")
    spot = me % line
    for array, shifts in zip(arrays, keys):
        for i, shift in enumerate(shifts):
            for here, there, size in chunks(owner(me, devices, shift) % line, devices, square):
                for l in range(layers):
                    at = l * (square // line) + here
                    to = pl.ds(pl.multiple_of(l * square + there, size), size)
                    right[:, to] = array[i * seqs:(i + 1) * seqs, at:at + size]
    runs = [(z * line + spot + 1, line - 1) for z in range(deep - 1)]
    runs += [((devices - line + spot + 1 + i) % devices, 1) for i in range(line - 1)]
    scale = jnp.float32(1.0 / seqs)
    copies = []
    for p in range(npair):
        left = right[:, pl.ds(pl.multiple_of(pairs[p, 0] * square + me * band, band), band)]
        here = 0
        for first, count in runs:
            size = count * band
            value = right[:, pl.ds(pl.multiple_of(pairs[p, 1] * square + first * band, band), size)]
            product = lax.dot_general(left, value, (((0,), (0,)), ((), ())), preferred_element_type=jnp.float32)
            held[p, :, here:here + size] = product * scale
            to = pl.ds(pl.multiple_of(first * band, band), size)
            copies.append(pltpu.make_async_copy(held.at[p, :, pl.ds(here, size)], out.at[p, :, to], sems.at[len(copies)]))
            copies[-1].start()
            here += size
    own = me * CAP + lax.broadcasted_iota(jnp.int32, (CAP, seqs), 0)
    picker = (jnp.broadcast_to(slots[...], (CAP, seqs)) == own).astype(jnp.float32).astype(jnp.bfloat16)
    logged[...] = jnp.dot(picker, right[...], preferred_element_type=jnp.float32).astype(jnp.bfloat16)
    for copy in copies:
        copy.wait()


def shards(acts, cots, proj_in, proj_out, lengths, slots, pairs):
    layers, rows, width = acts.shape
    wide = proj_out.shape[1]
    width_k = wide // layers
    square = width_k * width_k
    devices = lax.axis_size("seq")
    rows_all, per_row = lengths.shape
    seqs = slots.shape[0]
    npair = pairs.shape[0]
    per_part = devices // rows_all
    band = square // devices
    deep, across, cores = levels(devices)
    line = across * cores
    tall = proj_in.shape[0]
    params = pltpu.CompilerParams(vmem_limit_bytes=24 * MIB)

    light = pl.CostEstimate(flops=1, bytes_accessed=1, transcendentals=0)
    held, own, pg_t = pl.pallas_call(
        load_kernel,
        out_shape=(
            pltpu.VMEM(acts.shape, jnp.bfloat16),
            pltpu.VMEM(proj_in.shape, jnp.bfloat16),
            pltpu.VMEM((wide, rows), jnp.bfloat16),
        ),
        in_specs=[HBM] * 4,
        out_specs=(VMEM,) * 3,
        scratch_shapes=[
            pltpu.VMEM(cots.shape, jnp.bfloat16),
            pltpu.VMEM(proj_out.shape, jnp.bfloat16),
            pltpu.SemaphoreType.DMA((4,)),
        ],
        compiler_params=params,
        cost_estimate=light,
        name="load",
    )(*[pltpu.with_memory_space_constraint(a, pltpu.HBM) for a in (acts, cots, proj_in, proj_out)])

    def stack(arrays, after):
        return pl.pallas_call(
            functools.partial(stack_kernel, len(arrays)),
            out_shape=jax.ShapeDtypeStruct((sum(a.shape[0] for a in arrays), arrays[0].shape[1]), jnp.bfloat16),
            in_specs=[VMEM] * len(arrays) + [ANY] * len(after),
            out_specs=VMEM,
            compiler_params=params,
            cost_estimate=light,
            name="stack",
        )(*arrays, *after)

    def px(entries, before=None, end=False, keep=False):
        more = (() if before is None else (before,)) + ((pg_t,) if end else ())
        arrays, keys = zip(*entries)
        count = sum(map(len, keys))
        sums = feat_type if end else jax.ShapeDtypeStruct((layers, rows, wide), jnp.float32)
        stacked = [jax.ShapeDtypeStruct((count * tall, wide), jnp.bfloat16)] if keep else []
        result = pl.pallas_call(
            functools.partial(px_kernel, devices, keys, before is None, end, keep),
            out_shape=[sums] + stacked,
            in_specs=[VMEM] * (1 + len(arrays) + len(more)),
            out_specs=[VMEM] * (1 + len(stacked)),
            compiler_params=params,
            cost_estimate=light,
            name="px",
        )(held, *arrays, *more)
        return result if keep else result[0]

    feat_type = jax.ShapeDtypeStruct((2 * rows, wide), jnp.bfloat16)
    if tall % 128 == 0 and deep > 2 and across == 2 and cores == 2:
        *near, far = range(1, deep)
        got = [send(proj_in, devices, (z, 0, 0)) for z in near]
        side = send(proj_in, devices, (0, 1, 0))
        got_far = send(proj_in, devices, (far, 0, 0))
        got = stack(got, (pg_t, side))
        side_near = send(got, devices, (0, 1, 0))
        side_far = send(got_far, devices, (0, 1, 0))
        value, column = px(
            [(own, [(0, 0, 0)]), (got, [(z, 0, 0) for z in near]), (got_far, [(far, 0, 0)])], keep=True
        )
        twin = send(column, devices, (0, 0, 1))
        side = stack([side, side_near, side_far], (value,))
        twin_side = send(side, devices, (0, 0, 1))
        order = [0, *near, far]
        value = px([(side, [(z, 1, 0) for z in order]), (twin, [(z, 0, 1) for z in order])], value)
        value = px([(twin_side, [(z, 1, 1) for z in order])], value, end=True)
    else:
        groups = [[z * line + i for z in range(deep)] for i in range(line)]
        column = lax.all_to_all(jnp.tile(proj_in, (deep, 1)), "seq", 0, 0, axis_index_groups=groups, tiled=True)
        blocks = [column] + [send(column, devices, (0, x, 0)) for x in range(1, across)]
        blocks = [block if c == 0 else send(block, devices, (0, 0, c)) for block in blocks for c in range(cores)]
        value = pl.pallas_call(
            functools.partial(whole_kernel, devices),
            out_shape=feat_type,
            in_specs=[VMEM] * (2 + len(blocks)),
            out_specs=VMEM,
            scratch_shapes=[pltpu.VMEM((width, wide), jnp.bfloat16)],
            compiler_params=params,
            name="px",
        )(held, *blocks, pg_t)

    def plane(block):
        held = {(0, x, 0): send(block, devices, (0, x, 0)) if x else block for x in range(across)}
        return {(*k[:2], c): send(v, devices, (0, 0, c)) if c else v for c in range(cores) for k, v in held.items()}

    feats = plane(value)
    lanes = layers * square // line
    sums = pl.pallas_call(
        functools.partial(grads_kernel, devices, per_part, layers, rows, tuple(feats)),
        out_shape=jax.ShapeDtypeStruct((per_row, lanes), jnp.bfloat16),
        in_specs=[VMEM] * (len(feats) + 1),
        out_specs=VMEM,
        scratch_shapes=[pltpu.VMEM((wide, rows * line), jnp.float32)],
        compiler_params=params,
        name="grads",
    )(*feats.values(), lengths)
    terms = [send(sums, devices, (z, 0, 0)) if z else sums for z in range(deep)]
    total = pl.pallas_call(
        functools.partial(total_kernel, devices, per_part),
        out_shape=jax.ShapeDtypeStruct((seqs, lanes), jnp.bfloat16),
        in_specs=[VMEM] * deep,
        out_specs=VMEM,
        compiler_params=params,
        name="total",
    )(*terms)
    logged_type = jax.ShapeDtypeStruct((CAP, layers * square), jnp.bfloat16)
    covariance_type = jax.ShapeDtypeStruct((npair, band, square), jnp.float32)
    if band % 128 == 0 and across == 2 and cores == 2:
        width = square // line
        side = send(total, devices, (0, 1, 0))
        token, covariance = pl.pallas_call(
            functools.partial(own_kernel, devices),
            out_shape=[jax.ShapeDtypeStruct((8, 128), jnp.float32), covariance_type],
            in_specs=[VMEM, SMEM],
            out_specs=[VMEM, ANY],
            scratch_shapes=[
                pltpu.VMEM((npair, band, width), jnp.float32),
                pltpu.SemaphoreType.DMA((npair * deep,)),
            ],
            compiler_params=params,
            cost_estimate=pl.CostEstimate(
                flops=2 * npair * seqs * band * width, bytes_accessed=4 * npair * band * width, transcendentals=0
            ),
            name="own",
        )(total, pairs)
        both = stack([total, side], (token,))
        twin = send(both, devices, (0, 0, 1))
        return pl.pallas_call(
            functools.partial(rest_kernel, devices, [[(0, x, c) for x in range(across)] for c in range(cores)]),
            out_shape=[logged_type, covariance_type],
            in_specs=[VMEM, VMEM, VMEM, SMEM, ANY],
            out_specs=[VMEM, ANY],
            scratch_shapes=[
                pltpu.VMEM((npair, band, square - width), jnp.float32),
                pltpu.VMEM((seqs, layers * square), jnp.bfloat16),
                pltpu.SemaphoreType.DMA((npair * (deep + line - 2),)),
            ],
            input_output_aliases={4: 1},
            compiler_params=params,
            name="rest",
        )(both, twin, slots.reshape(1, seqs), pairs, covariance)
    full = plane(total)
    return pl.pallas_call(
        functools.partial(covariance_kernel, devices, tuple(full)),
        out_shape=[logged_type, covariance_type],
        in_specs=[VMEM] * (len(full) + 1) + [SMEM],
        out_specs=[VMEM, ANY],
        scratch_shapes=[
            pltpu.VMEM((seqs, layers * square), jnp.bfloat16),
            pltpu.VMEM((npair, band, square), jnp.float32),
            pltpu.SemaphoreType.DMA((npair * (square // min(1024, square)),)),
        ],
        compiler_params=params,
        name="covariance",
    )(*full.values(), slots.reshape(1, seqs), pairs)


def solution(mesh):
    in_specs = (
        P(None, ("groups", "seq"), None),
        P(None, ("groups", "seq"), None),
        P("seq", None),
        P(),
        P("groups", None),
        P("groups"),
        P(),
    )
    out_specs = (P(("groups", "seq"), None), P("groups", "seq", None))
    return jax.shard_map(shards, mesh=mesh, in_specs=in_specs, out_specs=out_specs, check_vma=False)
```

```python
import functools

import jax
import jax.numpy as jnp
from jax import lax
from jax.experimental import pallas as pl
from jax.experimental.pallas import tpu as pltpu
from jax.sharding import PartitionSpec as P

CAP = 2
MIB = 1 << 20
VMEM = pl.BlockSpec(memory_space=pltpu.VMEM)
SMEM = pl.BlockSpec(memory_space=pltpu.SMEM)
ANY = pl.BlockSpec(memory_space=pl.ANY)
HBM = pl.BlockSpec(memory_space=pltpu.HBM)


def levels(devices):
    cores = 2 if devices % 2 == 0 else 1
    wide = 4 if devices >= 64 and devices % 8 == 0 else 2 if devices % 4 == 0 else 1
    return devices // (cores * wide), wide, cores


def place(index, devices):
    _, wide, cores = levels(devices)
    return index // (wide * cores), index // cores % wide, index % cores


def owner(me, devices, shift):
    deep, wide, cores = levels(devices)
    z, x, core = place(me, devices)
    z = (z + (deep - shift[0])) % deep
    x = (x + (wide - shift[1])) % wide
    core = (core + (cores - shift[2])) % cores
    return (z * wide + x) * cores + core


def send(value, devices, shift):
    deep, wide, cores = levels(devices)
    perm = []
    for i in range(devices):
        z, x, core = place(i, devices)
        z, x, core = (z + shift[0]) % deep, (x + shift[1]) % wide, (core + shift[2]) % cores
        perm.append((i, (z * wide + x) * cores + core))
    return lax.ppermute(value, "seq", perm)


def chunks(spot, devices, square):
    deep, wide, cores = levels(devices)
    line = wide * cores
    band = square // devices
    if band % 128:
        return [(0, spot * (square // line), square // line)]
    return [(z * band, (z * line + spot) * band, band) for z in range(deep)]


def load_kernel(acts, cots, proj_in, proj_out, held, own, pg_t, cots_held, weights, sems):
    layers = cots.shape[0]
    width_k = proj_out.shape[1] // layers
    pairs = [(proj_out, weights), (cots, cots_held), (proj_in, own), (acts, held)]
    copies = [pltpu.make_async_copy(a, b, sems.at[i]) for i, (a, b) in enumerate(pairs)]
    for copy in copies:
        copy.start()
    copies[0].wait()
    copies[1].wait()
    for l in range(layers):
        pg = jnp.dot(cots_held[l], weights[...], preferred_element_type=jnp.float32)
        pg_t[l * width_k:(l + 1) * width_k, :] = pg.T[l * width_k:(l + 1) * width_k, :].astype(jnp.bfloat16)
    copies[2].wait()
    copies[3].wait()


def stack_kernel(count, *refs):
    out = refs[-1]
    at = 0
    for ref in refs[:count]:
        out[at:at + ref.shape[0], :] = ref[...]
        at += ref.shape[0]


def px_kernel(devices, keys, begin, end, keep, acts, *refs):
    count = len(keys)
    arrays, refs = refs[:count], refs[count:]
    layers, rows, _ = acts.shape
    wide = arrays[0].shape[1]
    me = lax.axis_index("seq")
    if keep:
        stack_kernel(count, *arrays, refs[-1])
        refs = refs[:-1]
    total = [jnp.zeros((rows, wide), jnp.float32) if begin else refs[0][l] for l in range(layers)]
    for array, shifts in zip(arrays, keys):
        tall = array.shape[0] // len(shifts)
        for i, shift in enumerate(shifts):
            at = pl.ds(pl.multiple_of(owner(me, devices, shift) * tall, tall), tall)
            block = array[i * tall:(i + 1) * tall, :]
            for l in range(layers):
                total[l] = total[l] + jnp.dot(acts[l, :, at], block, preferred_element_type=jnp.float32)
    if end:
        pack(total, refs[-2], refs[-1])
    else:
        for l in range(layers):
            refs[-1][l] = total[l]


def pack(total, pg_t, out):
    layers = len(total)
    rows, wide = total[0].shape
    width_k = wide // layers
    for l in range(layers):
        at = slice(l * width_k, (l + 1) * width_k)
        out[:rows, at] = total[l][:, at].astype(jnp.bfloat16)
    for i in range(rows // wide):
        out[rows + i * wide:rows + (i + 1) * wide, :] = pg_t[:, i * wide:(i + 1) * wide]


def whole_kernel(devices, acts, *refs):
    blocks, (pg_t, out, weights) = refs[:-3], refs[-3:]
    deep, wide, cores = levels(devices)
    me = lax.axis_index("seq")
    tall = blocks[0].shape[0] // deep
    for i, block in enumerate(blocks):
        for z in range(deep):
            at = owner(me, devices, (0, i // cores, i % cores)) % (wide * cores) + z * wide * cores
            weights[pl.ds(pl.multiple_of(at * tall, tall), tall), :] = block[z * tall:(z + 1) * tall, :]
    pack([jnp.dot(acts[l], weights[...], preferred_element_type=jnp.float32) for l in range(acts.shape[0])], pg_t, out)


def grads_kernel(devices, per_part, layers, rows, shifts, *refs):
    count = len(shifts)
    feats, (lengths, out, spread) = refs[:count], refs[count:]
    wide = feats[0].shape[1]
    runs = rows // wide
    width_k = wide // layers
    square = width_k * width_k
    _, across, cores = levels(devices)
    me = lax.axis_index("seq")
    sizes = lengths[pl.ds(me // per_part, 1), :]
    per_row = sizes.shape[1]
    upto = lax.broadcasted_iota(jnp.int32, (per_row, per_row), 1)
    which = lax.broadcasted_iota(jnp.int32, (per_row, per_row), 0)
    sizes = jnp.broadcast_to(sizes, (per_row, per_row))
    ends = jnp.sum(jnp.where(upto <= which, sizes, 0), axis=1, keepdims=True)
    starts = jnp.sum(jnp.where(upto < which, sizes, 0), axis=1, keepdims=True)
    member = []
    for shift in shifts:
        first = (owner(me, devices, shift) % per_part) * rows
        position = first + lax.broadcasted_iota(jnp.int32, (per_row, wide), 1)
        for i in range(runs):
            now = position + i * wide
            member.append(((now >= starts) & (now < ends)).astype(jnp.float32))
    member = jnp.concatenate(member, axis=1)
    for f, feat in enumerate(feats):
        for i in range(runs):
            at = (f * runs + i) * wide
            spread[:, at:at + wide] = feat[rows + i * wide:rows + (i + 1) * wide, :].astype(jnp.float32)
    low = lax.broadcasted_iota(jnp.int32, (per_row, 2 * width_k), 1) < width_k
    lanes = square // (across * cores)
    spot = me % (across * cores)
    for l in range(layers):
        px = []
        for feat in feats:
            own = feat[:rows, l * width_k:(l + 1) * width_k]
            px.append(jnp.concatenate([own, own], axis=1))
        px = jnp.concatenate(px, axis=0)
        for here, there, size in chunks(spot, devices, square):
            terms = []
            for i in range(size // width_k):
                row = l * width_k + there // width_k + i
                terms.append((member * spread[pl.ds(row, 1), :]).astype(jnp.bfloat16))
            sums = jnp.dot(jnp.concatenate(terms, axis=0), px, preferred_element_type=jnp.float32)
            for i in range(0, size // width_k, 2):
                even = sums[i * per_row:(i + 1) * per_row]
                odd = sums[(i + 1) * per_row:(i + 2) * per_row]
                at = l * lanes + here + i * width_k
                out[:, at:at + 2 * width_k] = jnp.where(low, even, odd).astype(jnp.bfloat16)


def total_kernel(devices, per_part, *refs):
    terms, out = refs[:-1], refs[-1]
    deep, across, cores = levels(devices)
    tall = terms[0].shape[0]
    if out.shape[0] == tall:
        total = terms[0][...].astype(jnp.float32)
        for term in terms[1:]:
            total = total + term[...].astype(jnp.float32)
        out[...] = total.astype(jnp.bfloat16)
        return
    me = lax.axis_index("seq")
    owned = [owner(me, devices, (shift, 0, 0)) // per_part for shift in range(deep)]
    for row in range(out.shape[0] // tall):
        total = jnp.zeros(terms[0].shape, jnp.float32)
        for home, term in zip(owned, terms):
            total = total + jnp.where(home == row, term[...].astype(jnp.float32), 0.0)
        out[row * tall:(row + 1) * tall, :] = total.astype(jnp.bfloat16)


def covariance_kernel(devices, shifts, *refs):
    count = len(shifts)
    blocks, (slots, pairs, logged, out, right, held, sems) = refs[:count], refs[count:]
    npair, band, square = held.shape
    seqs, full = right.shape
    layers = full // square
    _, across, cores = levels(devices)
    lanes = square // (across * cores)
    me = lax.axis_index("seq")
    for shift, block in zip(shifts, blocks):
        spot = owner(me, devices, shift) % (across * cores)
        for here, there, size in chunks(spot, devices, square):
            for l in range(layers):
                at = pl.multiple_of(l * square + there, size)
                right[:, pl.ds(at, size)] = block[:, l * lanes + here:l * lanes + here + size]
    scale = jnp.float32(1.0 / seqs)
    cols = min(1024, square)
    steps = square // cols
    copies = []
    for p in range(npair):
        if band % 128 == 0:
            at = pl.multiple_of(pairs[p, 0] * square + me * band, band)
            left = right[:, pl.ds(at, band)]
        else:
            offset = me * band
            at = pl.multiple_of(pairs[p, 0] * square + (offset // 128) * 128, 128)
            source = lax.broadcasted_iota(jnp.int32, (128, band), 0)
            target = lax.broadcasted_iota(jnp.int32, (128, band), 1)
            pick = (source == target + offset % 128).astype(jnp.float32).astype(jnp.bfloat16)
            left = jnp.dot(right[:, pl.ds(at, 128)], pick, preferred_element_type=jnp.float32).astype(jnp.bfloat16)
        for q in range(steps):
            at = pl.multiple_of(pairs[p, 1] * square + q * cols, cols)
            product = lax.dot_general(
                left, right[:, pl.ds(at, cols)], (((0,), (0,)), ((), ())), preferred_element_type=jnp.float32
            )
            held[p, :, q * cols:(q + 1) * cols] = product * scale
            where = (p, slice(None), pl.ds(q * cols, cols))
            copy = pltpu.make_async_copy(held.at[where], out.at[where], sems.at[p * steps + q])
            copy.start()
            copies.append(copy)
    own = me * CAP + lax.broadcasted_iota(jnp.int32, (CAP, seqs), 0)
    picker = (jnp.broadcast_to(slots[...], (CAP, seqs)) == own).astype(jnp.float32).astype(jnp.bfloat16)
    logged[...] = jnp.dot(picker, right[...], preferred_element_type=jnp.float32).astype(jnp.bfloat16)
    for copy in copies:
        copy.wait()


def own_kernel(devices, mine, pairs, token, out, held, sems):
    npair, band, lanes = held.shape
    seqs, full = mine.shape
    _, across, cores = levels(devices)
    line = across * cores
    me = lax.axis_index("seq")
    scale = jnp.float32(1.0 / seqs)
    copies = []
    for p in range(npair):
        at = pl.multiple_of(pairs[p, 0] * lanes + me // line * band, band)
        right = mine[:, pl.ds(pl.multiple_of(pairs[p, 1] * lanes, lanes), lanes)]
        product = lax.dot_general(
            mine[:, pl.ds(at, band)], right, (((0,), (0,)), ((), ())), preferred_element_type=jnp.float32
        )
        held[p] = product * scale
        for here, there, size in chunks(me % line, devices, band * devices):
            to = pl.ds(pl.multiple_of(there, size), size)
            copies.append(pltpu.make_async_copy(held.at[p, :, pl.ds(here, size)], out.at[p, :, to], sems.at[len(copies)]))
            copies[-1].start()
    token[...] = jnp.zeros(token.shape, token.dtype)
    for copy in copies:
        copy.wait()


def rest_kernel(devices, keys, *refs):
    arrays, (slots, pairs, _, logged, out, held, right, sems) = refs[:len(keys)], refs[len(keys):]
    npair, band, lanes = held.shape
    seqs, full = right.shape
    deep, across, cores = levels(devices)
    line = across * cores
    square = band * devices
    layers = full // square
    me = lax.axis_index("seq")
    spot = me % line
    for array, shifts in zip(arrays, keys):
        for i, shift in enumerate(shifts):
            for here, there, size in chunks(owner(me, devices, shift) % line, devices, square):
                for l in range(layers):
                    at = l * (square // line) + here
                    to = pl.ds(pl.multiple_of(l * square + there, size), size)
                    right[:, to] = array[i * seqs:(i + 1) * seqs, at:at + size]
    runs = [(z * line + spot + 1, line - 1) for z in range(deep - 1)]
    runs += [((devices - line + spot + 1 + i) % devices, 1) for i in range(line - 1)]
    scale = jnp.float32(1.0 / seqs)
    copies = []
    for p in range(npair):
        left = right[:, pl.ds(pl.multiple_of(pairs[p, 0] * square + me * band, band), band)]
        here = 0
        for first, count in runs:
            size = count * band
            value = right[:, pl.ds(pl.multiple_of(pairs[p, 1] * square + first * band, band), size)]
            product = lax.dot_general(left, value, (((0,), (0,)), ((), ())), preferred_element_type=jnp.float32)
            held[p, :, here:here + size] = product * scale
            to = pl.ds(pl.multiple_of(first * band, band), size)
            copies.append(pltpu.make_async_copy(held.at[p, :, pl.ds(here, size)], out.at[p, :, to], sems.at[len(copies)]))
            copies[-1].start()
            here += size
    own = me * CAP + lax.broadcasted_iota(jnp.int32, (CAP, seqs), 0)
    picker = (jnp.broadcast_to(slots[...], (CAP, seqs)) == own).astype(jnp.float32).astype(jnp.bfloat16)
    logged[...] = jnp.dot(picker, right[...], preferred_element_type=jnp.float32).astype(jnp.bfloat16)
    for copy in copies:
        copy.wait()


def shards(acts, cots, proj_in, proj_out, lengths, slots, pairs):
    layers, rows, width = acts.shape
    wide = proj_out.shape[1]
    width_k = wide // layers
    square = width_k * width_k
    devices = lax.axis_size("seq")
    rows_all, per_row = lengths.shape
    seqs = slots.shape[0]
    npair = pairs.shape[0]
    per_part = devices // rows_all
    band = square // devices
    deep, across, cores = levels(devices)
    line = across * cores
    tall = proj_in.shape[0]
    params = pltpu.CompilerParams(vmem_limit_bytes=24 * MIB)

    light = pl.CostEstimate(flops=1, bytes_accessed=1, transcendentals=0)
    held, own, pg_t = pl.pallas_call(
        load_kernel,
        out_shape=(
            pltpu.VMEM(acts.shape, jnp.bfloat16),
            pltpu.VMEM(proj_in.shape, jnp.bfloat16),
            pltpu.VMEM((wide, rows), jnp.bfloat16),
        ),
        in_specs=[HBM] * 4,
        out_specs=(VMEM,) * 3,
        scratch_shapes=[
            pltpu.VMEM(cots.shape, jnp.bfloat16),
            pltpu.VMEM(proj_out.shape, jnp.bfloat16),
            pltpu.SemaphoreType.DMA((4,)),
        ],
        compiler_params=params,
        cost_estimate=light,
        name="load",
    )(*[pltpu.with_memory_space_constraint(a, pltpu.HBM) for a in (acts, cots, proj_in, proj_out)])

    def stack(arrays, after):
        return pl.pallas_call(
            functools.partial(stack_kernel, len(arrays)),
            out_shape=jax.ShapeDtypeStruct((sum(a.shape[0] for a in arrays), arrays[0].shape[1]), jnp.bfloat16),
            in_specs=[VMEM] * len(arrays) + [ANY] * len(after),
            out_specs=VMEM,
            compiler_params=params,
            cost_estimate=light,
            name="stack",
        )(*arrays, *after)

    def px(entries, before=None, end=False, keep=False):
        more = (() if before is None else (before,)) + ((pg_t,) if end else ())
        arrays, keys = zip(*entries)
        count = sum(map(len, keys))
        sums = feat_type if end else jax.ShapeDtypeStruct((layers, rows, wide), jnp.float32)
        stacked = [jax.ShapeDtypeStruct((count * tall, wide), jnp.bfloat16)] if keep else []
        result = pl.pallas_call(
            functools.partial(px_kernel, devices, keys, before is None, end, keep),
            out_shape=[sums] + stacked,
            in_specs=[VMEM] * (1 + len(arrays) + len(more)),
            out_specs=[VMEM] * (1 + len(stacked)),
            compiler_params=params,
            cost_estimate=light,
            name="px",
        )(held, *arrays, *more)
        return result if keep else result[0]

    feat_type = jax.ShapeDtypeStruct((2 * rows, wide), jnp.bfloat16)
    if tall % 128 == 0 and deep > 2 and across == 2 and cores == 2:
        *near, far = sorted(range(1, deep), key=lambda z: min(z, deep - z))
        got = [send(proj_in, devices, (z, 0, 0)) for z in near]
        side = send(proj_in, devices, (0, 1, 0))
        got_far = send(proj_in, devices, (far, 0, 0))
        got = stack(got, (pg_t, side))
        side_near = send(got, devices, (0, 1, 0))
        side_far = send(got_far, devices, (0, 1, 0))
        value, column = px(
            [(own, [(0, 0, 0)]), (got, [(z, 0, 0) for z in near]), (got_far, [(far, 0, 0)])], keep=True
        )
        twin = send(column, devices, (0, 0, 1))
        side = stack([side, side_near, side_far], (value,))
        twin_side = send(side, devices, (0, 0, 1))
        order = [0, *near, far]
        value = px([(side, [(z, 1, 0) for z in order]), (twin, [(z, 0, 1) for z in order])], value)
        value = px([(twin_side, [(z, 1, 1) for z in order])], value, end=True)
    else:
        groups = [[z * line + i for z in range(deep)] for i in range(line)]
        column = lax.all_to_all(jnp.tile(proj_in, (deep, 1)), "seq", 0, 0, axis_index_groups=groups, tiled=True)
        blocks = [column] + [send(column, devices, (0, x, 0)) for x in range(1, across)]
        blocks = [block if c == 0 else send(block, devices, (0, 0, c)) for block in blocks for c in range(cores)]
        value = pl.pallas_call(
            functools.partial(whole_kernel, devices),
            out_shape=feat_type,
            in_specs=[VMEM] * (2 + len(blocks)),
            out_specs=VMEM,
            scratch_shapes=[pltpu.VMEM((width, wide), jnp.bfloat16)],
            compiler_params=params,
            name="px",
        )(held, *blocks, pg_t)

    def plane(block):
        held = {(0, x, 0): send(block, devices, (0, x, 0)) if x else block for x in range(across)}
        return {(*k[:2], c): send(v, devices, (0, 0, c)) if c else v for c in range(cores) for k, v in held.items()}

    feats = plane(value)
    lanes = layers * square // line
    sums = pl.pallas_call(
        functools.partial(grads_kernel, devices, per_part, layers, rows, tuple(feats)),
        out_shape=jax.ShapeDtypeStruct((per_row, lanes), jnp.bfloat16),
        in_specs=[VMEM] * (len(feats) + 1),
        out_specs=VMEM,
        scratch_shapes=[pltpu.VMEM((wide, rows * line), jnp.float32)],
        compiler_params=params,
        name="grads",
    )(*feats.values(), lengths)
    terms = [send(sums, devices, (z, 0, 0)) if z else sums for z in range(deep)]
    total = pl.pallas_call(
        functools.partial(total_kernel, devices, per_part),
        out_shape=jax.ShapeDtypeStruct((seqs, lanes), jnp.bfloat16),
        in_specs=[VMEM] * deep,
        out_specs=VMEM,
        compiler_params=params,
        name="total",
    )(*terms)
    logged_type = jax.ShapeDtypeStruct((CAP, layers * square), jnp.bfloat16)
    covariance_type = jax.ShapeDtypeStruct((npair, band, square), jnp.float32)
    if band % 128 == 0 and across == 2 and cores == 2:
        width = square // line
        side = send(total, devices, (0, 1, 0))
        token, covariance = pl.pallas_call(
            functools.partial(own_kernel, devices),
            out_shape=[jax.ShapeDtypeStruct((8, 128), jnp.float32), covariance_type],
            in_specs=[VMEM, SMEM],
            out_specs=[VMEM, ANY],
            scratch_shapes=[
                pltpu.VMEM((npair, band, width), jnp.float32),
                pltpu.SemaphoreType.DMA((npair * deep,)),
            ],
            compiler_params=params,
            cost_estimate=pl.CostEstimate(
                flops=2 * npair * seqs * band * width, bytes_accessed=4 * npair * band * width, transcendentals=0
            ),
            name="own",
        )(total, pairs)
        both = stack([total, side], (token,))
        twin = send(both, devices, (0, 0, 1))
        return pl.pallas_call(
            functools.partial(rest_kernel, devices, [[(0, x, c) for x in range(across)] for c in range(cores)]),
            out_shape=[logged_type, covariance_type],
            in_specs=[VMEM, VMEM, VMEM, SMEM, ANY],
            out_specs=[VMEM, ANY],
            scratch_shapes=[
                pltpu.VMEM((npair, band, square - width), jnp.float32),
                pltpu.VMEM((seqs, layers * square), jnp.bfloat16),
                pltpu.SemaphoreType.DMA((npair * (deep + line - 2),)),
            ],
            input_output_aliases={4: 1},
            compiler_params=params,
            name="rest",
        )(both, twin, slots.reshape(1, seqs), pairs, covariance)
    full = plane(total)
    return pl.pallas_call(
        functools.partial(covariance_kernel, devices, tuple(full)),
        out_shape=[logged_type, covariance_type],
        in_specs=[VMEM] * (len(full) + 1) + [SMEM],
        out_specs=[VMEM, ANY],
        scratch_shapes=[
            pltpu.VMEM((seqs, layers * square), jnp.bfloat16),
            pltpu.VMEM((npair, band, square), jnp.float32),
            pltpu.SemaphoreType.DMA((npair * (square // min(1024, square)),)),
        ],
        compiler_params=params,
        name="covariance",
    )(*full.values(), slots.reshape(1, seqs), pairs)


def solution(mesh):
    in_specs = (
        P(None, ("groups", "seq"), None),
        P(None, ("groups", "seq"), None),
        P("seq", None),
        P(),
        P("groups", None),
        P("groups"),
        P(),
    )
    out_specs = (P(("groups", "seq"), None), P("groups", "seq", None))
    return jax.shard_map(shards, mesh=mesh, in_specs=in_specs, out_specs=out_specs, check_vma=False)
```

```python
import functools

import jax
import jax.numpy as jnp
from jax import lax
from jax.experimental import pallas as pl
from jax.experimental.pallas import tpu as pltpu
from jax.sharding import PartitionSpec as P

CAP = 2
MIB = 1 << 20
VMEM = pl.BlockSpec(memory_space=pltpu.VMEM)
SMEM = pl.BlockSpec(memory_space=pltpu.SMEM)
ANY = pl.BlockSpec(memory_space=pl.ANY)
HBM = pl.BlockSpec(memory_space=pltpu.HBM)


def levels(devices):
    cores = 2 if devices % 2 == 0 else 1
    wide = 4 if devices >= 64 and devices % 8 == 0 else 2 if devices % 4 == 0 else 1
    return devices // (cores * wide), wide, cores


def place(index, devices):
    _, wide, cores = levels(devices)
    return index // (wide * cores), index // cores % wide, index % cores


def owner(me, devices, shift):
    deep, wide, cores = levels(devices)
    z, x, core = place(me, devices)
    z = (z + (deep - shift[0])) % deep
    x = (x + (wide - shift[1])) % wide
    core = (core + (cores - shift[2])) % cores
    return (z * wide + x) * cores + core


def flipped(z, shift, deep):
    return z ^ shift if deep & (deep - 1) == 0 else (z + shift) % deep


def send(value, devices, shift, pair=False):
    deep, wide, cores = levels(devices)
    perm = []
    for i in range(devices):
        z, x, core = place(i, devices)
        z = flipped(z, shift[0], deep) if pair else (z + shift[0]) % deep
        x, core = (x + shift[1]) % wide, (core + shift[2]) % cores
        perm.append((i, (z * wide + x) * cores + core))
    return lax.ppermute(value, "seq", perm)


def chunks(spot, devices, square):
    deep, wide, cores = levels(devices)
    line = wide * cores
    band = square // devices
    if band % 128:
        return [(0, spot * (square // line), square // line)]
    return [(z * band, (z * line + spot) * band, band) for z in range(deep)]


def load_kernel(acts, cots, proj_in, proj_out, held, own, pg_t, cots_held, weights, sems):
    layers = cots.shape[0]
    width_k = proj_out.shape[1] // layers
    pairs = [(proj_out, weights), (cots, cots_held), (proj_in, own), (acts, held)]
    copies = [pltpu.make_async_copy(a, b, sems.at[i]) for i, (a, b) in enumerate(pairs)]
    for copy in copies:
        copy.start()
    copies[0].wait()
    copies[1].wait()
    for l in range(layers):
        pg = jnp.dot(cots_held[l], weights[...], preferred_element_type=jnp.float32)
        pg_t[l * width_k:(l + 1) * width_k, :] = pg.T[l * width_k:(l + 1) * width_k, :].astype(jnp.bfloat16)
    copies[2].wait()
    copies[3].wait()


def stack_kernel(count, *refs):
    out = refs[-1]
    at = 0
    for ref in refs[:count]:
        out[at:at + ref.shape[0], :] = ref[...]
        at += ref.shape[0]


def px_kernel(devices, keys, begin, end, keep, acts, *refs):
    count = len(keys)
    arrays, refs = refs[:count], refs[count:]
    layers, rows, _ = acts.shape
    wide = arrays[0].shape[1]
    me = lax.axis_index("seq")
    if keep:
        stack_kernel(count, *arrays, refs[-1])
        refs = refs[:-1]
    total = [jnp.zeros((rows, wide), jnp.float32) if begin else refs[0][l] for l in range(layers)]
    for array, shifts in zip(arrays, keys):
        tall = array.shape[0] // len(shifts)
        for i, shift in enumerate(shifts):
            at = pl.ds(pl.multiple_of(owner(me, devices, shift) * tall, tall), tall)
            block = array[i * tall:(i + 1) * tall, :]
            for l in range(layers):
                total[l] = total[l] + jnp.dot(acts[l, :, at], block, preferred_element_type=jnp.float32)
    if end:
        pack(total, refs[-2], refs[-1])
    else:
        for l in range(layers):
            refs[-1][l] = total[l]


def pack(total, pg_t, out):
    layers = len(total)
    rows, wide = total[0].shape
    width_k = wide // layers
    for l in range(layers):
        at = slice(l * width_k, (l + 1) * width_k)
        out[:rows, at] = total[l][:, at].astype(jnp.bfloat16)
    for i in range(rows // wide):
        out[rows + i * wide:rows + (i + 1) * wide, :] = pg_t[:, i * wide:(i + 1) * wide]


def whole_kernel(devices, acts, *refs):
    blocks, (pg_t, out, weights) = refs[:-3], refs[-3:]
    deep, wide, cores = levels(devices)
    me = lax.axis_index("seq")
    tall = blocks[0].shape[0] // deep
    for i, block in enumerate(blocks):
        for z in range(deep):
            at = owner(me, devices, (0, i // cores, i % cores)) % (wide * cores) + z * wide * cores
            weights[pl.ds(pl.multiple_of(at * tall, tall), tall), :] = block[z * tall:(z + 1) * tall, :]
    pack([jnp.dot(acts[l], weights[...], preferred_element_type=jnp.float32) for l in range(acts.shape[0])], pg_t, out)


def grads_kernel(devices, per_part, layers, rows, shifts, *refs):
    count = len(shifts)
    feats, (lengths, out, spread) = refs[:count], refs[count:]
    wide = feats[0].shape[1]
    runs = rows // wide
    width_k = wide // layers
    square = width_k * width_k
    _, across, cores = levels(devices)
    me = lax.axis_index("seq")
    sizes = lengths[pl.ds(me // per_part, 1), :]
    per_row = sizes.shape[1]
    upto = lax.broadcasted_iota(jnp.int32, (per_row, per_row), 1)
    which = lax.broadcasted_iota(jnp.int32, (per_row, per_row), 0)
    sizes = jnp.broadcast_to(sizes, (per_row, per_row))
    ends = jnp.sum(jnp.where(upto <= which, sizes, 0), axis=1, keepdims=True)
    starts = jnp.sum(jnp.where(upto < which, sizes, 0), axis=1, keepdims=True)
    member = []
    for shift in shifts:
        first = (owner(me, devices, shift) % per_part) * rows
        position = first + lax.broadcasted_iota(jnp.int32, (per_row, wide), 1)
        for i in range(runs):
            now = position + i * wide
            member.append(((now >= starts) & (now < ends)).astype(jnp.float32))
    member = jnp.concatenate(member, axis=1)
    for f, feat in enumerate(feats):
        for i in range(runs):
            at = (f * runs + i) * wide
            spread[:, at:at + wide] = feat[rows + i * wide:rows + (i + 1) * wide, :].astype(jnp.float32)
    low = lax.broadcasted_iota(jnp.int32, (per_row, 2 * width_k), 1) < width_k
    lanes = square // (across * cores)
    spot = me % (across * cores)
    for l in range(layers):
        px = []
        for feat in feats:
            own = feat[:rows, l * width_k:(l + 1) * width_k]
            px.append(jnp.concatenate([own, own], axis=1))
        px = jnp.concatenate(px, axis=0)
        for here, there, size in chunks(spot, devices, square):
            terms = []
            for i in range(size // width_k):
                row = l * width_k + there // width_k + i
                terms.append((member * spread[pl.ds(row, 1), :]).astype(jnp.bfloat16))
            sums = jnp.dot(jnp.concatenate(terms, axis=0), px, preferred_element_type=jnp.float32)
            for i in range(0, size // width_k, 2):
                even = sums[i * per_row:(i + 1) * per_row]
                odd = sums[(i + 1) * per_row:(i + 2) * per_row]
                at = l * lanes + here + i * width_k
                out[:, at:at + 2 * width_k] = jnp.where(low, even, odd).astype(jnp.bfloat16)


def total_kernel(devices, per_part, *refs):
    terms, out = refs[:-1], refs[-1]
    deep, across, cores = levels(devices)
    tall = terms[0].shape[0]
    if out.shape[0] == tall:
        total = terms[0][...].astype(jnp.float32)
        for term in terms[1:]:
            total = total + term[...].astype(jnp.float32)
        out[...] = total.astype(jnp.bfloat16)
        return
    me = lax.axis_index("seq")
    line = across * cores
    power = deep & (deep - 1) == 0
    homes = [flipped(me // line, shift if power else deep - shift, deep) for shift in range(deep)]
    owned = [(home * line + me % line) // per_part for home in homes]
    for row in range(out.shape[0] // tall):
        total = jnp.zeros(terms[0].shape, jnp.float32)
        for home, term in zip(owned, terms):
            total = total + jnp.where(home == row, term[...].astype(jnp.float32), 0.0)
        out[row * tall:(row + 1) * tall, :] = total.astype(jnp.bfloat16)


def covariance_kernel(devices, shifts, *refs):
    count = len(shifts)
    blocks, (slots, pairs, logged, out, right, held, sems) = refs[:count], refs[count:]
    npair, band, square = held.shape
    seqs, full = right.shape
    layers = full // square
    _, across, cores = levels(devices)
    lanes = square // (across * cores)
    me = lax.axis_index("seq")
    for shift, block in zip(shifts, blocks):
        spot = owner(me, devices, shift) % (across * cores)
        for here, there, size in chunks(spot, devices, square):
            for l in range(layers):
                at = pl.multiple_of(l * square + there, size)
                right[:, pl.ds(at, size)] = block[:, l * lanes + here:l * lanes + here + size]
    scale = jnp.float32(1.0 / seqs)
    cols = min(1024, square)
    steps = square // cols
    copies = []
    for p in range(npair):
        if band % 128 == 0:
            at = pl.multiple_of(pairs[p, 0] * square + me * band, band)
            left = right[:, pl.ds(at, band)]
        else:
            offset = me * band
            at = pl.multiple_of(pairs[p, 0] * square + (offset // 128) * 128, 128)
            source = lax.broadcasted_iota(jnp.int32, (128, band), 0)
            target = lax.broadcasted_iota(jnp.int32, (128, band), 1)
            pick = (source == target + offset % 128).astype(jnp.float32).astype(jnp.bfloat16)
            left = jnp.dot(right[:, pl.ds(at, 128)], pick, preferred_element_type=jnp.float32).astype(jnp.bfloat16)
        for q in range(steps):
            at = pl.multiple_of(pairs[p, 1] * square + q * cols, cols)
            product = lax.dot_general(
                left, right[:, pl.ds(at, cols)], (((0,), (0,)), ((), ())), preferred_element_type=jnp.float32
            )
            held[p, :, q * cols:(q + 1) * cols] = product * scale
            where = (p, slice(None), pl.ds(q * cols, cols))
            copy = pltpu.make_async_copy(held.at[where], out.at[where], sems.at[p * steps + q])
            copy.start()
            copies.append(copy)
    own = me * CAP + lax.broadcasted_iota(jnp.int32, (CAP, seqs), 0)
    picker = (jnp.broadcast_to(slots[...], (CAP, seqs)) == own).astype(jnp.float32).astype(jnp.bfloat16)
    logged[...] = jnp.dot(picker, right[...], preferred_element_type=jnp.float32).astype(jnp.bfloat16)
    for copy in copies:
        copy.wait()


def own_kernel(devices, mine, pairs, token, out, held, sems):
    npair, band, lanes = held.shape
    seqs, full = mine.shape
    _, across, cores = levels(devices)
    line = across * cores
    me = lax.axis_index("seq")
    scale = jnp.float32(1.0 / seqs)
    copies = []
    for p in range(npair):
        at = pl.multiple_of(pairs[p, 0] * lanes + me // line * band, band)
        right = mine[:, pl.ds(pl.multiple_of(pairs[p, 1] * lanes, lanes), lanes)]
        product = lax.dot_general(
            mine[:, pl.ds(at, band)], right, (((0,), (0,)), ((), ())), preferred_element_type=jnp.float32
        )
        held[p] = product * scale
        for here, there, size in chunks(me % line, devices, band * devices):
            to = pl.ds(pl.multiple_of(there, size), size)
            copies.append(pltpu.make_async_copy(held.at[p, :, pl.ds(here, size)], out.at[p, :, to], sems.at[len(copies)]))
            copies[-1].start()
    token[...] = jnp.zeros(token.shape, token.dtype)
    for copy in copies:
        copy.wait()


def rest_kernel(devices, keys, *refs):
    arrays, (slots, pairs, _, logged, out, held, right, sems) = refs[:len(keys)], refs[len(keys):]
    npair, band, lanes = held.shape
    seqs, full = right.shape
    deep, across, cores = levels(devices)
    line = across * cores
    square = band * devices
    layers = full // square
    me = lax.axis_index("seq")
    spot = me % line
    for array, shifts in zip(arrays, keys):
        for i, shift in enumerate(shifts):
            for here, there, size in chunks(owner(me, devices, shift) % line, devices, square):
                for l in range(layers):
                    at = l * (square // line) + here
                    to = pl.ds(pl.multiple_of(l * square + there, size), size)
                    right[:, to] = array[i * seqs:(i + 1) * seqs, at:at + size]
    runs = [(z * line + spot + 1, line - 1) for z in range(deep - 1)]
    runs += [((devices - line + spot + 1 + i) % devices, 1) for i in range(line - 1)]
    scale = jnp.float32(1.0 / seqs)
    copies = []
    for p in range(npair):
        left = right[:, pl.ds(pl.multiple_of(pairs[p, 0] * square + me * band, band), band)]
        here = 0
        for first, count in runs:
            size = count * band
            value = right[:, pl.ds(pl.multiple_of(pairs[p, 1] * square + first * band, band), size)]
            product = lax.dot_general(left, value, (((0,), (0,)), ((), ())), preferred_element_type=jnp.float32)
            held[p, :, here:here + size] = product * scale
            to = pl.ds(pl.multiple_of(first * band, band), size)
            copies.append(pltpu.make_async_copy(held.at[p, :, pl.ds(here, size)], out.at[p, :, to], sems.at[len(copies)]))
            copies[-1].start()
            here += size
    own = me * CAP + lax.broadcasted_iota(jnp.int32, (CAP, seqs), 0)
    picker = (jnp.broadcast_to(slots[...], (CAP, seqs)) == own).astype(jnp.float32).astype(jnp.bfloat16)
    logged[...] = jnp.dot(picker, right[...], preferred_element_type=jnp.float32).astype(jnp.bfloat16)
    for copy in copies:
        copy.wait()


def shards(acts, cots, proj_in, proj_out, lengths, slots, pairs):
    layers, rows, width = acts.shape
    wide = proj_out.shape[1]
    width_k = wide // layers
    square = width_k * width_k
    devices = lax.axis_size("seq")
    rows_all, per_row = lengths.shape
    seqs = slots.shape[0]
    npair = pairs.shape[0]
    per_part = devices // rows_all
    band = square // devices
    deep, across, cores = levels(devices)
    line = across * cores
    tall = proj_in.shape[0]
    params = pltpu.CompilerParams(vmem_limit_bytes=24 * MIB)

    light = pl.CostEstimate(flops=1, bytes_accessed=1, transcendentals=0)
    held, own, pg_t = pl.pallas_call(
        load_kernel,
        out_shape=(
            pltpu.VMEM(acts.shape, jnp.bfloat16),
            pltpu.VMEM(proj_in.shape, jnp.bfloat16),
            pltpu.VMEM((wide, rows), jnp.bfloat16),
        ),
        in_specs=[HBM] * 4,
        out_specs=(VMEM,) * 3,
        scratch_shapes=[
            pltpu.VMEM(cots.shape, jnp.bfloat16),
            pltpu.VMEM(proj_out.shape, jnp.bfloat16),
            pltpu.SemaphoreType.DMA((4,)),
        ],
        compiler_params=params,
        cost_estimate=light,
        name="load",
    )(*[pltpu.with_memory_space_constraint(a, pltpu.HBM) for a in (acts, cots, proj_in, proj_out)])

    def stack(arrays, after):
        return pl.pallas_call(
            functools.partial(stack_kernel, len(arrays)),
            out_shape=jax.ShapeDtypeStruct((sum(a.shape[0] for a in arrays), arrays[0].shape[1]), jnp.bfloat16),
            in_specs=[VMEM] * len(arrays) + [ANY] * len(after),
            out_specs=VMEM,
            compiler_params=params,
            cost_estimate=light,
            name="stack",
        )(*arrays, *after)

    def px(entries, before=None, end=False, keep=False):
        more = (() if before is None else (before,)) + ((pg_t,) if end else ())
        arrays, keys = zip(*entries)
        count = sum(map(len, keys))
        sums = feat_type if end else jax.ShapeDtypeStruct((layers, rows, wide), jnp.float32)
        stacked = [jax.ShapeDtypeStruct((count * tall, wide), jnp.bfloat16)] if keep else []
        result = pl.pallas_call(
            functools.partial(px_kernel, devices, keys, before is None, end, keep),
            out_shape=[sums] + stacked,
            in_specs=[VMEM] * (1 + len(arrays) + len(more)),
            out_specs=[VMEM] * (1 + len(stacked)),
            compiler_params=params,
            cost_estimate=light,
            name="px",
        )(held, *arrays, *more)
        return result if keep else result[0]

    feat_type = jax.ShapeDtypeStruct((2 * rows, wide), jnp.bfloat16)
    if tall % 128 == 0 and deep > 2 and across == 2 and cores == 2:
        *near, far = sorted(range(1, deep), key=lambda z: min(z, deep - z))
        got = [send(proj_in, devices, (z, 0, 0)) for z in near]
        side = send(proj_in, devices, (0, 1, 0))
        got_far = send(proj_in, devices, (far, 0, 0))
        got = stack(got, (pg_t, side))
        side_near = send(got, devices, (0, 1, 0))
        side_far = send(got_far, devices, (0, 1, 0))
        value, column = px(
            [(own, [(0, 0, 0)]), (got, [(z, 0, 0) for z in near]), (got_far, [(far, 0, 0)])], keep=True
        )
        twin = send(column, devices, (0, 0, 1))
        side = stack([side, side_near, side_far], (value,))
        twin_side = send(side, devices, (0, 0, 1))
        order = [0, *near, far]
        value = px([(side, [(z, 1, 0) for z in order]), (twin, [(z, 0, 1) for z in order])], value)
        value = px([(twin_side, [(z, 1, 1) for z in order])], value, end=True)
    else:
        groups = [[z * line + i for z in range(deep)] for i in range(line)]
        column = lax.all_to_all(jnp.tile(proj_in, (deep, 1)), "seq", 0, 0, axis_index_groups=groups, tiled=True)
        blocks = [column] + [send(column, devices, (0, x, 0)) for x in range(1, across)]
        blocks = [block if c == 0 else send(block, devices, (0, 0, c)) for block in blocks for c in range(cores)]
        value = pl.pallas_call(
            functools.partial(whole_kernel, devices),
            out_shape=feat_type,
            in_specs=[VMEM] * (2 + len(blocks)),
            out_specs=VMEM,
            scratch_shapes=[pltpu.VMEM((width, wide), jnp.bfloat16)],
            compiler_params=params,
            name="px",
        )(held, *blocks, pg_t)

    def plane(block):
        held = {(0, x, 0): send(block, devices, (0, x, 0)) if x else block for x in range(across)}
        return {(*k[:2], c): send(v, devices, (0, 0, c)) if c else v for c in range(cores) for k, v in held.items()}

    feats = plane(value)
    lanes = layers * square // line
    sums = pl.pallas_call(
        functools.partial(grads_kernel, devices, per_part, layers, rows, tuple(feats)),
        out_shape=jax.ShapeDtypeStruct((per_row, lanes), jnp.bfloat16),
        in_specs=[VMEM] * (len(feats) + 1),
        out_specs=VMEM,
        scratch_shapes=[pltpu.VMEM((wide, rows * line), jnp.float32)],
        compiler_params=params,
        name="grads",
    )(*feats.values(), lengths)
    terms = [send(sums, devices, (z, 0, 0), pair=True) if z else sums for z in range(deep)]
    total = pl.pallas_call(
        functools.partial(total_kernel, devices, per_part),
        out_shape=jax.ShapeDtypeStruct((seqs, lanes), jnp.bfloat16),
        in_specs=[VMEM] * deep,
        out_specs=VMEM,
        compiler_params=params,
        name="total",
    )(*terms)
    logged_type = jax.ShapeDtypeStruct((CAP, layers * square), jnp.bfloat16)
    covariance_type = jax.ShapeDtypeStruct((npair, band, square), jnp.float32)
    if band % 128 == 0 and across == 2 and cores == 2:
        width = square // line
        side = send(total, devices, (0, 1, 0))
        token, covariance = pl.pallas_call(
            functools.partial(own_kernel, devices),
            out_shape=[jax.ShapeDtypeStruct((8, 128), jnp.float32), covariance_type],
            in_specs=[VMEM, SMEM],
            out_specs=[VMEM, ANY],
            scratch_shapes=[
                pltpu.VMEM((npair, band, width), jnp.float32),
                pltpu.SemaphoreType.DMA((npair * deep,)),
            ],
            compiler_params=params,
            cost_estimate=pl.CostEstimate(
                flops=2 * npair * seqs * band * width, bytes_accessed=4 * npair * band * width, transcendentals=0
            ),
            name="own",
        )(total, pairs)
        both = stack([total, side], (token,))
        twin = send(both, devices, (0, 0, 1))
        return pl.pallas_call(
            functools.partial(rest_kernel, devices, [[(0, x, c) for x in range(across)] for c in range(cores)]),
            out_shape=[logged_type, covariance_type],
            in_specs=[VMEM, VMEM, VMEM, SMEM, ANY],
            out_specs=[VMEM, ANY],
            scratch_shapes=[
                pltpu.VMEM((npair, band, square - width), jnp.float32),
                pltpu.VMEM((seqs, layers * square), jnp.bfloat16),
                pltpu.SemaphoreType.DMA((npair * (deep + line - 2),)),
            ],
            input_output_aliases={4: 1},
            compiler_params=params,
            name="rest",
        )(both, twin, slots.reshape(1, seqs), pairs, covariance)
    full = plane(total)
    return pl.pallas_call(
        functools.partial(covariance_kernel, devices, tuple(full)),
        out_shape=[logged_type, covariance_type],
        in_specs=[VMEM] * (len(full) + 1) + [SMEM],
        out_specs=[VMEM, ANY],
        scratch_shapes=[
            pltpu.VMEM((seqs, layers * square), jnp.bfloat16),
            pltpu.VMEM((npair, band, square), jnp.float32),
            pltpu.SemaphoreType.DMA((npair * (square // min(1024, square)),)),
        ],
        compiler_params=params,
        name="covariance",
    )(*full.values(), slots.reshape(1, seqs), pairs)


def solution(mesh):
    in_specs = (
        P(None, ("groups", "seq"), None),
        P(None, ("groups", "seq"), None),
        P("seq", None),
        P(),
        P("groups", None),
        P("groups"),
        P(),
    )
    out_specs = (P(("groups", "seq"), None), P("groups", "seq", None))
    return jax.shard_map(shards, mesh=mesh, in_specs=in_specs, out_specs=out_specs, check_vma=False)
```
